128 devices in a mesh: ctx: 16 (over y_hi, x, core), grp: 8 (over y_lo, z).
Axes of the slice: x: 4, y: 4 (y_hi: 2, y_lo: 2; y = y_hi * 2 + y_lo), z: 4, core: 2. Of those that a mesh axis runs over, the one named last changes fastest.
Arguments:
- residual: bfloat16 [4096, 4096], P('ctx', 'grp'), may hold values from -48 to 48
- queries: bfloat16 [4096, 4096], P('ctx', 'grp'), may hold values from -200 to 200
- keys: bfloat16 [4096, 4096], P('ctx', 'grp'), may hold values from -6 to 6
- values: bfloat16 [4096, 4096], P('ctx', 'grp'), may hold values from -6 to 6
- frame_lengths: int32 [16], replicated, may hold values from 1 to 512, 4096 in all
- routes: int32 [4096, 2], P('ctx'), may hold values from 0 to 31, all different within a row; in each aligned block of 256 rows (0 to 255, 256 to 511, ...) at most 48 rows name the same one
- route_gates: float32 [4096, 2], P('ctx'), may hold values from 0.2 to 1
- w_in: bfloat16 [32, 4096, 1536], P('ctx', 'grp'), may hold values from -0.09375 to 0.09375
- w_out: bfloat16 [32, 1536, 4096], P('ctx', None, 'grp'), may hold values from -0.15625 to 0.15625
- out_grad: bfloat16 [4096, 4096], P('ctx', 'grp'), may hold values from -6 to 6
Outputs:
- layer_out: bfloat16 [4096, 4096], P('ctx', 'grp')
- input_grad: bfloat16 [4096, 4096], P('ctx', 'grp')
- query_grad: bfloat16 [4096, 4096], P('ctx', 'grp')
- key_grad: bfloat16 [4096, 4096], P('ctx', 'grp')
- value_grad: bfloat16 [4096, 4096], P('ctx', 'grp')
- w_in_grad: bfloat16 [32, 4096, 1536], P('ctx', 'grp')
- w_out_grad: bfloat16 [32, 1536, 4096], P('ctx', None, 'grp')
The draws below stay inside these ranges and needn't reach their ends.
Inputs may be any that keep to these rules, and one draw needn't show every extreme that they name: `routes`: in every aligned block of 256 rows no expert is named more than 48 times, and in every draw some expert is named exactly 48 times in some block. The two experts of a row differ. `frame_lengths`: the 16 lengths sum to 4096 and the longest is exactly 512.
All inputs are finite; a program needn't handle non-finite values.
Results may differ from the reference program's by a relative error of at most 0.035.
Values may be sent and summed in bfloat16 or wider, within the bound.
A program may use at most 192 MiB of HBM per device.

```python
import math
import jax
import jax.numpy as jnp
import numpy as np
from jax import lax

HEADS = 32
HEAD_DIM = 128
D = 4096
FF = 1536
EXPERTS = 32
TOK_CTX = 256
SEQ = 4096
NFRAMES = 16
FMOST = 512
CAP = 48
N_CTX = 16
N_GRP = 8


def shared_base(key):
    query_base = jnp.clip(jax.random.normal(jax.random.fold_in(key, 101), (SEQ, D), jnp.float32), -6.0, 6.0)
    key_base = jnp.clip(jax.random.normal(jax.random.fold_in(key, 102), (SEQ, D), jnp.float32), -6.0, 6.0)
    return (query_base, key_base)


def draw_queries(key, part):
    query_base, key_base = shared_base(key)
    return jnp.clip(query_base, -200.0, 200.0).astype(jnp.bfloat16)


def draw_keys(key, part):
    query_base, key_base = shared_base(key)
    return jnp.clip(key_base, -6.0, 6.0).astype(jnp.bfloat16)


def draw_residual(key, part):
    key = jax.random.fold_in(key, 5)
    key_list = jax.random.split(key, 3)
    columns = jnp.arange(D, dtype=jnp.float32) / D
    jitter = jax.random.uniform(key_list[0], (D,), jnp.float32, -0.15, 0.15)
    column_scale = 0.5 * 10.0 ** jnp.clip(columns + jitter, 0.0, 1.0)
    row_scale = 10.0 ** jax.random.uniform(key_list[1], (SEQ, 1), jnp.float32, -0.5, 0.5)
    base = jnp.clip(jax.random.normal(key_list[2], (SEQ, D), jnp.float32), -4.0, 4.0)
    return jnp.clip(base * row_scale * column_scale[None, :], -48.0, 48.0).astype(jnp.bfloat16)


def steps_of(own_key, extent, cuts, smallest, high):
    level = 1.0
    for position, parts in cuts:
        draws = jax.random.uniform(jax.random.fold_in(jax.random.fold_in(own_key, 6), position), (parts,), jnp.float32, smallest / len(cuts), high / len(cuts))
        level = level * jnp.repeat(jnp.exp(draws), extent[position] // parts).reshape((-1,) + (1,) * (len(extent) - 1 - position))
    return level


def length_profile(amount, total, bound, slope):
    loads = [(1 << 20) // math.isqrt(rank ** slope) + 1 for rank in range(2, amount + 1)]
    rest, holding = total - bound - (amount - 1), [1] * (amount - 1)
    while rest > 0:
        free = [i for i in range(amount - 1) if holding[i] < bound]
        mass, remaining = sum([loads[i] for i in free]), rest
        for i in free:
            extra = min(bound - holding[i], max(1, remaining * loads[i] // mass), rest)
            holding[i] = holding[i] + extra
            rest = rest - extra
    return np.array([bound] + holding)


def uneven(rng, amount, total, limit, skew):
    if amount == 2:
        one = jax.random.randint(rng, (), max(1, total - limit), min(limit, total - 1) + 1)
        return jnp.stack([one, total - one])
    sizes = jnp.asarray(length_profile(amount, total, limit, skew), jnp.int32)
    twos = (amount - 1) // 2
    source_of, sink = sizes[1:1 + 2 * twos:2], sizes[2:2 + 2 * twos:2]
    slack = jnp.minimum(source_of - 1, limit - sink)
    passed = jax.random.randint(jax.random.fold_in(rng, 1), (twos,), 0, 1 << 20) % (slack + 1)
    sizes = sizes.at[1:1 + 2 * twos:2].set(source_of - passed).at[2:2 + 2 * twos:2].set(sink + passed)
    return sizes[jax.random.permutation(jax.random.fold_in(rng, 2), amount)]


def routed_block(key, own, number, rows, amount, top, bound, slope):
    ranking = jax.random.permutation(key, amount)
    packed, usual = load_shares(amount, rows * top, bound, slope, True), load_shares(amount, rows * top, bound, slope, False)
    places = jnp.arange(amount)

    def named(tallies, rotation):
        used = int((tallies > 0).sum())
        fixed = max(1, used // 4)
        shifted = fixed + (places - fixed + rotation * (used - fixed)) % max(1, amount - fixed)
        return jnp.zeros((amount,), jnp.int32).at[ranking[jnp.where(places < fixed, places, shifted)]].set(jnp.asarray(tallies, jnp.int32))

    tallies = jnp.where(number % 4 == 0, named(packed, number // 4), named(usual, number - number // 4 - 1))
    mixed = jax.random.permutation(jax.random.fold_in(own, 3), amount)
    giver, taker = mixed[0:amount // 2 * 2:2], mixed[1:amount // 2 * 2:2]
    room = jnp.minimum(tallies[giver] - 1, bound - tallies[taker]) // 2
    room = jnp.where((giver == ranking[0]) | (taker == ranking[0]) | (tallies[taker] == 0), 0, jnp.maximum(room, 0))
    shifted = jax.random.randint(jax.random.fold_in(own, 4), (amount // 2,), 0, 1 << 20) % (room + 1)
    tallies = tallies.at[giver].add(-shifted).at[taker].add(shifted)
    labels = jnp.searchsorted(jnp.cumsum(tallies), jnp.arange(rows * top), side="right").astype(jnp.int32)
    listing = labels.reshape(top, rows).T
    listing = listing[jax.random.permutation(jax.random.fold_in(own, 1), rows)]
    rotation = jax.random.randint(jax.random.fold_in(own, 2), (rows, 1), 0, top)
    return jnp.take_along_axis(listing, (jnp.arange(top)[None, :] + rotation) % top, axis=1)


def load_shares(amount, total, bound, slope, full):
    loads = [(1 << 20) // math.isqrt(standing ** slope) + 1 for standing in range(1, amount + 1)]
    largest = bound if full else min(bound, max(-(-total // amount), total * loads[0] // sum(loads)))
    least = 1 if total - largest >= amount - 1 else 0
    holding, rest = [largest] + [least] * (amount - 1), total - largest - least * (amount - 1)
    while rest > 0:
        free = [i for i in range(1, amount) if holding[i] < largest] or [i for i in range(1, amount) if holding[i] < bound]
        mass, remaining = sum([loads[i] for i in free]), rest
        for i in free:
            more = min(bound - holding[i], max(1, remaining * loads[i] // mass), rest)
            holding[i] = holding[i] + more
            rest = rest - more
    return np.array(holding)


def noise(key, dims, deviation, reach, pieces=(), kind=jnp.bfloat16):
    drawn = jax.random.normal(key, dims, jnp.float32) * deviation
    if len(pieces) > 0:
        drawn = steps_of(key, dims, pieces, -0.22, 0.18) * drawn
    return jnp.clip(drawn, min=-reach, max=reach).astype(kind)


def setup_inputs(seed: int = 0) -> dict:
    arg_keys = jax.random.split(jax.random.key(seed), 11)
    residual = draw_residual(jax.random.fold_in(arg_keys[10], 71), 0)
    queries = draw_queries(jax.random.fold_in(arg_keys[10], 71), 0)
    keys = draw_keys(jax.random.fold_in(arg_keys[10], 71), 0)
    values = noise(arg_keys[3], (SEQ, D), 1.0, 6.0, ((0, 16), (1, 8)))
    frame_lengths = uneven(arg_keys[4], NFRAMES, SEQ, FMOST, 1).astype(jnp.int32)
    routes_keys = jax.random.split(jax.random.fold_in(arg_keys[5], 1), SEQ // TOK_CTX)
    routes_turns = jax.random.permutation(jax.random.fold_in(arg_keys[5], 3), SEQ // TOK_CTX)
    routes = jax.vmap(lambda own, number: routed_block(jax.random.fold_in(arg_keys[5], 2), own, number, TOK_CTX, EXPERTS, 2, CAP, 2))(routes_keys, routes_turns).reshape((SEQ, 2))
    route_gates = jnp.clip(0.2 + 0.8 * jax.random.uniform(arg_keys[6], (SEQ, 2), jnp.float32) ** steps_of(arg_keys[6], (SEQ, 2), ((0, 16),), -0.2, 0.2), 0.2, 1.0)
    w_in = noise(arg_keys[7], (EXPERTS, D, FF), D ** -0.5, 0.09375, ((0, 16), (1, 8)))
    w_out = noise(arg_keys[8], (EXPERTS, FF, D), FF ** -0.5, 0.15625, ((0, 16), (2, 8)))
    out_grad = noise(arg_keys[9], (SEQ, D), 1.0, 6.0, ((0, 16), (1, 8)))
    return dict(residual=residual, queries=queries, keys=keys, values=values, frame_lengths=frame_lengths, routes=routes, route_gates=route_gates, w_in=w_in, w_out=w_out, out_grad=out_grad)


gelu_coef = 0.7978845608028654

def gelu_tanh(field):
    return 0.5 * field * (1.0 + jnp.tanh(gelu_coef * (field + 0.044715 * field * field * field)))

def gelu_slope(field):
    tanh_val = jnp.tanh(gelu_coef * (field + 0.044715 * field * field * field))
    return 0.5 * (1.0 + tanh_val) + 0.5 * field * (1.0 - tanh_val * tanh_val) * gelu_coef * (1.0 + 3.0 * 0.044715 * field * field)

def frame_index(frame_lengths, positions):
    frame_ends = jnp.cumsum(frame_lengths).astype(jnp.int32)
    return lax.optimization_barrier(jnp.sum((frame_ends[None, :] <= positions[:, None]).astype(jnp.int32), axis=1))

def block_sum(partial_value):
    rounded = lax.optimization_barrier(partial_value.astype(jnp.bfloat16))
    return lax.optimization_barrier(jnp.sum(rounded.astype(jnp.float32), axis=0))

def slot_rank(routes_block):
    expert_flat = routes_block.reshape(-1).astype(jnp.int32)
    onehot = (expert_flat[:, None] == jnp.arange(EXPERTS, dtype=jnp.int32)[None, :]).astype(jnp.int32)
    earlier = jnp.cumsum(onehot, axis=0) - onehot
    return (expert_flat, lax.optimization_barrier(jnp.sum(earlier * onehot, axis=1)).astype(jnp.int32))

def block_buffers(routes_block, gates_block, normed_block, grad_block):
    expert_flat, ranks = slot_rank(routes_block)
    slot_ids = jnp.arange(EXPERTS * CAP, dtype=jnp.int32)
    matched = (expert_flat[None, :] == (slot_ids // CAP)[:, None]) & (ranks[None, :] == (slot_ids % CAP)[:, None])
    source = lax.optimization_barrier(jnp.sum(jnp.where(matched, jnp.arange(2 * TOK_CTX, dtype=jnp.int32)[None, :], 0), axis=1)).astype(jnp.int32)
    filled = jnp.any(matched, axis=1)[:, None]
    token_of = source // 2
    rows_in = jnp.where(filled, normed_block[token_of], jnp.zeros_like(normed_block[token_of]))
    gate_of = gates_block.reshape(-1)[source]
    grad_rows = (gate_of[:, None] * grad_block[token_of].astype(jnp.float32)).astype(jnp.bfloat16)
    rows_grad = jnp.where(filled, grad_rows, jnp.zeros_like(grad_rows))
    return (rows_in, rows_grad, expert_flat * CAP + ranks)

def reference(residual, queries, keys, values, frame_lengths, routes, route_gates, w_in, w_out, out_grad):
    score_scale = HEAD_DIM ** (-0.5)
    feat_dev = D // N_GRP
    row_count = N_CTX * CAP
    positions = jnp.arange(SEQ, dtype=jnp.int32)
    frames = frame_index(frame_lengths, positions)
    allowed = frames[None, :] <= frames[:, None]

    def split_heads(array):
        return array.reshape(SEQ, HEADS, HEAD_DIM).transpose(1, 0, 2)
    query_heads = split_heads(queries)
    key_heads = split_heads(keys)
    value_heads = split_heads(values)

    def head_scores(query_h, key_h):
        scores = jnp.dot(query_h, key_h.T, preferred_element_type=jnp.float32) * score_scale
        return jnp.where(allowed, scores, -jnp.inf)

    def head_forward(inputs_h):
        query_h, key_h, value_h = inputs_h
        scores = head_scores(query_h, key_h)
        row_max = lax.optimization_barrier(jnp.max(scores, axis=1, keepdims=True))
        log_total = row_max + jnp.log(lax.optimization_barrier(jnp.sum(jnp.exp(scores - row_max), axis=1, keepdims=True)))
        prob = jnp.exp(scores - log_total).astype(jnp.bfloat16)
        attn_h = jnp.dot(prob, value_h, preferred_element_type=jnp.float32).astype(jnp.bfloat16)
        return (attn_h, log_total)
    attn_heads, log_totals = lax.map(head_forward, (query_heads, key_heads, value_heads))
    attn = attn_heads.transpose(1, 0, 2).reshape(SEQ, D)
    mixed = (residual.astype(jnp.float32) + attn.astype(jnp.float32)).astype(jnp.bfloat16)
    mixed_f = mixed.astype(jnp.float32)
    inv_rms = lax.rsqrt(lax.optimization_barrier(jnp.sum(mixed_f * mixed_f, axis=1)) / D + 1e-06)
    normed = (mixed_f * inv_rms[:, None]).astype(jnp.bfloat16)
    rows_in, rows_grad, row_index = jax.vmap(block_buffers)(routes.reshape(N_CTX, TOK_CTX, 2), route_gates.reshape(N_CTX, TOK_CTX, 2), normed.reshape(N_CTX, TOK_CTX, D), out_grad.reshape(N_CTX, TOK_CTX, D))

    def by_expert(buffer):
        return buffer.reshape(N_CTX, EXPERTS, CAP, D).transpose(1, 0, 2, 3).reshape(EXPERTS, row_count, D)

    def expert_pass(inputs_e):
        x_rows, g_rows, weight_in, weight_out = inputs_e
        pre_act = block_sum(jnp.einsum('rgf,gfh->grh', x_rows.reshape(row_count, N_GRP, feat_dev).astype(jnp.float32), weight_in.reshape(N_GRP, feat_dev, FF).astype(jnp.float32)))
        activated = gelu_tanh(pre_act).astype(jnp.bfloat16)
        expert_out = jnp.dot(activated, weight_out, preferred_element_type=jnp.float32).astype(jnp.bfloat16)
        out_weight_grad = jnp.dot(activated.T, g_rows, preferred_element_type=jnp.float32).astype(jnp.bfloat16)
        act_grad = block_sum(jnp.einsum('rgf,hgf->grh', g_rows.reshape(row_count, N_GRP, feat_dev).astype(jnp.float32), weight_out.reshape(FF, N_GRP, feat_dev).astype(jnp.float32)))
        pre_grad = (act_grad * gelu_slope(pre_act)).astype(jnp.bfloat16)
        in_weight_grad = jnp.dot(x_rows.T, pre_grad, preferred_element_type=jnp.float32).astype(jnp.bfloat16)
        row_grad = jnp.dot(pre_grad, weight_in.T, preferred_element_type=jnp.float32).astype(jnp.bfloat16)
        return (expert_out, row_grad, in_weight_grad, out_weight_grad)
    expert_out, row_grad, w_in_grad, w_out_grad = lax.map(expert_pass, (by_expert(rows_in), by_expert(rows_grad), w_in, w_out))

    def to_tokens(buffer):
        per_block = buffer.reshape(EXPERTS, N_CTX, CAP, D).transpose(1, 0, 2, 3).reshape(N_CTX, EXPERTS * CAP, D)
        picked = jax.vmap(lambda block_rows, index_rows: block_rows[index_rows])(per_block, row_index)
        return picked.reshape(SEQ, 2, D).astype(jnp.float32)
    combined = lax.optimization_barrier(jnp.sum(route_gates[:, :, None] * to_tokens(expert_out), axis=1))
    layer_out = (mixed_f + combined).astype(jnp.bfloat16)
    normed_grad = lax.optimization_barrier(jnp.sum(to_tokens(row_grad), axis=1))
    input_grad_f = out_grad.astype(jnp.float32) + inv_rms[:, None] * normed_grad
    input_grad = input_grad_f.astype(jnp.bfloat16)
    grad_heads = split_heads(input_grad)

    def head_backward(inputs_h):
        query_h, key_h, value_h, attn_h, grad_h, log_total = inputs_h
        scores = head_scores(query_h, key_h)
        prob_f = jnp.exp(scores - log_total)
        prob = prob_f.astype(jnp.bfloat16)
        row_dot = lax.optimization_barrier(jnp.sum(grad_h.astype(jnp.float32) * attn_h.astype(jnp.float32), axis=1))
        dprob = jnp.dot(grad_h, value_h.T, preferred_element_type=jnp.float32)
        dscore = (prob_f * (dprob - row_dot[:, None]) * score_scale).astype(jnp.bfloat16)
        query_g = jnp.dot(dscore, key_h, preferred_element_type=jnp.float32).astype(jnp.bfloat16)
        key_part = jnp.einsum('cqk,cqd->ckd', dscore.reshape(N_CTX, TOK_CTX, SEQ).astype(jnp.float32), query_h.reshape(N_CTX, TOK_CTX, HEAD_DIM).astype(jnp.float32))
        value_part = jnp.einsum('cqk,cqd->ckd', prob.reshape(N_CTX, TOK_CTX, SEQ).astype(jnp.float32), grad_h.reshape(N_CTX, TOK_CTX, HEAD_DIM).astype(jnp.float32))
        key_g = block_sum(key_part).astype(jnp.bfloat16)
        value_g = block_sum(value_part).astype(jnp.bfloat16)
        return (query_g, key_g, value_g)
    query_g, key_g, value_g = lax.map(head_backward, (query_heads, key_heads, value_heads, attn_heads, grad_heads, log_totals))

    def join_heads(array):
        return array.transpose(1, 0, 2).reshape(SEQ, D)
    return (layer_out, input_grad, join_heads(query_g), join_heads(key_g), join_heads(value_g), w_in_grad, w_out_grad)
```

```python
import jax
import jax.numpy as jnp
from jax import lax
from jax.sharding import PartitionSpec as P

HEAD_DIM = 128


gelu_coef = 0.7978845608028654


def gelu_tanh(field):
    return 0.5 * field * (1.0 + jnp.tanh(gelu_coef * (field + 0.044715 * field * field * field)))


def gelu_slope(field):
    tanh_val = jnp.tanh(gelu_coef * (field + 0.044715 * field * field * field))
    return 0.5 * (1.0 + tanh_val) + 0.5 * field * (1.0 - tanh_val * tanh_val) * gelu_coef * (
        1.0 + 3.0 * 0.044715 * field * field
    )


def frame_index(frame_lengths, positions):
    frame_ends = jnp.cumsum(frame_lengths)
    return jnp.sum((frame_ends[None, :] <= positions[:, None]).astype(jnp.int32), axis=1)


def masked_scores(query_heads, key_heads, key_frames, own_frames, score_scale):
    scores = (
        jnp.einsum("qhd,khd->hqk", query_heads, key_heads, preferred_element_type=jnp.float32)
        * score_scale
    )
    allowed = key_frames[None, :] <= own_frames[:, None]
    return jnp.where(allowed[None, :, :], scores, -jnp.inf)


def shards(
    residual, queries, keys, values, frame_lengths, routes, route_gates, w_in, w_out, out_grad
):
    n_ctx = lax.axis_size("ctx")
    n_grp = lax.axis_size("grp")
    tok_rows, feat_dev = residual.shape
    exp_dev = w_in.shape[0]
    head_dim = HEAD_DIM
    heads_dev = feat_dev // head_dim
    seq_len = tok_rows * n_ctx
    experts_all = exp_dev * n_ctx
    capacity = 6 * tok_rows // experts_all
    width_all = feat_dev * n_grp
    score_scale = head_dim ** (-0.5)
    expert_flat = routes.reshape(-1)
    onehot = (expert_flat[:, None] == jnp.arange(experts_all, dtype=jnp.int32)[None, :]).astype(
        jnp.int32
    )
    earlier = jnp.cumsum(onehot, axis=0) - onehot
    ranks = jnp.sum(earlier * onehot, axis=1)
    row_index = (expert_flat * capacity + ranks).reshape(tok_rows, 2)
    slot_ids = jnp.arange(experts_all * capacity, dtype=jnp.int32)
    pick = [
        (slot_ids[:, None] == row_index[None, :, a]).astype(jnp.bfloat16) for a in range(2)
    ]
    pick_both = pick[0] + pick[1]
    pick_two = jnp.concatenate(pick, axis=1)

    def to_experts(rows):
        rows = rows.reshape(n_ctx, exp_dev * capacity, feat_dev)
        recv = lax.all_to_all(rows, "ctx", split_axis=0, concat_axis=0, tiled=True)
        recv = recv.reshape(n_ctx, exp_dev, capacity, feat_dev)
        return recv.transpose(1, 0, 2, 3).reshape(exp_dev, n_ctx * capacity, feat_dev)

    def to_tokens(rows):
        rows = rows.reshape(exp_dev, n_ctx, capacity, feat_dev).transpose(1, 0, 2, 3)
        rows = rows.reshape(n_ctx, exp_dev * capacity, feat_dev)
        back = lax.all_to_all(rows, "ctx", split_axis=0, concat_axis=0, tiled=True)
        return back.reshape(experts_all * capacity, feat_dev)

    def sum_scatter(partial):
        flat = partial.astype(jnp.bfloat16).reshape(-1, partial.shape[-1])
        return lax.psum_scatter(flat, "grp", scatter_dimension=0, tiled=True).astype(jnp.float32)

    def gather(shard):
        full = lax.all_gather(shard, "grp", axis=0, tiled=True)
        return full.reshape(exp_dev, n_ctx * capacity, -1)

    out_grad_f = out_grad.astype(jnp.float32)
    gated = jnp.concatenate(
        [(route_gates[:, a : a + 1] * out_grad_f).astype(jnp.bfloat16) for a in range(2)], axis=0
    )
    grad_rows = jnp.dot(pick_two, gated, preferred_element_type=jnp.float32).astype(jnp.bfloat16)
    grads_recv = to_experts(grad_rows)
    act_grad = sum_scatter(
        jnp.einsum("erf,ehf->erh", grads_recv, w_out, preferred_element_type=jnp.float32)
    )
    ctx_index = lax.axis_index("ctx")
    frames = frame_index(frame_lengths, jnp.arange(seq_len, dtype=jnp.int32))
    own_frames = lax.dynamic_slice_in_dim(frames, ctx_index * tok_rows, tok_rows)
    query_heads = queries.reshape(tok_rows, heads_dev, head_dim)
    keys_all, values_all = (
        lax.all_gather(keys, "ctx", axis=0, tiled=True),
        lax.all_gather(values, "ctx", axis=0, tiled=True),
    )
    key_heads_all = keys_all.reshape(seq_len, heads_dev, head_dim)
    value_heads_all = values_all.reshape(seq_len, heads_dev, head_dim)
    scores = masked_scores(query_heads, key_heads_all, frames, own_frames, score_scale)
    row_max = jnp.max(scores, axis=2, keepdims=True)
    log_total = row_max + jnp.log(jnp.sum(jnp.exp(scores - row_max), axis=2, keepdims=True))
    prob = jnp.exp(scores - log_total).astype(jnp.bfloat16)
    attn_heads = jnp.einsum(
        "hqk,khd->qhd", prob, value_heads_all, preferred_element_type=jnp.float32
    ).astype(jnp.bfloat16)
    attn = attn_heads.reshape(tok_rows, feat_dev)
    mixed = (residual.astype(jnp.float32) + attn.astype(jnp.float32)).astype(jnp.bfloat16)
    mixed_f = mixed.astype(jnp.float32)
    square_sum = lax.psum(jnp.sum(mixed_f * mixed_f, axis=1), "grp")
    inv_rms = lax.rsqrt(square_sum / width_all + 1e-06)
    normed = (mixed_f * inv_rms[:, None]).astype(jnp.bfloat16)
    norm_rows = jnp.dot(pick_both, normed, preferred_element_type=jnp.float32).astype(jnp.bfloat16)
    rows_recv = to_experts(norm_rows)
    rows_recv, act_grad = lax.optimization_barrier((rows_recv, act_grad))
    pre_act = sum_scatter(
        jnp.einsum("erf,efh->erh", rows_recv, w_in, preferred_element_type=jnp.float32)
    )
    pre_grad = gather((act_grad * gelu_slope(pre_act)).astype(jnp.bfloat16))
    act_shard, pre_grad = lax.optimization_barrier(
        (gelu_tanh(pre_act).astype(jnp.bfloat16), pre_grad)
    )
    activated = gather(act_shard)
    row_grad = jnp.einsum(
        "erh,efh->erf", pre_grad, w_in, preferred_element_type=jnp.float32
    ).astype(jnp.bfloat16)
    normed_grad = jnp.dot(pick_both.T, to_tokens(row_grad), preferred_element_type=jnp.float32)
    w_in_grad = jnp.einsum(
        "erf,erh->efh", rows_recv, pre_grad, preferred_element_type=jnp.float32
    ).astype(jnp.bfloat16)
    expert_out = jnp.einsum(
        "erh,ehf->erf", activated, w_out, preferred_element_type=jnp.float32
    ).astype(jnp.bfloat16)
    returned = jnp.dot(pick_two.T, to_tokens(expert_out), preferred_element_type=jnp.float32)
    combined = (
        route_gates[:, 0:1] * returned[:tok_rows] + route_gates[:, 1:2] * returned[tok_rows:]
    )
    layer_out = (mixed_f + combined).astype(jnp.bfloat16)
    w_out_grad = jnp.einsum(
        "erh,erf->ehf", activated, grads_recv, preferred_element_type=jnp.float32
    ).astype(jnp.bfloat16)
    input_grad_f = out_grad_f + inv_rms[:, None] * normed_grad
    input_grad = input_grad_f.astype(jnp.bfloat16)
    grad_heads = input_grad.reshape(tok_rows, heads_dev, head_dim)
    row_dot = jnp.sum(grad_heads.astype(jnp.float32) * attn_heads.astype(jnp.float32), axis=2).T
    prob_f = jnp.exp(scores - log_total)
    prob_all = prob_f.astype(jnp.bfloat16)
    dprob = jnp.einsum(
        "qhd,khd->hqk", grad_heads, value_heads_all, preferred_element_type=jnp.float32
    )
    dscore_all = (prob_f * (dprob - row_dot[:, :, None]) * score_scale).astype(jnp.bfloat16)
    query_sum = jnp.einsum(
        "hqk,khd->qhd", dscore_all, key_heads_all, preferred_element_type=jnp.float32
    )
    key_term = jnp.einsum(
        "hqk,qhd->khd", dscore_all, query_heads, preferred_element_type=jnp.float32
    ).reshape(seq_len, feat_dev)
    value_term = jnp.einsum(
        "hqk,qhd->khd", prob_all, grad_heads, preferred_element_type=jnp.float32
    ).reshape(seq_len, feat_dev)
    both_terms = jnp.concatenate([key_term, value_term], axis=1)
    key_grad_f, value_grad_f = (
        lax.psum_scatter(
            both_terms[:, :feat_dev].astype(jnp.bfloat16), "ctx", scatter_dimension=0, tiled=True
        ).astype(jnp.float32),
        lax.psum_scatter(
            both_terms[:, feat_dev:].astype(jnp.bfloat16), "ctx", scatter_dimension=0, tiled=True
        ).astype(jnp.float32),
    )
    query_grad = query_sum.reshape(tok_rows, feat_dev).astype(jnp.bfloat16)
    return (
        layer_out,
        input_grad,
        query_grad,
        key_grad_f.astype(jnp.bfloat16),
        value_grad_f.astype(jnp.bfloat16),
        w_in_grad,
        w_out_grad,
    )


def solution(mesh):
    in_specs = (
        P("ctx", "grp"),
        P("ctx", "grp"),
        P("ctx", "grp"),
        P("ctx", "grp"),
        P(),
        P("ctx", None),
        P("ctx", None),
        P("ctx", "grp", None),
        P("ctx", None, "grp"),
        P("ctx", "grp"),
    )
    out_specs = (
        P("ctx", "grp"),
        P("ctx", "grp"),
        P("ctx", "grp"),
        P("ctx", "grp"),
        P("ctx", "grp"),
        P("ctx", "grp", None),
        P("ctx", None, "grp"),
    )
    return jax.shard_map(shards, mesh=mesh, in_specs=in_specs, out_specs=out_specs, check_vma=False)
```

```python
import jax
import jax.numpy as jnp
from jax import lax
from jax.experimental import pallas as pl
from jax.experimental.pallas import tpu as pltpu
from jax.sharding import PartitionSpec as P

HEAD_DIM = 128


gelu_coef = 0.7978845608028654


def gelu_tanh(field):
    return 0.5 * field * (1.0 + jnp.tanh(gelu_coef * (field + 0.044715 * field * field * field)))


def gelu_slope(field):
    tanh_val = jnp.tanh(gelu_coef * (field + 0.044715 * field * field * field))
    return 0.5 * (1.0 + tanh_val) + 0.5 * field * (1.0 - tanh_val * tanh_val) * gelu_coef * (
        1.0 + 3.0 * 0.044715 * field * field
    )


MESH_ID = pl.DeviceIdType.MESH
LOG2E = 1.4426950408889634
LOW = -1e30


def dot_nt(a, b):
    return lax.dot_general(a, b, (((1,), (1,)), ((), ())), preferred_element_type=jnp.float32)


def dot_tn(a, b):
    return lax.dot_general(a, b, (((0,), (0,)), ((), ())), preferred_element_type=jnp.float32)


def dot_nn(a, b):
    return jnp.dot(a, b, preferred_element_type=jnp.float32)


def greet():
    me = lax.axis_index("ctx")
    grp = lax.axis_index("grp")
    barrier = pltpu.get_barrier_semaphore()

    @pl.loop(1, 16)
    def _(k):
        pl.semaphore_signal(
            barrier, inc=1, device_id={"ctx": lax.rem(me + k, 16)}, device_id_type=MESH_ID
        )

    @pl.loop(1, 8)
    def _(k):
        pl.semaphore_signal(
            barrier, inc=1, device_id={"grp": lax.rem(grp + k, 8)}, device_id_type=MESH_ID
        )

    pl.semaphore_wait(barrier, 22)


def remote(src, dst, send_sem, recv_sem, where):
    return pltpu.make_async_remote_copy(
        src_ref=src,
        dst_ref=dst,
        send_sem=send_sem,
        recv_sem=recv_sem,
        device_id=where,
        device_id_type=MESH_ID,
    )


def forward_kernel(
    q_ref, k_ref, v_ref, res_ref, qend_ref, gated_ref, pick_two_ref, pick_both_ref, w_out_ref,
    attn_ref, lse_ref, mixed_ref, inv_ref, xrecv_ref, grecv_ref, act_grad_ref, kv_out_ref,
    kv, m_s, l_s, acc_s, gsend, xsend, psend, precv, sq_send, sq_recv,
    kv_send_sem, kv_recv_sem, out_sem, g_send_sem, g_recv_sem, x_send_sem, x_recv_sem,
    p_send_sem, p_recv_sem, sq_send_sem, sq_recv_sem,
):
    me = lax.axis_index("ctx")
    grp = lax.axis_index("grp")
    core = lax.rem(me, 2)
    chip = me // 2
    x = lax.rem(chip, 4)
    yh = chip // 4

    def device(dy, dx, dc):
        there = lax.rem(yh + dy, 2) * 4 + lax.rem(x + dx, 4)
        return {"ctx": there * 2 + lax.rem(core + dc, 2)}

    greet()

    copies = {}
    sent = []

    def move(src, slot, where):
        copy = remote(src, kv.at[slot], kv_send_sem.at[len(sent)], kv_recv_sem.at[slot], where)
        copy.start()
        copies[slot] = copy
        sent.append(copy)

    def own(which):
        return k_ref if which == 0 else v_ref

    right, left = device(0, 1, 0), device(0, 3, 0)
    sibling, partner = device(0, 0, 1), device(1, 0, 0)
    for which in range(2):
        move(own(which), (1, 0, 0, which), partner)
        move(own(which), (0, 3, 0, which), right)
        move(own(which), (0, 1, 0, which), left)
        move(own(which), (0, 0, 1, which), sibling)
    kv[0, 0, 0, 0] = k_ref[...]
    kv[0, 0, 0, 1] = v_ref[...]

    @pl.loop(0, 16)
    def _(k):
        there = lax.rem(me + k, 16)
        gsend[k] = dot_nn(pick_two_ref[there], gated_ref[...]).astype(jnp.bfloat16)

        @pl.when(k > 0)
        def _():
            remote(
                gsend.at[k], grecv_ref.at[me], g_send_sem.at[k], g_recv_sem.at[k], {"ctx": there}
            ).start()

    grecv_ref[me] = gsend[0]
    m_s[...] = jnp.full_like(m_s, LOW)
    l_s[...] = jnp.zeros_like(l_s)
    acc_s[...] = jnp.zeros_like(acc_s)
    outs = []

    def wait_slot(dy, dx, dc, which):
        copies[(dy, dx, dc, which)].wait_recv()

    def forward(dy, dx, which):
        wait_slot(dy, dx, 0, which)
        move(kv.at[dy, dx, 0, which], (dy, dx, 1, which), sibling)

    def relay(dy):
        forward(dy, 3, 0)
        move(kv.at[dy, 3, 0, 0], (dy, 2, 0, 0), right)
        forward(dy, 1, 1)
        move(kv.at[dy, 1, 0, 1], (dy, 2, 0, 1), left)
        forward(dy, 3, 1)
        forward(dy, 1, 0)

    def attend(dy, dx):
        for which in range(2):
            wait_slot(dy, dx, 1, which)
        copy = pltpu.make_async_copy(kv.at[dy, dx], kv_out_ref.at[dy, dx], out_sem.at[dy, dx])
        copy.start()
        outs.append(copy)
        there = lax.rem(yh + dy, 2) * 4 + lax.rem(x + dx, 4)
        lane = lax.broadcasted_iota(jnp.int32, (256, 256), 1)
        qend = qend_ref[:, 0:1]
        limits = [qend - (there * 512 + lax.rem(core + dc, 2) * 256) for dc in range(2)]

        @pl.loop(0, 4)
        def _(h):
            cols = pl.ds(pl.multiple_of(h * 128, 128), 128)
            qh = q_ref[:, cols]
            scores = []
            for dc in range(2):
                s = dot_nt(qh, kv[dy, dx, dc, 0, :, cols]) * (LOG2E * HEAD_DIM**-0.5)
                scores.append(jnp.where(lane < limits[dc], s, LOW))
            top = jnp.max(jnp.maximum(scores[0], scores[1]), axis=1, keepdims=True)
            m_old = m_s[h]
            m_new = jnp.maximum(m_old, top)
            alpha = jnp.exp2(m_old - m_new)
            probs = [jnp.exp2(s - m_new[:, 0:1]) for s in scores]
            total = jnp.sum(probs[0] + probs[1], axis=1, keepdims=True)
            m_s[h] = m_new
            l_s[h] = l_s[h] * alpha + total
            acc = acc_s[h] * alpha
            for dc in range(2):
                acc += dot_nn(probs[dc].astype(jnp.bfloat16), kv[dy, dx, dc, 1, :, cols])
            acc_s[h] = acc

    attend(0, 0)
    for which in range(2):
        wait_slot(1, 0, 0, which)
        move(kv.at[1, 0, 0, which], (1, 3, 0, which), right)
        move(kv.at[1, 0, 0, which], (1, 1, 0, which), left)
        move(kv.at[1, 0, 0, which], (1, 0, 1, which), sibling)
    relay(0)
    attend(0, 3)
    attend(0, 1)

    @pl.loop(1, 16)
    def _(k):
        source = lax.rem(me + 16 - k, 16)
        remote(
            gsend.at[k], grecv_ref.at[source], g_send_sem.at[k], g_recv_sem.at[k], {"ctx": source}
        ).wait_recv()

    @pl.loop(0, 8)
    def _(k):
        there = lax.rem(grp + k, 8)
        expert = there // 4
        first = lax.rem(there, 4) * 4
        rows = grecv_ref[pl.ds(first, 4), pl.ds(pl.multiple_of(expert * 48, 16), 48), :]
        rows = rows.reshape(192, 512)

        @pl.loop(0, 3)
        def _(part):
            cols = pl.ds(pl.multiple_of(part * 512, 512), 512)
            psend[k, :, cols] = dot_nt(rows, w_out_ref[expert, cols, :]).astype(jnp.bfloat16)

        @pl.when(k > 0)
        def _():
            remote(
                psend.at[k], precv.at[k], p_send_sem.at[k], p_recv_sem.at[k], {"grp": there}
            ).start()

    relay(1)
    attend(1, 0)
    for which in range(2):
        forward(0, 2, which)
    attend(0, 2)
    attend(1, 3)
    attend(1, 1)
    for which in range(2):
        forward(1, 2, which)
    attend(1, 2)

    squares = jnp.zeros((256, 1), jnp.float32)
    for h in range(4):
        cols = slice(h * 128, h * 128 + 128)
        out = (acc_s[h] / l_s[h]).astype(jnp.bfloat16)
        lse_ref[h] = m_s[h] + jnp.log2(l_s[h])
        attn_ref[:, cols] = out
        mixed = (res_ref[:, cols].astype(jnp.float32) + out.astype(jnp.float32)).astype(
            jnp.bfloat16
        )
        mixed_ref[:, cols] = mixed
        mixed_f = mixed.astype(jnp.float32)
        squares += jnp.sum(mixed_f * mixed_f, axis=1, keepdims=True)
    turned = jnp.transpose(jnp.broadcast_to(squares, (256, 128)))
    sq_send[...] = turned[0:8]
    sq_recv[grp] = turned[0:8]

    @pl.loop(1, 8)
    def _(k):
        there = lax.rem(grp + k, 8)
        remote(
            sq_send, sq_recv.at[grp], sq_send_sem.at[k], sq_recv_sem.at[k], {"grp": there}
        ).start()

    @pl.loop(1, 8)
    def _(k):
        source = lax.rem(grp + 8 - k, 8)
        copy = remote(
            sq_send, sq_recv.at[source], sq_send_sem.at[k], sq_recv_sem.at[k], {"grp": source}
        )
        copy.wait_recv()
        copy.wait_send()

    total = sq_recv[0]
    for k in range(1, 8):
        total = total + sq_recv[k]
    inv = lax.rsqrt(total / 4096 + 1e-06)
    inv = jnp.transpose(jnp.concatenate([inv] * 16, axis=0))
    inv_ref[...] = inv
    normed = jnp.concatenate(
        [
            (mixed_ref[:, h * 128 : h * 128 + 128].astype(jnp.float32) * inv).astype(jnp.bfloat16)
            for h in range(4)
        ],
        axis=1,
    )
    attn_rows = normed

    @pl.loop(0, 16)
    def _(k):
        there = lax.rem(me + k, 16)
        xsend[k] = dot_nn(pick_both_ref[there], attn_rows).astype(jnp.bfloat16)

        @pl.when(k > 0)
        def _():
            remote(
                xsend.at[k], xrecv_ref.at[me], x_send_sem.at[k], x_recv_sem.at[k], {"ctx": there}
            ).start()

    xrecv_ref[me] = xsend[0]

    @pl.loop(1, 8)
    def _(k):
        source = lax.rem(grp + 8 - k, 8)
        copy = remote(
            psend.at[k], precv.at[k], p_send_sem.at[k], p_recv_sem.at[k], {"grp": source}
        )
        copy.wait_recv()
        copy.wait_send()

    @pl.loop(0, 12)
    def _(part):
        rows = pl.ds(pl.multiple_of(part * 16, 16), 16)
        total = psend[0, rows, :].astype(jnp.float32)
        for k in range(1, 8):
            total += precv[k, rows, :].astype(jnp.float32)
        act_grad_ref[rows, :] = total

    @pl.loop(1, 16)
    def _(k):
        source = lax.rem(me + 16 - k, 16)
        copy = remote(
            gsend.at[k], grecv_ref.at[source], g_send_sem.at[k], g_recv_sem.at[k], {"ctx": source}
        )
        copy.wait_send()
        copy = remote(
            xsend.at[k], xrecv_ref.at[source], x_send_sem.at[k], x_recv_sem.at[k], {"ctx": source}
        )
        copy.wait_recv()
        copy.wait_send()

    for copy in sent:
        copy.wait_send()
    for copy in outs:
        copy.wait()


def forward_call(q, k, v, res, qend, gated, pick_two, pick_both, w_out):
    bf, f32 = jnp.bfloat16, jnp.float32
    vmem = pl.BlockSpec(memory_space=pltpu.VMEM)
    shape = jax.ShapeDtypeStruct
    return pl.pallas_call(
        forward_kernel,
        out_shape=(
            shape((256, 512), bf),
            shape((4, 256, 128), f32),
            shape((256, 512), bf),
            shape((256, 128), f32),
            shape((16, 96, 512), bf),
            shape((16, 96, 512), bf),
            shape((192, 1536), f32),
            shape((2, 4, 2, 2, 256, 512), bf),
        ),
        in_specs=[vmem] * 9,
        out_specs=[vmem] * 7 + [pl.BlockSpec(memory_space=pl.ANY)],
        scratch_shapes=[
            pltpu.VMEM((2, 4, 2, 2, 256, 512), bf),
            pltpu.VMEM((4, 256, 128), f32),
            pltpu.VMEM((4, 256, 128), f32),
            pltpu.VMEM((4, 256, 128), f32),
            pltpu.VMEM((16, 96, 512), bf),
            pltpu.VMEM((16, 96, 512), bf),
            pltpu.VMEM((8, 192, 1536), bf),
            pltpu.VMEM((8, 192, 1536), bf),
            pltpu.VMEM((8, 256), f32),
            pltpu.VMEM((8, 8, 256), f32),
            pltpu.SemaphoreType.DMA((30,)),
            pltpu.SemaphoreType.DMA((2, 4, 2, 2)),
            pltpu.SemaphoreType.DMA((2, 4)),
            pltpu.SemaphoreType.DMA((16,)),
            pltpu.SemaphoreType.DMA((16,)),
            pltpu.SemaphoreType.DMA((16,)),
            pltpu.SemaphoreType.DMA((16,)),
            pltpu.SemaphoreType.DMA((8,)),
            pltpu.SemaphoreType.DMA((8,)),
            pltpu.SemaphoreType.DMA((8,)),
            pltpu.SemaphoreType.DMA((8,)),
        ],
        compiler_params=pltpu.CompilerParams(
            collective_id=0, has_side_effects=True, vmem_limit_bytes=56 * 2**20
        ),
        name="forward",
    )(q, k, v, res, qend, gated, pick_two, pick_both, w_out)


def shards(
    residual, queries, keys, values, frame_lengths, routes, route_gates, w_in, w_out, out_grad
):
    n_ctx = lax.axis_size("ctx")
    n_grp = lax.axis_size("grp")
    tok_rows, feat_dev = residual.shape
    exp_dev = w_in.shape[0]
    head_dim = HEAD_DIM
    heads_dev = feat_dev // head_dim
    seq_len = tok_rows * n_ctx
    experts_all = exp_dev * n_ctx
    capacity = 6 * tok_rows // experts_all
    width_all = feat_dev * n_grp
    score_scale = head_dim ** (-0.5)
    expert_flat = routes.reshape(-1)
    onehot = (expert_flat[:, None] == jnp.arange(experts_all, dtype=jnp.int32)[None, :]).astype(
        jnp.int32
    )
    earlier = jnp.cumsum(onehot, axis=0) - onehot
    ranks = jnp.sum(earlier * onehot, axis=1)
    row_index = (expert_flat * capacity + ranks).reshape(tok_rows, 2)
    slot_ids = jnp.arange(experts_all * capacity, dtype=jnp.int32)
    pick = [
        (slot_ids[:, None] == row_index[None, :, a]).astype(jnp.bfloat16) for a in range(2)
    ]
    pick_both = pick[0] + pick[1]
    pick_two = jnp.concatenate(pick, axis=1)

    def to_experts(rows):
        rows = rows.reshape(n_ctx, exp_dev * capacity, feat_dev)
        recv = lax.all_to_all(rows, "ctx", split_axis=0, concat_axis=0, tiled=True)
        recv = recv.reshape(n_ctx, exp_dev, capacity, feat_dev)
        return recv.transpose(1, 0, 2, 3).reshape(exp_dev, n_ctx * capacity, feat_dev)

    def to_tokens(rows):
        rows = rows.reshape(exp_dev, n_ctx, capacity, feat_dev).transpose(1, 0, 2, 3)
        rows = rows.reshape(n_ctx, exp_dev * capacity, feat_dev)
        back = lax.all_to_all(rows, "ctx", split_axis=0, concat_axis=0, tiled=True)
        return back.reshape(experts_all * capacity, feat_dev)

    def sum_scatter(partial):
        flat = partial.astype(jnp.bfloat16).reshape(-1, partial.shape[-1])
        return lax.psum_scatter(flat, "grp", scatter_dimension=0, tiled=True).astype(jnp.float32)

    def gather(shard):
        full = lax.all_gather(shard, "grp", axis=0, tiled=True)
        return full.reshape(exp_dev, n_ctx * capacity, -1)

    out_grad_f = out_grad.astype(jnp.float32)
    gated = jnp.concatenate(
        [(route_gates[:, a : a + 1] * out_grad_f).astype(jnp.bfloat16) for a in range(2)], axis=0
    )
    ctx_index = lax.axis_index("ctx")
    frame_ends = jnp.cumsum(frame_lengths)
    positions = ctx_index * tok_rows + jnp.arange(tok_rows, dtype=jnp.int32)
    ends = jnp.min(
        jnp.where(frame_ends[None, :] > positions[:, None], frame_ends[None, :], seq_len), axis=1
    )
    qend = jnp.broadcast_to(ends[:, None], (tok_rows, 128)).astype(jnp.int32)
    attn, lse, mixed, inv_wide, rows_recv, grads_recv, act_grad, kv_all = forward_call(
        queries,
        keys,
        values,
        residual,
        qend,
        gated,
        pick_two.reshape(n_ctx, exp_dev * capacity, 2 * tok_rows),
        pick_both.reshape(n_ctx, exp_dev * capacity, tok_rows),
        w_out,
    )
    mixed_f = mixed.astype(jnp.float32)
    inv_rms = inv_wide[:, 0]
    attn_heads = attn.reshape(tok_rows, heads_dev, head_dim)

    def by_expert(rows):
        rows = rows.reshape(n_ctx, exp_dev, capacity, feat_dev)
        return rows.transpose(1, 0, 2, 3).reshape(exp_dev, n_ctx * capacity, feat_dev)

    rows_recv, grads_recv = by_expert(rows_recv), by_expert(grads_recv)
    pre_act = sum_scatter(
        jnp.einsum("erf,efh->erh", rows_recv, w_in, preferred_element_type=jnp.float32)
    )
    pre_grad = gather((act_grad * gelu_slope(pre_act)).astype(jnp.bfloat16))
    act_shard, pre_grad = lax.optimization_barrier(
        (gelu_tanh(pre_act).astype(jnp.bfloat16), pre_grad)
    )
    activated = gather(act_shard)
    row_grad = jnp.einsum(
        "erh,efh->erf", pre_grad, w_in, preferred_element_type=jnp.float32
    ).astype(jnp.bfloat16)
    normed_grad = jnp.dot(pick_both.T, to_tokens(row_grad), preferred_element_type=jnp.float32)
    w_in_grad = jnp.einsum(
        "erf,erh->efh", rows_recv, pre_grad, preferred_element_type=jnp.float32
    ).astype(jnp.bfloat16)
    expert_out = jnp.einsum(
        "erh,ehf->erf", activated, w_out, preferred_element_type=jnp.float32
    ).astype(jnp.bfloat16)
    returned = jnp.dot(pick_two.T, to_tokens(expert_out), preferred_element_type=jnp.float32)
    combined = (
        route_gates[:, 0:1] * returned[:tok_rows] + route_gates[:, 1:2] * returned[tok_rows:]
    )
    layer_out = (mixed_f + combined).astype(jnp.bfloat16)
    w_out_grad = jnp.einsum(
        "erh,erf->ehf", activated, grads_recv, preferred_element_type=jnp.float32
    ).astype(jnp.bfloat16)
    input_grad_f = out_grad_f + inv_rms[:, None] * normed_grad
    input_grad = input_grad_f.astype(jnp.bfloat16)
    grad_heads = input_grad.reshape(tok_rows, heads_dev, head_dim)
    row_dot = jnp.sum(grad_heads.astype(jnp.float32) * attn_heads.astype(jnp.float32), axis=2).T
    core, chip = ctx_index % 2, ctx_index // 2
    chip_y, chip_x = chip // 4, chip % 4
    there = [
        ((chip_y + dy) % 2 * 4 + (chip_x + dx) % 4) * 2 + (core + dc) % 2
        for dy in range(2)
        for dx in range(4)
        for dc in range(2)
    ]
    there = jnp.stack(there)
    key_pos = (there[:, None] * tok_rows + jnp.arange(tok_rows)[None, :]).reshape(-1)
    key_heads_all = kv_all[:, :, :, 0].reshape(seq_len, heads_dev, head_dim)
    value_heads_all = kv_all[:, :, :, 1].reshape(seq_len, heads_dev, head_dim)
    query_heads = queries.reshape(tok_rows, heads_dev, head_dim)
    scores = (
        jnp.einsum("qhd,khd->hqk", query_heads, key_heads_all, preferred_element_type=jnp.float32)
        * score_scale
    )
    scores = jnp.where((key_pos[None, :] < ends[:, None])[None], scores, -jnp.inf)
    log_total = lse[:, :, 0:1] / LOG2E
    prob_f = jnp.exp(scores - log_total)
    prob_all = prob_f.astype(jnp.bfloat16)
    dprob = jnp.einsum(
        "qhd,khd->hqk", grad_heads, value_heads_all, preferred_element_type=jnp.float32
    )
    dscore_all = (prob_f * (dprob - row_dot[:, :, None]) * score_scale).astype(jnp.bfloat16)
    query_sum = jnp.einsum(
        "hqk,khd->qhd", dscore_all, key_heads_all, preferred_element_type=jnp.float32
    )
    key_term = jnp.einsum(
        "hqk,qhd->khd", dscore_all, query_heads, preferred_element_type=jnp.float32
    ).reshape(seq_len, feat_dev)
    value_term = jnp.einsum(
        "hqk,qhd->khd", prob_all, grad_heads, preferred_element_type=jnp.float32
    ).reshape(seq_len, feat_dev)
    both_terms = jnp.concatenate([key_term, value_term], axis=1)
    both_terms = both_terms.reshape(n_ctx, tok_rows, 2 * feat_dev)
    both_terms = (
        jnp.zeros_like(both_terms).at[there].set(both_terms).reshape(seq_len, 2 * feat_dev)
    )
    key_grad_f, value_grad_f = (
        lax.psum_scatter(
            both_terms[:, :feat_dev].astype(jnp.bfloat16), "ctx", scatter_dimension=0, tiled=True
        ).astype(jnp.float32),
        lax.psum_scatter(
            both_terms[:, feat_dev:].astype(jnp.bfloat16), "ctx", scatter_dimension=0, tiled=True
        ).astype(jnp.float32),
    )
    query_grad = query_sum.reshape(tok_rows, feat_dev).astype(jnp.bfloat16)
    return (
        layer_out,
        input_grad,
        query_grad,
        key_grad_f.astype(jnp.bfloat16),
        value_grad_f.astype(jnp.bfloat16),
        w_in_grad,
        w_out_grad,
    )


def solution(mesh):
    in_specs = (
        P("ctx", "grp"),
        P("ctx", "grp"),
        P("ctx", "grp"),
        P("ctx", "grp"),
        P(),
        P("ctx", None),
        P("ctx", None),
        P("ctx", "grp", None),
        P("ctx", None, "grp"),
        P("ctx", "grp"),
    )
    out_specs = (
        P("ctx", "grp"),
        P("ctx", "grp"),
        P("ctx", "grp"),
        P("ctx", "grp"),
        P("ctx", "grp"),
        P("ctx", "grp", None),
        P("ctx", None, "grp"),
    )
    return jax.shard_map(shards, mesh=mesh, in_specs=in_specs, out_specs=out_specs, check_vma=False)
```

```python
import jax
import jax.numpy as jnp
from jax import lax
from jax.experimental import pallas as pl
from jax.experimental.pallas import tpu as pltpu
from jax.sharding import PartitionSpec as P

HEAD_DIM = 128


gelu_coef = 0.7978845608028654


def gelu_tanh(field):
    return 0.5 * field * (1.0 + jnp.tanh(gelu_coef * (field + 0.044715 * field * field * field)))


def gelu_slope(field):
    tanh_val = jnp.tanh(gelu_coef * (field + 0.044715 * field * field * field))
    return 0.5 * (1.0 + tanh_val) + 0.5 * field * (1.0 - tanh_val * tanh_val) * gelu_coef * (
        1.0 + 3.0 * 0.044715 * field * field
    )


MESH_ID = pl.DeviceIdType.MESH
LOG2E = 1.4426950408889634
LOW = -1e30


def dot_nt(a, b):
    return lax.dot_general(a, b, (((1,), (1,)), ((), ())), preferred_element_type=jnp.float32)


def dot_tn(a, b):
    return lax.dot_general(a, b, (((0,), (0,)), ((), ())), preferred_element_type=jnp.float32)


def dot_nn(a, b):
    return jnp.dot(a, b, preferred_element_type=jnp.float32)


def greet():
    me = lax.axis_index("ctx")
    grp = lax.axis_index("grp")
    barrier = pltpu.get_barrier_semaphore()

    @pl.loop(1, 16)
    def _(k):
        pl.semaphore_signal(
            barrier, inc=1, device_id={"ctx": lax.rem(me + k, 16)}, device_id_type=MESH_ID
        )

    @pl.loop(1, 8)
    def _(k):
        pl.semaphore_signal(
            barrier, inc=1, device_id={"grp": lax.rem(grp + k, 8)}, device_id_type=MESH_ID
        )

    pl.semaphore_wait(barrier, 22)


def remote(src, dst, send_sem, recv_sem, where):
    return pltpu.make_async_remote_copy(
        src_ref=src,
        dst_ref=dst,
        send_sem=send_sem,
        recv_sem=recv_sem,
        device_id=where,
        device_id_type=MESH_ID,
    )


def forward_kernel(
    q_ref, k_ref, v_ref, res_ref, qend_ref, gated_ref, pick_two_ref, pick_both_ref, w_out_ref,
    attn_ref, lse_ref, mixed_ref, inv_ref, xrecv_ref, grecv_ref, act_grad_ref, kv_out_ref,
    kv, m_s, l_s, acc_s, gsend, xsend, psend, precv, sq_send, sq_recv,
    kv_send_sem, kv_recv_sem, out_sem, g_send_sem, g_recv_sem, x_send_sem, x_recv_sem,
    p_send_sem, p_recv_sem, sq_send_sem, sq_recv_sem,
):
    me = lax.axis_index("ctx")
    grp = lax.axis_index("grp")
    core = lax.rem(me, 2)
    chip = me // 2
    x = lax.rem(chip, 4)
    yh = chip // 4

    def device(dy, dx, dc):
        there = lax.rem(yh + dy, 2) * 4 + lax.rem(x + dx, 4)
        return {"ctx": there * 2 + lax.rem(core + dc, 2)}

    greet()

    copies = {}
    sent = []

    def move(src, slot, where):
        copy = remote(src, kv.at[slot], kv_send_sem.at[len(sent)], kv_recv_sem.at[slot], where)
        copy.start()
        copies[slot] = copy
        sent.append(copy)

    def own(which):
        return k_ref if which == 0 else v_ref

    right, left = device(0, 1, 0), device(0, 3, 0)
    sibling, partner = device(0, 0, 1), device(1, 0, 0)
    for which in range(2):
        move(own(which), (1, 0, 0, which), partner)
        move(own(which), (0, 3, 0, which), right)
        move(own(which), (0, 1, 0, which), left)
        move(own(which), (0, 0, 1, which), sibling)
    kv[0, 0, 0, 0] = k_ref[...]
    kv[0, 0, 0, 1] = v_ref[...]

    @pl.loop(0, 16)
    def _(k):
        there = lax.rem(me + k, 16)
        gsend[k] = dot_nn(pick_two_ref[there], gated_ref[...]).astype(jnp.bfloat16)

        @pl.when(k > 0)
        def _():
            remote(
                gsend.at[k], grecv_ref.at[me], g_send_sem.at[k], g_recv_sem.at[k], {"ctx": there}
            ).start()

    grecv_ref[me] = gsend[0]
    m_s[...] = jnp.full_like(m_s, LOW)
    l_s[...] = jnp.zeros_like(l_s)
    acc_s[...] = jnp.zeros_like(acc_s)
    outs = []

    def wait_slot(dy, dx, dc, which):
        copies[(dy, dx, dc, which)].wait_recv()

    def forward(dy, dx, which):
        wait_slot(dy, dx, 0, which)
        move(kv.at[dy, dx, 0, which], (dy, dx, 1, which), sibling)

    def relay(dy):
        forward(dy, 3, 0)
        move(kv.at[dy, 3, 0, 0], (dy, 2, 0, 0), right)
        forward(dy, 1, 1)
        move(kv.at[dy, 1, 0, 1], (dy, 2, 0, 1), left)
        forward(dy, 3, 1)
        forward(dy, 1, 0)

    def attend(dy, dx):
        for which in range(2):
            wait_slot(dy, dx, 1, which)
        copy = pltpu.make_async_copy(kv.at[dy, dx], kv_out_ref.at[dy, dx], out_sem.at[dy, dx])
        copy.start()
        outs.append(copy)
        there = lax.rem(yh + dy, 2) * 4 + lax.rem(x + dx, 4)
        lane = lax.broadcasted_iota(jnp.int32, (256, 256), 1)
        qend = qend_ref[:, 0:1]
        limits = [qend - (there * 512 + lax.rem(core + dc, 2) * 256) for dc in range(2)]

        @pl.loop(0, 4)
        def _(h):
            cols = pl.ds(pl.multiple_of(h * 128, 128), 128)
            qh = q_ref[:, cols]
            scores = []
            for dc in range(2):
                s = dot_nt(qh, kv[dy, dx, dc, 0, :, cols]) * (LOG2E * HEAD_DIM**-0.5)
                scores.append(jnp.where(lane < limits[dc], s, LOW))
            top = jnp.max(jnp.maximum(scores[0], scores[1]), axis=1, keepdims=True)
            m_old = m_s[h]
            m_new = jnp.maximum(m_old, top)
            alpha = jnp.exp2(m_old - m_new)
            probs = [jnp.exp2(s - m_new[:, 0:1]) for s in scores]
            total = jnp.sum(probs[0] + probs[1], axis=1, keepdims=True)
            m_s[h] = m_new
            l_s[h] = l_s[h] * alpha + total
            acc = acc_s[h] * alpha
            for dc in range(2):
                acc += dot_nn(probs[dc].astype(jnp.bfloat16), kv[dy, dx, dc, 1, :, cols])
            acc_s[h] = acc

    attend(0, 0)
    for which in range(2):
        wait_slot(1, 0, 0, which)
        move(kv.at[1, 0, 0, which], (1, 3, 0, which), right)
        move(kv.at[1, 0, 0, which], (1, 1, 0, which), left)
        move(kv.at[1, 0, 0, which], (1, 0, 1, which), sibling)
    relay(0)
    attend(0, 3)
    attend(0, 1)

    @pl.loop(1, 16)
    def _(k):
        source = lax.rem(me + 16 - k, 16)
        remote(
            gsend.at[k], grecv_ref.at[source], g_send_sem.at[k], g_recv_sem.at[k], {"ctx": source}
        ).wait_recv()

    @pl.loop(0, 8)
    def _(k):
        there = lax.rem(grp + k, 8)
        expert = there // 4
        first = lax.rem(there, 4) * 4
        rows = grecv_ref[pl.ds(first, 4), pl.ds(pl.multiple_of(expert * 48, 16), 48), :]
        rows = rows.reshape(192, 512)

        @pl.loop(0, 3)
        def _(part):
            cols = pl.ds(pl.multiple_of(part * 512, 512), 512)
            psend[k, :, cols] = dot_nt(rows, w_out_ref[expert, cols, :]).astype(jnp.bfloat16)

        @pl.when(k > 0)
        def _():
            remote(
                psend.at[k], precv.at[k], p_send_sem.at[k], p_recv_sem.at[k], {"grp": there}
            ).start()

    relay(1)
    attend(1, 0)
    for which in range(2):
        forward(0, 2, which)
    attend(0, 2)
    attend(1, 3)
    attend(1, 1)
    for which in range(2):
        forward(1, 2, which)
    attend(1, 2)

    squares = jnp.zeros((256, 1), jnp.float32)
    for h in range(4):
        cols = slice(h * 128, h * 128 + 128)
        out = (acc_s[h] / l_s[h]).astype(jnp.bfloat16)
        lse_ref[h] = jnp.transpose(m_s[h] + jnp.log2(l_s[h]))[0:8]
        attn_ref[:, cols] = out
        mixed = (res_ref[:, cols].astype(jnp.float32) + out.astype(jnp.float32)).astype(
            jnp.bfloat16
        )
        mixed_ref[:, cols] = mixed
        mixed_f = mixed.astype(jnp.float32)
        squares += jnp.sum(mixed_f * mixed_f, axis=1, keepdims=True)
    turned = jnp.transpose(jnp.broadcast_to(squares, (256, 128)))
    sq_send[...] = turned[0:8]
    sq_recv[grp] = turned[0:8]

    @pl.loop(1, 8)
    def _(k):
        there = lax.rem(grp + k, 8)
        remote(
            sq_send, sq_recv.at[grp], sq_send_sem.at[k], sq_recv_sem.at[k], {"grp": there}
        ).start()

    @pl.loop(1, 8)
    def _(k):
        source = lax.rem(grp + 8 - k, 8)
        copy = remote(
            sq_send, sq_recv.at[source], sq_send_sem.at[k], sq_recv_sem.at[k], {"grp": source}
        )
        copy.wait_recv()
        copy.wait_send()

    total = sq_recv[0]
    for k in range(1, 8):
        total = total + sq_recv[k]
    inv = lax.rsqrt(total / 4096 + 1e-06)
    inv = jnp.transpose(jnp.concatenate([inv] * 16, axis=0))
    inv_ref[...] = inv
    normed = jnp.concatenate(
        [
            (mixed_ref[:, h * 128 : h * 128 + 128].astype(jnp.float32) * inv).astype(jnp.bfloat16)
            for h in range(4)
        ],
        axis=1,
    )
    attn_rows = normed

    @pl.loop(0, 16)
    def _(k):
        there = lax.rem(me + k, 16)
        xsend[k] = dot_nn(pick_both_ref[there], attn_rows).astype(jnp.bfloat16)

        @pl.when(k > 0)
        def _():
            remote(
                xsend.at[k], xrecv_ref.at[me], x_send_sem.at[k], x_recv_sem.at[k], {"ctx": there}
            ).start()

    xrecv_ref[me] = xsend[0]

    @pl.loop(1, 8)
    def _(k):
        source = lax.rem(grp + 8 - k, 8)
        copy = remote(
            psend.at[k], precv.at[k], p_send_sem.at[k], p_recv_sem.at[k], {"grp": source}
        )
        copy.wait_recv()
        copy.wait_send()

    @pl.loop(0, 12)
    def _(part):
        rows = pl.ds(pl.multiple_of(part * 16, 16), 16)
        total = psend[0, rows, :].astype(jnp.float32)
        for k in range(1, 8):
            total += precv[k, rows, :].astype(jnp.float32)
        act_grad_ref[rows, :] = total

    @pl.loop(1, 16)
    def _(k):
        source = lax.rem(me + 16 - k, 16)
        copy = remote(
            gsend.at[k], grecv_ref.at[source], g_send_sem.at[k], g_recv_sem.at[k], {"ctx": source}
        )
        copy.wait_send()
        copy = remote(
            xsend.at[k], xrecv_ref.at[source], x_send_sem.at[k], x_recv_sem.at[k], {"ctx": source}
        )
        copy.wait_recv()
        copy.wait_send()

    for copy in sent:
        copy.wait_send()
    for copy in outs:
        copy.wait()


def forward_call(q, k, v, res, qend, gated, pick_two, pick_both, w_out):
    bf, f32 = jnp.bfloat16, jnp.float32
    vmem = pl.BlockSpec(memory_space=pltpu.VMEM)
    shape = jax.ShapeDtypeStruct
    return pl.pallas_call(
        forward_kernel,
        out_shape=(
            shape((256, 512), bf),
            shape((4, 8, 256), f32),
            shape((256, 512), bf),
            shape((256, 128), f32),
            shape((16, 96, 512), bf),
            shape((16, 96, 512), bf),
            shape((192, 1536), f32),
            shape((2, 4, 2, 2, 256, 512), bf),
        ),
        in_specs=[vmem] * 9,
        out_specs=[vmem] * 7 + [pl.BlockSpec(memory_space=pl.ANY)],
        scratch_shapes=[
            pltpu.VMEM((2, 4, 2, 2, 256, 512), bf),
            pltpu.VMEM((4, 256, 128), f32),
            pltpu.VMEM((4, 256, 128), f32),
            pltpu.VMEM((4, 256, 128), f32),
            pltpu.VMEM((16, 96, 512), bf),
            pltpu.VMEM((16, 96, 512), bf),
            pltpu.VMEM((8, 192, 1536), bf),
            pltpu.VMEM((8, 192, 1536), bf),
            pltpu.VMEM((8, 256), f32),
            pltpu.VMEM((8, 8, 256), f32),
            pltpu.SemaphoreType.DMA((30,)),
            pltpu.SemaphoreType.DMA((2, 4, 2, 2)),
            pltpu.SemaphoreType.DMA((2, 4)),
            pltpu.SemaphoreType.DMA((16,)),
            pltpu.SemaphoreType.DMA((16,)),
            pltpu.SemaphoreType.DMA((16,)),
            pltpu.SemaphoreType.DMA((16,)),
            pltpu.SemaphoreType.DMA((8,)),
            pltpu.SemaphoreType.DMA((8,)),
            pltpu.SemaphoreType.DMA((8,)),
            pltpu.SemaphoreType.DMA((8,)),
        ],
        compiler_params=pltpu.CompilerParams(
            collective_id=0, has_side_effects=True, vmem_limit_bytes=56 * 2**20
        ),
        name="forward",
    )(q, k, v, res, qend, gated, pick_two, pick_both, w_out)


def backward_kernel(
    q_ref, kv_ref, lse_ref, attn_ref, qend_ref, og_ref, inv_ref, pick_ref, rg_ref,
    ig_ref, dq_ref, dk_ref, dv_ref,
    rg_recv, normed_grad, row_dot, dqt, own_terms, sib_send, sib_recv, ring_send,
    ring_recv, part_send, part_recv,
    rg_send_sem, rg_recv_sem, sib_send_sem, sib_recv_sem, ring_send_sem, ring_recv_sem,
    part_send_sem, part_recv_sem,
):
    me = lax.axis_index("ctx")
    core = lax.rem(me, 2)
    chip = me // 2
    x = lax.rem(chip, 4)
    yh = chip // 4
    bf, f32 = jnp.bfloat16, jnp.float32

    def device(dy, dx, dc):
        there = lax.rem(yh + dy, 2) * 4 + lax.rem(x + dx, 4)
        return {"ctx": there * 2 + lax.rem(core + dc, 2)}

    right, left = device(0, 1, 0), device(0, 3, 0)
    sibling, partner = device(0, 0, 1), device(1, 0, 0)
    greet_ctx()

    @pl.loop(1, 16)
    def _(k):
        there = lax.rem(me + k, 16)
        remote(
            rg_ref.at[there], rg_recv.at[k], rg_send_sem.at[k], rg_recv_sem.at[k], {"ctx": there}
        ).start()

    dqt[...] = jnp.zeros_like(dqt)
    normed_grad[...] = dot_tn(pick_ref[me], rg_ref[me])

    @pl.loop(1, 16)
    def _(k):
        source = lax.rem(me + 16 - k, 16)
        remote(
            rg_ref.at[source], rg_recv.at[k], rg_send_sem.at[k], rg_recv_sem.at[k], {"ctx": source}
        ).wait_recv()
        normed_grad[...] += dot_tn(pick_ref[source], rg_recv[k])

    for h in range(4):
        cols = slice(h * 128, h * 128 + 128)
        grad = og_ref[:, cols].astype(f32) + inv_ref[...] * normed_grad[:, cols]
        grad = grad.astype(bf)
        ig_ref[:, cols] = grad
        dots = jnp.sum(grad.astype(f32) * attn_ref[:, cols].astype(f32), axis=1, keepdims=True)
        row_dot[h] = jnp.transpose(jnp.broadcast_to(dots, (256, 128)))[0:8]

    scale = HEAD_DIM**-0.5

    def terms(dy, dx):
        there = lax.rem(yh + dy, 2) * 4 + lax.rem(x + dx, 4)
        sub = lax.broadcasted_iota(jnp.int32, (256, 256), 0)
        qend = qend_ref[0:1, :]
        limits = [qend - (there * 512 + lax.rem(core + dc, 2) * 256) for dc in range(2)]

        @pl.loop(0, 4)
        def _(h):
            cols = pl.ds(pl.multiple_of(h * 128, 128), 128)
            qh = q_ref[:, cols]
            gh = ig_ref[:, cols]
            lse = lse_ref[h][0:1, :]
            dots = row_dot[h][0:1, :]
            for dc in range(2):
                kh = kv_ref[dy, dx, dc, 0, :, cols]
                vh = kv_ref[dy, dx, dc, 1, :, cols]
                s = dot_nt(kh, qh) * (LOG2E * scale)
                p = jnp.exp2(jnp.where(sub < limits[dc], s, LOW) - lse)
                dp = dot_nt(vh, gh)
                ds = (p * (dp - dots) * scale).astype(bf)
                dk = dot_nn(ds, qh).astype(bf)
                dv = dot_nn(p.astype(bf), gh).astype(bf)
                dqt[h] += dot_tn(kh, ds)
                to = own_terms if dc == 0 else sib_send
                to[dy, dx, 0, :, cols] = dk
                to[dy, dx, 1, :, cols] = dv

        for which in range(2):
            sib_copy(dy, dx, which).start()

    def sib_copy(dy, dx, which):
        return remote(
            sib_send.at[dy, dx, which],
            sib_recv.at[dy, dx, which],
            sib_send_sem.at[dy, dx, which],
            sib_recv_sem.at[dy, dx, which],
            sibling,
        )

    def ring_copy(dy, dx, which):
        to = (dx + 3) % 4 if which == 0 else (dx + 1) % 4
        return remote(
            ring_send.at[dy, dx, which],
            ring_recv.at[dy, to, which],
            ring_send_sem.at[dy, dx, which],
            ring_recv_sem.at[dy, to, which],
            right if which == 0 else left,
        )

    def arrival(dy, dx, which):
        return ring_copy(dy, (dx + 1) % 4 if which == 0 else (dx + 3) % 4, which)

    def total_of(dy, dx, which, ring):
        sib_copy(dy, dx, which).wait_recv()
        if ring:
            arrival(dy, dx, which).wait_recv()
        sums = own_terms[dy, dx, which].astype(f32) + sib_recv[dy, dx, which].astype(f32)
        if ring:
            sums = sums + ring_recv[dy, dx, which].astype(f32)
        return sums

    def send_ring(dy, dx, which, ring):
        ring_send[dy, dx, which] = total_of(dy, dx, which, ring).astype(bf)
        ring_copy(dy, dx, which).start()

    def part_copy(which):
        return remote(
            part_send.at[which],
            part_recv.at[which],
            part_send_sem.at[which],
            part_recv_sem.at[which],
            partner,
        )

    terms(1, 3)
    terms(1, 1)
    send_ring(1, 3, 0, False)
    send_ring(1, 1, 1, False)
    terms(1, 2)
    terms(1, 0)
    send_ring(1, 2, 0, True)
    send_ring(1, 2, 1, True)
    terms(0, 3)
    terms(0, 1)
    send_ring(1, 1, 0, True)
    send_ring(1, 3, 1, True)
    send_ring(0, 3, 0, False)
    send_ring(0, 1, 1, False)
    terms(0, 2)
    for which in range(2):
        part_send[which] = total_of(1, 0, which, True).astype(bf)
        part_copy(which).start()
    send_ring(0, 2, 0, True)
    send_ring(0, 2, 1, True)
    terms(0, 0)
    for h in range(4):
        dq_ref[:, h * 128 : h * 128 + 128] = jnp.transpose(dqt[h]).astype(bf)
    send_ring(0, 1, 0, True)
    send_ring(0, 3, 1, True)
    for which in range(2):
        sums = total_of(0, 0, which, True)
        part_copy(which).wait_recv()
        sums = sums + part_recv[which].astype(f32)
        if which == 0:
            dk_ref[...] = sums.astype(bf)
        else:
            dv_ref[...] = sums.astype(bf)

    for dy in range(2):
        for dx in range(4):
            for which in range(2):
                sib_copy(dy, dx, which).wait_send()
                if dx > 0:
                    ring_copy(dy, dx, which).wait_send()
    for which in range(2):
        part_copy(which).wait_send()

    @pl.loop(1, 16)
    def _(k):
        there = lax.rem(me + k, 16)
        remote(
            rg_ref.at[there], rg_recv.at[k], rg_send_sem.at[k], rg_recv_sem.at[k], {"ctx": there}
        ).wait_send()


def greet_ctx():
    me = lax.axis_index("ctx")
    barrier = pltpu.get_barrier_semaphore()

    @pl.loop(1, 16)
    def _(k):
        pl.semaphore_signal(
            barrier, inc=1, device_id={"ctx": lax.rem(me + k, 16)}, device_id_type=MESH_ID
        )

    pl.semaphore_wait(barrier, 15)


def backward_call(q, kv, lse, attn, qend, og, inv, pick, rg):
    bf, f32 = jnp.bfloat16, jnp.float32
    vmem = pl.BlockSpec(memory_space=pltpu.VMEM)
    shape = jax.ShapeDtypeStruct
    return pl.pallas_call(
        backward_kernel,
        out_shape=(shape((256, 512), bf),) * 4,
        in_specs=[vmem] * 9,
        out_specs=(vmem,) * 4,
        scratch_shapes=[
            pltpu.VMEM((16, 96, 512), bf),
            pltpu.VMEM((256, 512), f32),
            pltpu.VMEM((4, 8, 256), f32),
            pltpu.VMEM((4, 128, 256), f32),
            pltpu.VMEM((2, 4, 2, 256, 512), bf),
            pltpu.VMEM((2, 4, 2, 256, 512), bf),
            pltpu.VMEM((2, 4, 2, 256, 512), bf),
            pltpu.VMEM((2, 4, 2, 256, 512), bf),
            pltpu.VMEM((2, 4, 2, 256, 512), bf),
            pltpu.VMEM((2, 256, 512), bf),
            pltpu.VMEM((2, 256, 512), bf),
            pltpu.SemaphoreType.DMA((16,)),
            pltpu.SemaphoreType.DMA((16,)),
            pltpu.SemaphoreType.DMA((2, 4, 2)),
            pltpu.SemaphoreType.DMA((2, 4, 2)),
            pltpu.SemaphoreType.DMA((2, 4, 2)),
            pltpu.SemaphoreType.DMA((2, 4, 2)),
            pltpu.SemaphoreType.DMA((2,)),
            pltpu.SemaphoreType.DMA((2,)),
        ],
        compiler_params=pltpu.CompilerParams(
            collective_id=1, has_side_effects=True, vmem_limit_bytes=56 * 2**20
        ),
        name="backward",
    )(q, kv, lse, attn, qend, og, inv, pick, rg)


def shards(
    residual, queries, keys, values, frame_lengths, routes, route_gates, w_in, w_out, out_grad
):
    n_ctx = lax.axis_size("ctx")
    n_grp = lax.axis_size("grp")
    tok_rows, feat_dev = residual.shape
    exp_dev = w_in.shape[0]
    seq_len = tok_rows * n_ctx
    experts_all = exp_dev * n_ctx
    capacity = 6 * tok_rows // experts_all
    expert_flat = routes.reshape(-1)
    onehot = (expert_flat[:, None] == jnp.arange(experts_all, dtype=jnp.int32)[None, :]).astype(
        jnp.int32
    )
    earlier = jnp.cumsum(onehot, axis=0) - onehot
    ranks = jnp.sum(earlier * onehot, axis=1)
    row_index = (expert_flat * capacity + ranks).reshape(tok_rows, 2)
    slot_ids = jnp.arange(experts_all * capacity, dtype=jnp.int32)
    pick = [
        (slot_ids[:, None] == row_index[None, :, a]).astype(jnp.bfloat16) for a in range(2)
    ]
    pick_both = pick[0] + pick[1]
    pick_two = jnp.concatenate(pick, axis=1)

    def by_source(rows):
        rows = rows.reshape(exp_dev, n_ctx, capacity, feat_dev).transpose(1, 0, 2, 3)
        return rows.reshape(n_ctx, exp_dev * capacity, feat_dev)

    def to_tokens(rows):
        back = lax.all_to_all(by_source(rows), "ctx", split_axis=0, concat_axis=0, tiled=True)
        return back.reshape(experts_all * capacity, feat_dev)

    def sum_scatter(partial):
        flat = partial.astype(jnp.bfloat16).reshape(-1, partial.shape[-1])
        return lax.psum_scatter(flat, "grp", scatter_dimension=0, tiled=True).astype(jnp.float32)

    def gather(shard):
        full = lax.all_gather(shard, "grp", axis=0, tiled=True)
        return full.reshape(exp_dev, n_ctx * capacity, -1)

    out_grad_f = out_grad.astype(jnp.float32)
    gated = jnp.concatenate(
        [(route_gates[:, a : a + 1] * out_grad_f).astype(jnp.bfloat16) for a in range(2)], axis=0
    )
    ctx_index = lax.axis_index("ctx")
    frame_ends = jnp.cumsum(frame_lengths)
    positions = ctx_index * tok_rows + jnp.arange(tok_rows, dtype=jnp.int32)
    ends = jnp.min(
        jnp.where(frame_ends[None, :] > positions[:, None], frame_ends[None, :], seq_len), axis=1
    )
    qend = jnp.broadcast_to(ends[:, None], (tok_rows, 128)).astype(jnp.int32)
    attn, lse, mixed, inv_wide, rows_recv, grads_recv, act_grad, kv_all = forward_call(
        queries,
        keys,
        values,
        residual,
        qend,
        gated,
        pick_two.reshape(n_ctx, exp_dev * capacity, 2 * tok_rows),
        pick_both.reshape(n_ctx, exp_dev * capacity, tok_rows),
        w_out,
    )
    mixed_f = mixed.astype(jnp.float32)

    def by_expert(rows):
        rows = rows.reshape(n_ctx, exp_dev, capacity, feat_dev)
        return rows.transpose(1, 0, 2, 3).reshape(exp_dev, n_ctx * capacity, feat_dev)

    rows_recv, grads_recv = by_expert(rows_recv), by_expert(grads_recv)
    pre_act = sum_scatter(
        jnp.einsum("erf,efh->erh", rows_recv, w_in, preferred_element_type=jnp.float32)
    )
    pre_grad = gather((act_grad * gelu_slope(pre_act)).astype(jnp.bfloat16))
    act_shard, pre_grad = lax.optimization_barrier(
        (gelu_tanh(pre_act).astype(jnp.bfloat16), pre_grad)
    )
    activated = gather(act_shard)
    row_grad = jnp.einsum(
        "erh,efh->erf", pre_grad, w_in, preferred_element_type=jnp.float32
    ).astype(jnp.bfloat16)
    input_grad, query_grad, key_grad, value_grad = backward_call(
        queries,
        kv_all,
        lse,
        attn,
        jnp.broadcast_to(ends[None, :], (8, tok_rows)).astype(jnp.int32),
        out_grad,
        inv_wide,
        pick_both.reshape(n_ctx, exp_dev * capacity, tok_rows),
        by_source(row_grad),
    )
    w_in_grad = jnp.einsum(
        "erf,erh->efh", rows_recv, pre_grad, preferred_element_type=jnp.float32
    ).astype(jnp.bfloat16)
    expert_out = jnp.einsum(
        "erh,ehf->erf", activated, w_out, preferred_element_type=jnp.float32
    ).astype(jnp.bfloat16)
    returned = jnp.dot(pick_two.T, to_tokens(expert_out), preferred_element_type=jnp.float32)
    combined = (
        route_gates[:, 0:1] * returned[:tok_rows] + route_gates[:, 1:2] * returned[tok_rows:]
    )
    layer_out = (mixed_f + combined).astype(jnp.bfloat16)
    w_out_grad = jnp.einsum(
        "erh,erf->ehf", activated, grads_recv, preferred_element_type=jnp.float32
    ).astype(jnp.bfloat16)
    return (
        layer_out,
        input_grad,
        query_grad,
        key_grad,
        value_grad,
        w_in_grad,
        w_out_grad,
    )


def solution(mesh):
    in_specs = (
        P("ctx", "grp"),
        P("ctx", "grp"),
        P("ctx", "grp"),
        P("ctx", "grp"),
        P(),
        P("ctx", None),
        P("ctx", None),
        P("ctx", "grp", None),
        P("ctx", None, "grp"),
        P("ctx", "grp"),
    )
    out_specs = (
        P("ctx", "grp"),
        P("ctx", "grp"),
        P("ctx", "grp"),
        P("ctx", "grp"),
        P("ctx", "grp"),
        P("ctx", "grp", None),
        P("ctx", None, "grp"),
    )
    return jax.shard_map(shards, mesh=mesh, in_specs=in_specs, out_specs=out_specs, check_vma=False)
```

```python
import jax
import jax.numpy as jnp
from jax import lax
from jax.experimental import pallas as pl
from jax.experimental.pallas import tpu as pltpu
from jax.sharding import PartitionSpec as P

HEAD_DIM = 128


gelu_coef = 0.7978845608028654


def gelu_tanh(field):
    return 0.5 * field * (1.0 + jnp.tanh(gelu_coef * (field + 0.044715 * field * field * field)))


def gelu_slope(field):
    tanh_val = jnp.tanh(gelu_coef * (field + 0.044715 * field * field * field))
    return 0.5 * (1.0 + tanh_val) + 0.5 * field * (1.0 - tanh_val * tanh_val) * gelu_coef * (
        1.0 + 3.0 * 0.044715 * field * field
    )


MESH_ID = pl.DeviceIdType.MESH
LOG2E = 1.4426950408889634
LOW = -1e30


def dot_nt(a, b):
    return lax.dot_general(a, b, (((1,), (1,)), ((), ())), preferred_element_type=jnp.float32)


def dot_tn(a, b):
    return lax.dot_general(a, b, (((0,), (0,)), ((), ())), preferred_element_type=jnp.float32)


def dot_nn(a, b):
    return jnp.dot(a, b, preferred_element_type=jnp.float32)


def greet():
    me = lax.axis_index("ctx")
    grp = lax.axis_index("grp")
    barrier = pltpu.get_barrier_semaphore()

    @pl.loop(1, 16)
    def _(k):
        pl.semaphore_signal(
            barrier, inc=1, device_id={"ctx": lax.rem(me + k, 16)}, device_id_type=MESH_ID
        )

    @pl.loop(1, 8)
    def _(k):
        pl.semaphore_signal(
            barrier, inc=1, device_id={"grp": lax.rem(grp + k, 8)}, device_id_type=MESH_ID
        )

    pl.semaphore_wait(barrier, 22)


def remote(src, dst, send_sem, recv_sem, where):
    return pltpu.make_async_remote_copy(
        src_ref=src,
        dst_ref=dst,
        send_sem=send_sem,
        recv_sem=recv_sem,
        device_id=where,
        device_id_type=MESH_ID,
    )


def pick_two(rows_ref, there):
    rows = lax.broadcasted_iota(jnp.int32, (96, 512), 0) + there * 96
    return jnp.where(rows == rows_ref[0:1, :], 1.0, 0.0).astype(jnp.bfloat16)


def pick_both(rows_ref, there):
    rows = lax.broadcasted_iota(jnp.int32, (96, 256), 0) + there * 96
    hit = (rows == rows_ref[0:1, 0:256]) | (rows == rows_ref[0:1, 256:512])
    return jnp.where(hit, 1.0, 0.0).astype(jnp.bfloat16)


def grp_device(dy, dz):
    grp = lax.axis_index("grp")
    there = lax.rem(grp // 4 + dy, 2) * 4 + lax.rem(lax.rem(grp, 4) + dz, 4)
    return {"grp": there}


class GrpSum:
    def __init__(self, cut, part, recv, send_sem, recv_sem):
        self.cut, self.part, self.recv = cut, part, recv
        self.send_sem, self.recv_sem = send_sem, recv_sem
        self.head, self.rest = pl.ds(0, cut), pl.ds(cut, 192 - cut)

    def copy(self, number):
        part, head, rest = self.part, self.head, self.rest
        if number < 4:
            src, rows, where = part.at[1, number, head], head, grp_device(1, 0)
        elif number < 10:
            dz, dy = (number - 4) // 2 + 1, (number - 4) % 2
            src, rows, where = part.at[dy, dz, rest], rest, grp_device(0, dz)
        elif number < 13:
            dz = number - 9
            src, rows, where = part.at[0, dz, head], head, grp_device(0, dz)
        else:
            src, rows, where = part.at[1, 0, rest], rest, grp_device(1, 0)
        return remote(
            src,
            self.recv.at[number, rows],
            self.send_sem.at[number],
            self.recv_sem.at[number],
            where,
        )

    def send_first(self, dy, dz):
        if dy == 1:
            self.copy(dz).start()
        if dz > 0:
            self.copy(4 + (dz - 1) * 2 + dy).start()

    def add(self, target, start, size, slots, out):
        @pl.loop(0, size // 16)
        def _(step):
            rows = pl.ds(pl.multiple_of(start + step * 16, 16), 16)
            total = self.part[target[0], target[1], rows, :].astype(jnp.float32)
            for slot in slots:
                total += self.recv[slot, rows, :].astype(jnp.float32)
            out(rows, total)

    def second(self, dz):
        self.copy(dz).wait_recv()

        def out(rows, total):
            self.part[0, dz, rows, :] = total.astype(jnp.bfloat16)

        self.add((0, dz), 0, self.cut, [dz], out)
        self.copy(9 + dz).start()

    def second_rest(self):
        for number in (5, 7, 9):
            self.copy(number).wait_recv()

        def out(rows, total):
            self.part[1, 0, rows, :] = total.astype(jnp.bfloat16)

        self.add((1, 0), self.cut, 192 - self.cut, [5, 7, 9], out)
        self.copy(13).start()

    def finish(self, out):
        for number in (0, 4, 6, 8, 10, 11, 12, 13):
            self.copy(number).wait_recv()
        self.add((0, 0), 0, self.cut, [0, 10, 11, 12], out)
        self.add((0, 0), self.cut, 192 - self.cut, [4, 6, 8, 13], out)

    def drain(self):
        for number in range(14):
            self.copy(number).wait_send()


class GrpGather:
    def __init__(self, cut, full, send_sem, recv_sem):
        self.full, self.send_sem, self.recv_sem = full, send_sem, recv_sem
        self.head, self.rest = pl.ds(0, cut), pl.ds(cut, 192 - cut)

    def copy(self, number):
        head, rest = self.head, self.rest
        if number < 3:
            dz = number + 1
            src, dst, rows, where = (0, 0), (0, 4 - dz), head, grp_device(0, dz)
        elif number == 3:
            src, dst, rows, where = (0, 0), (1, 0), rest, grp_device(1, 0)
        elif number < 8:
            dz = number - 4
            src, dst, rows, where = (0, dz), (1, dz), head, grp_device(1, 0)
        else:
            dz, dy = (number - 8) // 2 + 1, (number - 8) % 2
            src, dst, rows, where = (dy, 0), (dy, 4 - dz), rest, grp_device(0, dz)
        return remote(
            self.full.at[src[0], src[1], rows],
            self.full.at[dst[0], dst[1], rows],
            self.send_sem.at[number],
            self.recv_sem.at[number],
            where,
        )

    def send_own(self):
        self.copy(3).start()
        for number in (0, 2, 1):
            self.copy(number).start()
        self.copy(4).start()
        for dz in (1, 3, 2):
            self.copy(8 + (dz - 1) * 2).start()

    def pass_rest(self):
        self.copy(3).wait_recv()
        for dz in (1, 3, 2):
            self.copy(8 + (dz - 1) * 2 + 1).start()

    def pass_head(self, dz):
        self.copy(3 - dz).wait_recv()
        self.copy(4 + dz).start()

    def wait_chunk(self, dy, dz):
        if dy == 1:
            self.copy(4 + dz).wait_recv()
        if dz > 0:
            self.copy(8 + (3 - dz) * 2 + dy).wait_recv()

    def drain(self):
        for number in range(14):
            self.copy(number).wait_send()


def chunk_of(dy, dz):
    grp = lax.axis_index("grp")
    return lax.rem(grp // 4 + dy, 2), lax.rem(lax.rem(grp, 4) + dz, 4) * 4


def chunk_rows(ref, dy, dz):
    expert, first = chunk_of(dy, dz)
    rows = ref[pl.ds(first, 4), pl.ds(pl.multiple_of(expert * 48, 16), 48), :]
    return rows.reshape(192, 512)


CHUNK_ORDER = [(1, 1), (1, 3), (1, 2), (1, 0), (0, 1), (0, 3), (0, 2), (0, 0)]


def return_rows(rows, dy, dz, send, recv, send_sem, recv_sem):
    me = lax.axis_index("ctx")
    expert, first = chunk_of(dy, dz)
    send[expert, pl.ds(first, 4)] = rows.reshape(4, 48, 512)

    @pl.loop(0, 4)
    def _(i):
        there = first + i

        @pl.when(there != me)
        def _():
            return_copy(expert, there, me, there, send, recv, send_sem, recv_sem).start()


def return_copy(expert, there, mine, partner, send, recv, send_sem, recv_sem):
    return remote(
        send.at[expert, there],
        recv.at[mine, expert],
        send_sem.at[expert, there],
        recv_sem.at[expert, mine],
        {"ctx": partner},
    )


def wait_returns(send, recv, send_sem, recv_sem):
    me = lax.axis_index("ctx")
    for expert in range(2):
        recv[me, expert] = send[expert, me]

        @pl.loop(1, 16)
        def _(k):
            source = lax.rem(me + k, 16)
            copy = return_copy(
                expert, source, source, source, send, recv, send_sem, recv_sem
            )
            copy.wait_recv()
            copy.wait_send()


def experts_kernel(
    x_ref, act_grad_ref, w_in_ref,
    act_ref, rg_ref, w_in_grad_ref,
    part, sums, full, rg_send,
    s_send_sem, s_recv_sem, f_send_sem, f_recv_sem, r_send_sem, r_recv_sem,
):
    bf = jnp.bfloat16
    greet()
    summing = GrpSum(112, part, sums, s_send_sem, s_recv_sem)
    gathering = GrpGather(112, full, f_send_sem, f_recv_sem)
    for dy, dz in CHUNK_ORDER:
        expert, _ = chunk_of(dy, dz)
        rows = chunk_rows(x_ref, dy, dz)

        @pl.loop(0, 3)
        def _(piece):
            cols = pl.ds(pl.multiple_of(piece * 512, 512), 512)
            part[dy, dz, :, cols] = dot_nn(rows, w_in_ref[expert, :, cols]).astype(bf)

        summing.send_first(dy, dz)
    for dz in (1, 3, 2):
        summing.second(dz)
    summing.second_rest()

    def activate(rows, pre):
        act_ref[rows, :] = gelu_tanh(pre).astype(bf)
        full[0, 0, rows, :] = (act_grad_ref[rows, :] * gelu_slope(pre)).astype(bf)

    summing.finish(activate)
    gathering.send_own()

    def row_grads(dy, dz):
        expert, _ = chunk_of(dy, dz)
        rows = dot_nt(full[dy, dz], w_in_ref[expert]).astype(bf)
        return_rows(rows, dy, dz, rg_send, rg_ref, r_send_sem, r_recv_sem)

    row_grads(0, 0)
    gathering.pass_rest()
    for dz in (1, 3, 2):
        gathering.pass_head(dz)
    for dz in (0, 1, 3, 2):
        for dy in range(2):
            if (dy, dz) != (0, 0):
                gathering.wait_chunk(dy, dz)
                row_grads(dy, dz)
    for dy in range(2):
        expert, _ = chunk_of(dy, 0)

        @pl.loop(0, 3)
        def _(piece):
            cols = pl.ds(pl.multiple_of(piece * 512, 512), 512)
            total = dot_tn(chunk_rows(x_ref, dy, 0), full[dy, 0, :, cols])
            for dz in range(1, 4):
                total += dot_tn(chunk_rows(x_ref, dy, dz), full[dy, dz, :, cols])
            w_in_grad_ref[expert, :, cols] = total.astype(bf)

    wait_returns(rg_send, rg_ref, r_send_sem, r_recv_sem)
    summing.drain()
    gathering.drain()


def experts_call(x_rows, act_grad, w_in):
    bf = jnp.bfloat16
    vmem = pl.BlockSpec(memory_space=pltpu.VMEM)
    shape = jax.ShapeDtypeStruct
    return pl.pallas_call(
        experts_kernel,
        out_shape=(
            shape((192, 1536), bf),
            shape((16, 2, 48, 512), bf),
            shape((2, 512, 1536), bf),
        ),
        in_specs=[vmem] * 3,
        out_specs=(vmem,) * 3,
        scratch_shapes=[
            pltpu.VMEM((2, 4, 192, 1536), bf),
            pltpu.VMEM((14, 192, 1536), bf),
            pltpu.VMEM((2, 4, 192, 1536), bf),
            pltpu.VMEM((2, 16, 48, 512), bf),
            pltpu.SemaphoreType.DMA((14,)),
            pltpu.SemaphoreType.DMA((14,)),
            pltpu.SemaphoreType.DMA((14,)),
            pltpu.SemaphoreType.DMA((14,)),
            pltpu.SemaphoreType.DMA((2, 16)),
            pltpu.SemaphoreType.DMA((2, 16)),
        ],
        compiler_params=pltpu.CompilerParams(
            collective_id=2, has_side_effects=True, vmem_limit_bytes=56 * 2**20
        ),
        name="experts",
    )(x_rows, act_grad, w_in)


def forward_kernel(
    q_ref, k_ref, v_ref, res_ref, qend_ref, gated_ref, rows_ref, w_out_ref,
    attn_ref, lse_ref, mixed_ref, inv_ref, xrecv_ref, grecv_ref, act_grad_ref, kv_out_ref,
    kv, m_s, l_s, acc_s, gsend, xsend, part, sums, sq_send, sq_recv,
    kv_send_sem, kv_recv_sem, out_sem, g_send_sem, g_recv_sem, x_send_sem, x_recv_sem,
    p_send_sem, p_recv_sem, sq_send_sem, sq_recv_sem,
):
    me = lax.axis_index("ctx")
    grp = lax.axis_index("grp")
    core = lax.rem(me, 2)
    chip = me // 2
    x = lax.rem(chip, 4)
    yh = chip // 4

    def device(dy, dx, dc):
        there = lax.rem(yh + dy, 2) * 4 + lax.rem(x + dx, 4)
        return {"ctx": there * 2 + lax.rem(core + dc, 2)}

    greet()

    copies = {}
    sent = []

    def move(src, slot, where):
        copy = remote(src, kv.at[slot], kv_send_sem.at[len(sent)], kv_recv_sem.at[slot], where)
        copy.start()
        copies[slot] = copy
        sent.append(copy)

    def own(which):
        return k_ref if which == 0 else v_ref

    right, left = device(0, 1, 0), device(0, 3, 0)
    sibling, partner = device(0, 0, 1), device(1, 0, 0)
    for which in range(2):
        move(own(which), (1, 0, 0, which), partner)
    for which in range(2):
        move(own(which), (0, 0, 1, which), sibling)
    kv[0, 0, 0, 0] = k_ref[...]
    kv[0, 0, 0, 1] = v_ref[...]

    @pl.loop(0, 16)
    def _(k):
        there = lax.rem(me + k, 16)
        gsend[k] = dot_nn(pick_two(rows_ref, there), gated_ref[...]).astype(jnp.bfloat16)

        @pl.when(k > 0)
        def _():
            remote(
                gsend.at[k], grecv_ref.at[me], g_send_sem.at[k], g_recv_sem.at[k], {"ctx": there}
            ).start()

    for which in range(2):
        move(own(which), (0, 3, 0, which), right)
        move(own(which), (0, 1, 0, which), left)
    grecv_ref[me] = gsend[0]
    summing = GrpSum(48, part, sums, p_send_sem, p_recv_sem)
    m_s[...] = jnp.full_like(m_s, LOW)
    l_s[...] = jnp.zeros_like(l_s)
    acc_s[...] = jnp.zeros_like(acc_s)
    outs = []

    def wait_slot(dy, dx, dc, which):
        copies[(dy, dx, dc, which)].wait_recv()

    def forward(dy, dx, which):
        wait_slot(dy, dx, 0, which)
        move(kv.at[dy, dx, 0, which], (dy, dx, 1, which), sibling)

    def relay(dy):
        forward(dy, 3, 0)
        move(kv.at[dy, 3, 0, 0], (dy, 2, 0, 0), right)
        forward(dy, 1, 1)
        move(kv.at[dy, 1, 0, 1], (dy, 2, 0, 1), left)
        forward(dy, 3, 1)
        forward(dy, 1, 0)

    def attend(dy, dx):
        for which in range(2):
            wait_slot(dy, dx, 1, which)
        copy = pltpu.make_async_copy(kv.at[dy, dx], kv_out_ref.at[dy, dx], out_sem.at[dy, dx])
        copy.start()
        outs.append(copy)
        there = lax.rem(yh + dy, 2) * 4 + lax.rem(x + dx, 4)
        lane = lax.broadcasted_iota(jnp.int32, (256, 256), 1)
        qend = qend_ref[:, 0:1]
        limits = [qend - (there * 512 + lax.rem(core + dc, 2) * 256) for dc in range(2)]

        @pl.loop(0, 4)
        def _(h):
            cols = pl.ds(pl.multiple_of(h * 128, 128), 128)
            qh = q_ref[:, cols]
            scores = []
            for dc in range(2):
                s = dot_nt(qh, kv[dy, dx, dc, 0, :, cols]) * (LOG2E * HEAD_DIM**-0.5)
                scores.append(jnp.where(lane < limits[dc], s, LOW))
            top = jnp.max(jnp.maximum(scores[0], scores[1]), axis=1, keepdims=True)
            m_old = m_s[h]
            m_new = jnp.maximum(m_old, top)
            alpha = jnp.exp2(m_old - m_new)
            probs = [jnp.exp2(s - m_new[:, 0:1]) for s in scores]
            total = jnp.sum(probs[0] + probs[1], axis=1, keepdims=True)
            m_s[h] = m_new
            l_s[h] = l_s[h] * alpha + total
            acc = acc_s[h] * alpha
            for dc in range(2):
                acc += dot_nn(probs[dc].astype(jnp.bfloat16), kv[dy, dx, dc, 1, :, cols])
            acc_s[h] = acc

    attend(0, 0)
    for which in range(2):
        wait_slot(1, 0, 0, which)
        move(kv.at[1, 0, 0, which], (1, 3, 0, which), right)
        move(kv.at[1, 0, 0, which], (1, 1, 0, which), left)
        move(kv.at[1, 0, 0, which], (1, 0, 1, which), sibling)

    @pl.loop(1, 16)
    def _(k):
        source = lax.rem(me + 16 - k, 16)
        remote(
            gsend.at[k], grecv_ref.at[source], g_send_sem.at[k], g_recv_sem.at[k], {"ctx": source}
        ).wait_recv()

    for dy, dz in CHUNK_ORDER:
        expert, _ = chunk_of(dy, dz)
        rows = chunk_rows(grecv_ref, dy, dz)

        @pl.loop(0, 3)
        def _(piece):
            cols = pl.ds(pl.multiple_of(piece * 512, 512), 512)
            part[dy, dz, :, cols] = dot_nt(rows, w_out_ref[expert, cols, :]).astype(jnp.bfloat16)

        summing.send_first(dy, dz)

    relay(0)
    attend(0, 3)
    attend(0, 1)
    relay(1)
    attend(1, 0)
    for which in range(2):
        forward(0, 2, which)
    attend(0, 2)
    attend(1, 3)
    attend(1, 1)
    for which in range(2):
        forward(1, 2, which)
    attend(1, 2)

    squares = jnp.zeros((256, 1), jnp.float32)
    for h in range(4):
        cols = slice(h * 128, h * 128 + 128)
        out = (acc_s[h] / l_s[h]).astype(jnp.bfloat16)
        lse_ref[h] = jnp.transpose(m_s[h] + jnp.log2(l_s[h]))[0:8]
        attn_ref[:, cols] = out
        mixed = (res_ref[:, cols].astype(jnp.float32) + out.astype(jnp.float32)).astype(
            jnp.bfloat16
        )
        mixed_ref[:, cols] = mixed
        mixed_f = mixed.astype(jnp.float32)
        squares += jnp.sum(mixed_f * mixed_f, axis=1, keepdims=True)
    turned = jnp.transpose(jnp.broadcast_to(squares, (256, 128)))
    sq_send[...] = turned[0:8]
    sq_recv[grp] = turned[0:8]

    @pl.loop(1, 8)
    def _(k):
        there = lax.rem(grp + k, 8)
        remote(
            sq_send, sq_recv.at[grp], sq_send_sem.at[k], sq_recv_sem.at[k], {"grp": there}
        ).start()

    @pl.loop(1, 8)
    def _(k):
        source = lax.rem(grp + 8 - k, 8)
        copy = remote(
            sq_send, sq_recv.at[source], sq_send_sem.at[k], sq_recv_sem.at[k], {"grp": source}
        )
        copy.wait_recv()
        copy.wait_send()

    total = sq_recv[0]
    for k in range(1, 8):
        total = total + sq_recv[k]
    inv = lax.rsqrt(total / 4096 + 1e-06)
    inv = jnp.transpose(jnp.concatenate([inv] * 16, axis=0))
    inv_ref[...] = inv
    normed = jnp.concatenate(
        [
            (mixed_ref[:, h * 128 : h * 128 + 128].astype(jnp.float32) * inv).astype(jnp.bfloat16)
            for h in range(4)
        ],
        axis=1,
    )

    @pl.loop(0, 16)
    def _(k):
        there = lax.rem(me + k, 16)
        xsend[k] = dot_nn(pick_both(rows_ref, there), normed).astype(jnp.bfloat16)

        @pl.when(k > 0)
        def _():
            remote(
                xsend.at[k], xrecv_ref.at[me], x_send_sem.at[k], x_recv_sem.at[k], {"ctx": there}
            ).start()

    xrecv_ref[me] = xsend[0]

    for dz in (1, 3, 2):
        summing.second(dz)
    summing.second_rest()

    def keep(rows, total):
        act_grad_ref[rows, :] = total

    summing.finish(keep)
    summing.drain()

    @pl.loop(1, 16)
    def _(k):
        source = lax.rem(me + 16 - k, 16)
        copy = remote(
            gsend.at[k], grecv_ref.at[source], g_send_sem.at[k], g_recv_sem.at[k], {"ctx": source}
        )
        copy.wait_send()
        copy = remote(
            xsend.at[k], xrecv_ref.at[source], x_send_sem.at[k], x_recv_sem.at[k], {"ctx": source}
        )
        copy.wait_recv()
        copy.wait_send()

    for copy in sent:
        copy.wait_send()
    for copy in outs:
        copy.wait()


def forward_call(q, k, v, res, qend, gated, rows, w_out):
    bf, f32 = jnp.bfloat16, jnp.float32
    vmem = pl.BlockSpec(memory_space=pltpu.VMEM)
    shape = jax.ShapeDtypeStruct
    return pl.pallas_call(
        forward_kernel,
        out_shape=(
            shape((256, 512), bf),
            shape((4, 8, 256), f32),
            shape((256, 512), bf),
            shape((256, 128), f32),
            shape((16, 96, 512), bf),
            shape((16, 96, 512), bf),
            shape((192, 1536), f32),
            shape((2, 4, 2, 2, 256, 512), bf),
        ),
        in_specs=[vmem] * 8,
        out_specs=[vmem] * 7 + [pl.BlockSpec(memory_space=pl.ANY)],
        scratch_shapes=[
            pltpu.VMEM((2, 4, 2, 2, 256, 512), bf),
            pltpu.VMEM((4, 256, 128), f32),
            pltpu.VMEM((4, 256, 128), f32),
            pltpu.VMEM((4, 256, 128), f32),
            pltpu.VMEM((16, 96, 512), bf),
            pltpu.VMEM((16, 96, 512), bf),
            pltpu.VMEM((2, 4, 192, 1536), bf),
            pltpu.VMEM((14, 192, 1536), bf),
            pltpu.VMEM((8, 256), f32),
            pltpu.VMEM((8, 8, 256), f32),
            pltpu.SemaphoreType.DMA((30,)),
            pltpu.SemaphoreType.DMA((2, 4, 2, 2)),
            pltpu.SemaphoreType.DMA((2, 4)),
            pltpu.SemaphoreType.DMA((16,)),
            pltpu.SemaphoreType.DMA((16,)),
            pltpu.SemaphoreType.DMA((16,)),
            pltpu.SemaphoreType.DMA((16,)),
            pltpu.SemaphoreType.DMA((14,)),
            pltpu.SemaphoreType.DMA((14,)),
            pltpu.SemaphoreType.DMA((8,)),
            pltpu.SemaphoreType.DMA((8,)),
        ],
        compiler_params=pltpu.CompilerParams(
            collective_id=0, has_side_effects=True, vmem_limit_bytes=56 * 2**20
        ),
        name="forward",
    )(q, k, v, res, qend, gated, rows, w_out)


def backward_kernel(
    q_ref, kv_ref, lse_ref, attn_ref, qend_ref, og_ref, inv_ref, rows_ref, rg_ref, act_ref,
    w_out_ref, g_ref, mixed_ref, gates_ref,
    layer_ref, ig_ref, dq_ref, dk_ref, dv_ref, w_out_grad_ref,
    full, eo_send, eo_recv, normed_grad, returned, row_dot, dqt, own_terms, sib_send, sib_recv, ring_send,
    ring_recv, part_send, part_recv,
    f_send_sem, f_recv_sem, r_send_sem, r_recv_sem, sib_send_sem, sib_recv_sem, ring_send_sem, ring_recv_sem,
    part_send_sem, part_recv_sem,
):
    me = lax.axis_index("ctx")
    core = lax.rem(me, 2)
    chip = me // 2
    x = lax.rem(chip, 4)
    yh = chip // 4
    bf, f32 = jnp.bfloat16, jnp.float32

    def device(dy, dx, dc):
        there = lax.rem(yh + dy, 2) * 4 + lax.rem(x + dx, 4)
        return {"ctx": there * 2 + lax.rem(core + dc, 2)}

    right, left = device(0, 1, 0), device(0, 3, 0)
    sibling, partner = device(0, 0, 1), device(1, 0, 0)
    greet()
    gathering = GrpGather(48, full, f_send_sem, f_recv_sem)
    full[0, 0] = act_ref[...]
    gathering.send_own()
    dqt[...] = jnp.zeros_like(dqt)
    normed_grad[...] = jnp.zeros_like(normed_grad)

    @pl.loop(0, 16)
    def _(k):
        normed_grad[...] += dot_tn(pick_both(rows_ref, k), rg_ref[k])

    for h in range(4):
        cols = slice(h * 128, h * 128 + 128)
        grad = og_ref[:, cols].astype(f32) + inv_ref[...] * normed_grad[:, cols]
        grad = grad.astype(bf)
        ig_ref[:, cols] = grad
        dots = jnp.sum(grad.astype(f32) * attn_ref[:, cols].astype(f32), axis=1, keepdims=True)
        row_dot[h] = jnp.transpose(jnp.broadcast_to(dots, (256, 128)))[0:8]

    scale = HEAD_DIM**-0.5

    def terms(dy, dx):
        there = lax.rem(yh + dy, 2) * 4 + lax.rem(x + dx, 4)
        sub = lax.broadcasted_iota(jnp.int32, (256, 256), 0)
        qend = qend_ref[0:1, :]
        limits = [qend - (there * 512 + lax.rem(core + dc, 2) * 256) for dc in range(2)]

        @pl.loop(0, 4)
        def _(h):
            cols = pl.ds(pl.multiple_of(h * 128, 128), 128)
            qh = q_ref[:, cols]
            gh = ig_ref[:, cols]
            lse = lse_ref[h][0:1, :]
            dots = row_dot[h][0:1, :]
            for dc in range(2):
                kh = kv_ref[dy, dx, dc, 0, :, cols]
                vh = kv_ref[dy, dx, dc, 1, :, cols]
                s = dot_nt(kh, qh) * (LOG2E * scale)
                p = jnp.exp2(jnp.where(sub < limits[dc], s, LOW) - lse)
                dp = dot_nt(vh, gh)
                ds = (p * (dp - dots) * scale).astype(bf)
                dk = dot_nn(ds, qh).astype(bf)
                dv = dot_nn(p.astype(bf), gh).astype(bf)
                dqt[h] += dot_tn(kh, ds)
                to = own_terms if dc == 0 else sib_send
                to[dy, dx, 0, :, cols] = dk
                to[dy, dx, 1, :, cols] = dv

        for which in range(2):
            sib_copy(dy, dx, which).start()

    def sib_copy(dy, dx, which):
        return remote(
            sib_send.at[dy, dx, which],
            sib_recv.at[dy, dx, which],
            sib_send_sem.at[dy, dx, which],
            sib_recv_sem.at[dy, dx, which],
            sibling,
        )

    def ring_copy(dy, dx, which):
        to = (dx + 3) % 4 if which == 0 else (dx + 1) % 4
        return remote(
            ring_send.at[dy, dx, which],
            ring_recv.at[dy, to, which],
            ring_send_sem.at[dy, dx, which],
            ring_recv_sem.at[dy, to, which],
            right if which == 0 else left,
        )

    def arrival(dy, dx, which):
        return ring_copy(dy, (dx + 1) % 4 if which == 0 else (dx + 3) % 4, which)

    def total_of(dy, dx, which, ring):
        sib_copy(dy, dx, which).wait_recv()
        if ring:
            arrival(dy, dx, which).wait_recv()
        sums = own_terms[dy, dx, which].astype(f32) + sib_recv[dy, dx, which].astype(f32)
        if ring:
            sums = sums + ring_recv[dy, dx, which].astype(f32)
        return sums

    def send_ring(dy, dx, which, ring):
        ring_send[dy, dx, which] = total_of(dy, dx, which, ring).astype(bf)
        ring_copy(dy, dx, which).start()

    def part_copy(which):
        return remote(
            part_send.at[which],
            part_recv.at[which],
            part_send_sem.at[which],
            part_recv_sem.at[which],
            partner,
        )

    def expert_rows(dy, dz):
        expert, _ = chunk_of(dy, dz)
        rows = dot_nn(full[dy, dz], w_out_ref[expert]).astype(bf)
        return_rows(rows, dy, dz, eo_send, eo_recv, r_send_sem, r_recv_sem)

    terms(1, 3)
    terms(1, 1)
    send_ring(1, 3, 0, False)
    send_ring(1, 1, 1, False)
    terms(1, 2)
    terms(1, 0)
    gathering.pass_rest()
    for dz in (1, 3, 2):
        gathering.pass_head(dz)
    send_ring(1, 2, 0, True)
    send_ring(1, 2, 1, True)
    expert_rows(0, 0)
    terms(0, 3)
    terms(0, 1)
    send_ring(1, 1, 0, True)
    send_ring(1, 3, 1, True)
    send_ring(0, 3, 0, False)
    send_ring(0, 1, 1, False)
    terms(0, 2)
    for which in range(2):
        part_send[which] = total_of(1, 0, which, True).astype(bf)
        part_copy(which).start()
    send_ring(0, 2, 0, True)
    send_ring(0, 2, 1, True)
    terms(0, 0)
    gathering.wait_chunk(1, 0)
    expert_rows(1, 0)
    for h in range(4):
        dq_ref[:, h * 128 : h * 128 + 128] = jnp.transpose(dqt[h]).astype(bf)
    send_ring(0, 1, 0, True)
    send_ring(0, 3, 1, True)
    for dz in (1, 3, 2):
        for dy in range(2):
            gathering.wait_chunk(dy, dz)
            expert_rows(dy, dz)
    for which in range(2):
        sums = total_of(0, 0, which, True)
        part_copy(which).wait_recv()
        sums = sums + part_recv[which].astype(f32)
        if which == 0:
            dk_ref[...] = sums.astype(bf)
        else:
            dv_ref[...] = sums.astype(bf)

    for dy in range(2):
        for dx in range(4):
            for which in range(2):
                sib_copy(dy, dx, which).wait_send()
                if dx > 0:
                    ring_copy(dy, dx, which).wait_send()
    for which in range(2):
        part_copy(which).wait_send()

    for dy in range(2):
        expert, _ = chunk_of(dy, 0)

        @pl.loop(0, 3)
        def _(piece):
            cols = pl.ds(pl.multiple_of(piece * 512, 512), 512)
            total = dot_tn(full[dy, 0, :, cols], chunk_rows(g_ref, dy, 0))
            for dz in range(1, 4):
                total += dot_tn(full[dy, dz, :, cols], chunk_rows(g_ref, dy, dz))
            w_out_grad_ref[expert, cols, :] = total.astype(bf)

    wait_returns(eo_send, eo_recv, r_send_sem, r_recv_sem)
    returned[...] = jnp.zeros_like(returned)

    @pl.loop(0, 16)
    def _(k):
        returned[...] += dot_tn(pick_two(rows_ref, k), eo_recv[k].reshape(96, 512))

    for h in range(4):
        cols = slice(h * 128, h * 128 + 128)
        sums = gates_ref[0] * returned[0:256, cols] + gates_ref[1] * returned[256:512, cols]
        layer_ref[:, cols] = (mixed_ref[:, cols].astype(f32) + sums).astype(bf)

    gathering.drain()


def backward_call(*operands):
    bf, f32 = jnp.bfloat16, jnp.float32
    vmem = pl.BlockSpec(memory_space=pltpu.VMEM)
    shape = jax.ShapeDtypeStruct
    return pl.pallas_call(
        backward_kernel,
        out_shape=(shape((256, 512), bf),) * 5 + (shape((2, 1536, 512), bf),),
        in_specs=[vmem] * 14,
        out_specs=(vmem,) * 6,
        scratch_shapes=[
            pltpu.VMEM((2, 4, 192, 1536), bf),
            pltpu.VMEM((2, 16, 48, 512), bf),
            pltpu.VMEM((16, 2, 48, 512), bf),
            pltpu.VMEM((256, 512), f32),
            pltpu.VMEM((512, 512), f32),
            pltpu.VMEM((4, 8, 256), f32),
            pltpu.VMEM((4, 128, 256), f32),
            pltpu.VMEM((2, 4, 2, 256, 512), bf),
            pltpu.VMEM((2, 4, 2, 256, 512), bf),
            pltpu.VMEM((2, 4, 2, 256, 512), bf),
            pltpu.VMEM((2, 4, 2, 256, 512), bf),
            pltpu.VMEM((2, 4, 2, 256, 512), bf),
            pltpu.VMEM((2, 256, 512), bf),
            pltpu.VMEM((2, 256, 512), bf),
            pltpu.SemaphoreType.DMA((14,)),
            pltpu.SemaphoreType.DMA((14,)),
            pltpu.SemaphoreType.DMA((2, 16)),
            pltpu.SemaphoreType.DMA((2, 16)),
            pltpu.SemaphoreType.DMA((2, 4, 2)),
            pltpu.SemaphoreType.DMA((2, 4, 2)),
            pltpu.SemaphoreType.DMA((2, 4, 2)),
            pltpu.SemaphoreType.DMA((2, 4, 2)),
            pltpu.SemaphoreType.DMA((2,)),
            pltpu.SemaphoreType.DMA((2,)),
        ],
        compiler_params=pltpu.CompilerParams(
            collective_id=1, has_side_effects=True, vmem_limit_bytes=56 * 2**20
        ),
        name="backward",
    )(*operands)


def shards(
    residual, queries, keys, values, frame_lengths, routes, route_gates, w_in, w_out, out_grad
):
    n_ctx = lax.axis_size("ctx")
    tok_rows, feat_dev = residual.shape
    exp_dev = w_in.shape[0]
    seq_len = tok_rows * n_ctx
    experts_all = exp_dev * n_ctx
    capacity = 6 * tok_rows // experts_all
    expert_flat = routes.reshape(-1)
    onehot = (expert_flat[:, None] == jnp.arange(experts_all, dtype=jnp.int32)[None, :]).astype(
        jnp.int32
    )
    earlier = jnp.cumsum(onehot, axis=0) - onehot
    ranks = jnp.sum(earlier * onehot, axis=1)
    row_index = (expert_flat * capacity + ranks).reshape(tok_rows, 2).T.reshape(1, 2 * tok_rows)
    rows_wide = jnp.broadcast_to(row_index, (8, 2 * tok_rows))
    out_grad_f = out_grad.astype(jnp.float32)
    gated = jnp.concatenate(
        [(route_gates[:, a : a + 1] * out_grad_f).astype(jnp.bfloat16) for a in range(2)], axis=0
    )
    gates_wide = jnp.broadcast_to(route_gates.T[:, :, None], (2, tok_rows, 128))
    ctx_index = lax.axis_index("ctx")
    frame_ends = jnp.cumsum(frame_lengths)
    positions = ctx_index * tok_rows + jnp.arange(tok_rows, dtype=jnp.int32)
    ends = jnp.min(
        jnp.where(frame_ends[None, :] > positions[:, None], frame_ends[None, :], seq_len), axis=1
    ).astype(jnp.int32)
    attn, lse, mixed, inv_wide, rows_recv, grads_recv, act_grad, kv_all = forward_call(
        queries,
        keys,
        values,
        residual,
        jnp.broadcast_to(ends[:, None], (tok_rows, 128)),
        gated,
        rows_wide,
        w_out,
    )
    activated, row_grad, w_in_grad = experts_call(rows_recv, act_grad, w_in)
    layer_out, input_grad, query_grad, key_grad, value_grad, w_out_grad = backward_call(
        queries,
        kv_all,
        lse,
        attn,
        jnp.broadcast_to(ends[None, :], (8, tok_rows)),
        out_grad,
        inv_wide,
        rows_wide,
        row_grad.reshape(n_ctx, exp_dev * capacity, feat_dev),
        activated,
        w_out,
        grads_recv,
        mixed,
        gates_wide,
    )
    return (
        layer_out,
        input_grad,
        query_grad,
        key_grad,
        value_grad,
        w_in_grad,
        w_out_grad,
    )


def solution(mesh):
    in_specs = (
        P("ctx", "grp"),
        P("ctx", "grp"),
        P("ctx", "grp"),
        P("ctx", "grp"),
        P(),
        P("ctx", None),
        P("ctx", None),
        P("ctx", "grp", None),
        P("ctx", None, "grp"),
        P("ctx", "grp"),
    )
    out_specs = (
        P("ctx", "grp"),
        P("ctx", "grp"),
        P("ctx", "grp"),
        P("ctx", "grp"),
        P("ctx", "grp"),
        P("ctx", "grp", None),
        P("ctx", None, "grp"),
    )
    return jax.shard_map(shards, mesh=mesh, in_specs=in_specs, out_specs=out_specs, check_vma=False)
```

```python
import jax
import jax.numpy as jnp
from jax import lax
from jax.experimental import pallas as pl
from jax.experimental.pallas import tpu as pltpu
from jax.sharding import PartitionSpec as P

HEAD_DIM = 128


gelu_coef = 0.7978845608028654


def gelu_tanh(field):
    return 0.5 * field * (1.0 + jnp.tanh(gelu_coef * (field + 0.044715 * field * field * field)))


def gelu_slope(field):
    tanh_val = jnp.tanh(gelu_coef * (field + 0.044715 * field * field * field))
    return 0.5 * (1.0 + tanh_val) + 0.5 * field * (1.0 - tanh_val * tanh_val) * gelu_coef * (
        1.0 + 3.0 * 0.044715 * field * field
    )


MESH_ID = pl.DeviceIdType.MESH
LOG2E = 1.4426950408889634
LOW = -1e30


def dot_nt(a, b):
    return lax.dot_general(a, b, (((1,), (1,)), ((), ())), preferred_element_type=jnp.float32)


def dot_tn(a, b):
    return lax.dot_general(a, b, (((0,), (0,)), ((), ())), preferred_element_type=jnp.float32)


def dot_nn(a, b):
    return jnp.dot(a, b, preferred_element_type=jnp.float32)


def greet():
    me = lax.axis_index("ctx")
    grp = lax.axis_index("grp")
    barrier = pltpu.get_barrier_semaphore()

    @pl.loop(1, 16)
    def _(k):
        pl.semaphore_signal(
            barrier, inc=1, device_id={"ctx": lax.rem(me + k, 16)}, device_id_type=MESH_ID
        )

    @pl.loop(1, 8)
    def _(k):
        pl.semaphore_signal(
            barrier, inc=1, device_id={"grp": lax.rem(grp + k, 8)}, device_id_type=MESH_ID
        )

    pl.semaphore_wait(barrier, 22)


def remote(src, dst, send_sem, recv_sem, where):
    return pltpu.make_async_remote_copy(
        src_ref=src,
        dst_ref=dst,
        send_sem=send_sem,
        recv_sem=recv_sem,
        device_id=where,
        device_id_type=MESH_ID,
    )


def pick_two(rows_ref, there):
    rows = lax.broadcasted_iota(jnp.int32, (96, 512), 0) + there * 96
    return jnp.where(rows == rows_ref[0:1, :], 1.0, 0.0).astype(jnp.bfloat16)


def pick_both(rows_ref, there):
    rows = lax.broadcasted_iota(jnp.int32, (96, 256), 0) + there * 96
    hit = (rows == rows_ref[0:1, 0:256]) | (rows == rows_ref[0:1, 256:512])
    return jnp.where(hit, 1.0, 0.0).astype(jnp.bfloat16)


def grp_device(dy, dz):
    grp = lax.axis_index("grp")
    there = lax.rem(grp // 4 + dy, 2) * 4 + lax.rem(lax.rem(grp, 4) + dz, 4)
    return {"grp": there}


class GrpSum:
    def __init__(self, cut, part, recv, send_sem, recv_sem):
        self.cut, self.part, self.recv = cut, part, recv
        self.send_sem, self.recv_sem = send_sem, recv_sem
        self.head, self.rest = pl.ds(0, cut), pl.ds(cut, 192 - cut)

    def copy(self, number):
        part, head, rest = self.part, self.head, self.rest
        if number < 4:
            src, rows, where = part.at[1, number, head], head, grp_device(1, 0)
        elif number < 10:
            dz, dy = (number - 4) // 2 + 1, (number - 4) % 2
            src, rows, where = part.at[dy, dz, rest], rest, grp_device(0, dz)
        elif number < 13:
            dz = number - 9
            src, rows, where = part.at[0, dz, head], head, grp_device(0, dz)
        else:
            src, rows, where = part.at[1, 0, rest], rest, grp_device(1, 0)
        return remote(
            src,
            self.recv.at[number, rows],
            self.send_sem.at[number],
            self.recv_sem.at[number],
            where,
        )

    def send_first(self, dy, dz):
        if dy == 1:
            self.copy(dz).start()
        if dz > 0:
            self.copy(4 + (dz - 1) * 2 + dy).start()

    def add(self, target, start, size, slots, out):
        @pl.loop(0, size // 16)
        def _(step):
            rows = pl.ds(pl.multiple_of(start + step * 16, 16), 16)
            total = self.part[target[0], target[1], rows, :].astype(jnp.float32)
            for slot in slots:
                total += self.recv[slot, rows, :].astype(jnp.float32)
            out(rows, total)

    def second(self, dz):
        self.copy(dz).wait_recv()

        def out(rows, total):
            self.part[0, dz, rows, :] = total.astype(jnp.bfloat16)

        self.add((0, dz), 0, self.cut, [dz], out)
        self.copy(9 + dz).start()

    def second_rest(self):
        for number in (5, 7, 9):
            self.copy(number).wait_recv()

        def out(rows, total):
            self.part[1, 0, rows, :] = total.astype(jnp.bfloat16)

        self.add((1, 0), self.cut, 192 - self.cut, [5, 7, 9], out)
        self.copy(13).start()

    def finish(self, out):
        for number in (0, 4, 6, 8, 10, 11, 12, 13):
            self.copy(number).wait_recv()
        self.add((0, 0), 0, self.cut, [0, 10, 11, 12], out)
        self.add((0, 0), self.cut, 192 - self.cut, [4, 6, 8, 13], out)

    def drain(self):
        for number in range(14):
            self.copy(number).wait_send()


class GrpGather:
    def __init__(self, cut, full, send_sem, recv_sem):
        self.full, self.send_sem, self.recv_sem = full, send_sem, recv_sem
        self.head, self.rest = pl.ds(0, cut), pl.ds(cut, 192 - cut)

    def copy(self, number):
        head, rest = self.head, self.rest
        if number < 3:
            dz = number + 1
            src, dst, rows, where = (0, 0), (0, 4 - dz), head, grp_device(0, dz)
        elif number == 3:
            src, dst, rows, where = (0, 0), (1, 0), rest, grp_device(1, 0)
        elif number < 8:
            dz = number - 4
            src, dst, rows, where = (0, dz), (1, dz), head, grp_device(1, 0)
        else:
            dz, dy = (number - 8) // 2 + 1, (number - 8) % 2
            src, dst, rows, where = (dy, 0), (dy, 4 - dz), rest, grp_device(0, dz)
        return remote(
            self.full.at[src[0], src[1], rows],
            self.full.at[dst[0], dst[1], rows],
            self.send_sem.at[number],
            self.recv_sem.at[number],
            where,
        )

    def send_own(self):
        self.copy(3).start()
        for number in (0, 2, 1):
            self.copy(number).start()
        self.copy(4).start()
        for dz in (1, 3, 2):
            self.copy(8 + (dz - 1) * 2).start()

    def pass_rest(self):
        self.copy(3).wait_recv()
        for dz in (1, 3, 2):
            self.copy(8 + (dz - 1) * 2 + 1).start()

    def pass_head(self, dz):
        self.copy(3 - dz).wait_recv()
        self.copy(4 + dz).start()

    def wait_chunk(self, dy, dz):
        if dy == 1:
            self.copy(4 + dz).wait_recv()
        if dz > 0:
            self.copy(8 + (3 - dz) * 2 + dy).wait_recv()

    def drain(self):
        for number in range(14):
            self.copy(number).wait_send()


def chunk_of(dy, dz):
    grp = lax.axis_index("grp")
    return lax.rem(grp // 4 + dy, 2), lax.rem(lax.rem(grp, 4) + dz, 4) * 4


def chunk_rows(ref, dy, dz):
    expert, first = chunk_of(dy, dz)
    rows = ref[pl.ds(first, 4), pl.ds(pl.multiple_of(expert * 48, 16), 48), :]
    return rows.reshape(192, 512)


CHUNK_ORDER = [(1, 1), (1, 3), (1, 2), (1, 0), (0, 1), (0, 3), (0, 2), (0, 0)]


def return_rows(rows, dy, dz, send, recv, send_sem, recv_sem):
    me = lax.axis_index("ctx")
    expert, first = chunk_of(dy, dz)
    send[expert, pl.ds(first, 4)] = rows.reshape(4, 48, 512)

    @pl.loop(0, 4)
    def _(i):
        there = first + i

        @pl.when(there != me)
        def _():
            return_copy(expert, there, me, there, send, recv, send_sem, recv_sem).start()


def return_copy(expert, there, mine, partner, send, recv, send_sem, recv_sem):
    return remote(
        send.at[expert, there],
        recv.at[mine, expert],
        send_sem.at[expert, there],
        recv_sem.at[expert, mine],
        {"ctx": partner},
    )


def wait_returns(send, recv, send_sem, recv_sem):
    me = lax.axis_index("ctx")
    for expert in range(2):
        recv[me, expert] = send[expert, me]

        @pl.loop(1, 16)
        def _(k):
            source = lax.rem(me + k, 16)
            copy = return_copy(
                expert, source, source, source, send, recv, send_sem, recv_sem
            )
            copy.wait_recv()
            copy.wait_send()


def experts_kernel(
    x_ref, act_grad_ref, w_in_hbm,
    act_ref, rg_ref, w_in_grad_ref,
    part, sums, full, rg_send, w_in_ref, w_sem,
    s_send_sem, s_recv_sem, f_send_sem, f_recv_sem, r_send_sem, r_recv_sem,
):
    bf = jnp.bfloat16
    w_copy = pltpu.make_async_copy(w_in_hbm, w_in_ref, w_sem)
    w_copy.start()
    greet()
    w_copy.wait()
    summing = GrpSum(112, part, sums, s_send_sem, s_recv_sem)
    gathering = GrpGather(112, full, f_send_sem, f_recv_sem)
    for dy, dz in CHUNK_ORDER:
        expert, _ = chunk_of(dy, dz)
        rows = chunk_rows(x_ref, dy, dz)

        @pl.loop(0, 3)
        def _(piece):
            cols = pl.ds(pl.multiple_of(piece * 512, 512), 512)
            part[dy, dz, :, cols] = dot_nn(rows, w_in_ref[expert, :, cols]).astype(bf)

        summing.send_first(dy, dz)
    for dz in (1, 3, 2):
        summing.second(dz)
    summing.second_rest()

    def activate(rows, pre):
        act_ref[rows, :] = gelu_tanh(pre).astype(bf)
        full[0, 0, rows, :] = (act_grad_ref[rows, :] * gelu_slope(pre)).astype(bf)

    summing.finish(activate)
    gathering.send_own()

    def row_grads(dy, dz):
        expert, _ = chunk_of(dy, dz)
        rows = dot_nt(full[dy, dz], w_in_ref[expert]).astype(bf)
        return_rows(rows, dy, dz, rg_send, rg_ref, r_send_sem, r_recv_sem)

    row_grads(0, 0)
    gathering.pass_rest()
    for dz in (1, 3, 2):
        gathering.pass_head(dz)
    for dz in (0, 1, 3, 2):
        for dy in range(2):
            if (dy, dz) != (0, 0):
                gathering.wait_chunk(dy, dz)
                row_grads(dy, dz)
    for dy in range(2):
        expert, _ = chunk_of(dy, 0)

        @pl.loop(0, 3)
        def _(piece):
            cols = pl.ds(pl.multiple_of(piece * 512, 512), 512)
            total = dot_tn(chunk_rows(x_ref, dy, 0), full[dy, 0, :, cols])
            for dz in range(1, 4):
                total += dot_tn(chunk_rows(x_ref, dy, dz), full[dy, dz, :, cols])
            w_in_grad_ref[expert, :, cols] = total.astype(bf)

    wait_returns(rg_send, rg_ref, r_send_sem, r_recv_sem)
    summing.drain()
    gathering.drain()


def experts_call(x_rows, act_grad, w_in):
    bf = jnp.bfloat16
    vmem = pl.BlockSpec(memory_space=pltpu.VMEM)
    shape = jax.ShapeDtypeStruct
    return pl.pallas_call(
        experts_kernel,
        out_shape=(
            shape((192, 1536), bf),
            shape((16, 2, 48, 512), bf),
            shape((2, 512, 1536), bf),
        ),
        in_specs=[vmem] * 2 + [pl.BlockSpec(memory_space=pl.ANY)],
        out_specs=(vmem,) * 3,
        scratch_shapes=[
            pltpu.VMEM((2, 4, 192, 1536), bf),
            pltpu.VMEM((14, 192, 1536), bf),
            pltpu.VMEM((2, 4, 192, 1536), bf),
            pltpu.VMEM((2, 16, 48, 512), bf),
            pltpu.VMEM((2, 512, 1536), bf),
            pltpu.SemaphoreType.DMA,
            pltpu.SemaphoreType.DMA((14,)),
            pltpu.SemaphoreType.DMA((14,)),
            pltpu.SemaphoreType.DMA((14,)),
            pltpu.SemaphoreType.DMA((14,)),
            pltpu.SemaphoreType.DMA((2, 16)),
            pltpu.SemaphoreType.DMA((2, 16)),
        ],
        compiler_params=pltpu.CompilerParams(
            collective_id=2, has_side_effects=True, vmem_limit_bytes=56 * 2**20
        ),
        name="experts",
    )(x_rows, act_grad, w_in)


def forward_kernel(
    q_ref, k_ref, v_ref, res_ref, lengths_ref, routes_ref, gates_ref, og_ref, w_out_hbm,
    rows_ref, qend_row_ref, attn_ref, lse_ref, mixed_ref, inv_ref, xrecv_ref, grecv_ref, act_grad_ref, kv_out_ref,
    kv, m_s, l_s, acc_s, gsend, xsend, part, sums, sq_send, sq_recv, gated, qend_s, w_out_ref,
    w_sem,
    kv_send_sem, kv_recv_sem, out_sem, g_send_sem, g_recv_sem, x_send_sem, x_recv_sem,
    p_send_sem, p_recv_sem, sq_send_sem, sq_recv_sem,
):
    me = lax.axis_index("ctx")
    grp = lax.axis_index("grp")
    core = lax.rem(me, 2)
    chip = me // 2
    x = lax.rem(chip, 4)
    yh = chip // 4

    def device(dy, dx, dc):
        there = lax.rem(yh + dy, 2) * 4 + lax.rem(x + dx, 4)
        return {"ctx": there * 2 + lax.rem(core + dc, 2)}

    w_copy = pltpu.make_async_copy(w_out_hbm, w_out_ref, w_sem)
    w_copy.start()
    greet()

    copies = {}
    sent = []

    def move(src, slot, where):
        copy = remote(src, kv.at[slot], kv_send_sem.at[len(sent)], kv_recv_sem.at[slot], where)
        copy.start()
        copies[slot] = copy
        sent.append(copy)

    def own(which):
        return k_ref if which == 0 else v_ref

    right, left = device(0, 1, 0), device(0, 3, 0)
    sibling, partner = device(0, 0, 1), device(1, 0, 0)
    for which in range(2):
        move(own(which), (1, 0, 0, which), partner)
    for which in range(2):
        move(own(which), (0, 0, 1, which), sibling)
    early = lax.broadcasted_iota(jnp.int32, (256, 256), 0) < lax.broadcasted_iota(
        jnp.int32, (256, 256), 1
    )
    experts = [routes_ref[:, a : a + 1].astype(jnp.float32) for a in range(2)]
    for a in range(2):
        expert_row = jnp.transpose(jnp.broadcast_to(experts[a], (256, 128)))[0:8]
        rank = jnp.zeros((1, 256), jnp.float32)
        for b in range(2):
            same = early & (experts[b] == expert_row[0:1])
            rank += jnp.sum(jnp.where(same, 1.0, 0.0), axis=0, keepdims=True)
        cols = slice(a * 256, a * 256 + 256)
        rows_ref[:, cols] = (expert_row * 48 + rank).astype(jnp.int32)
        gate = gates_ref[:, a : a + 1]
        gated[cols, :] = (gate * og_ref[...].astype(jnp.float32)).astype(jnp.bfloat16)

    @pl.loop(0, 16)
    def _(k):
        there = lax.rem(me + k, 16)
        gsend[k] = dot_nn(pick_two(rows_ref, there), gated[...]).astype(jnp.bfloat16)

        @pl.when(k > 0)
        def _():
            remote(
                gsend.at[k], grecv_ref.at[me], g_send_sem.at[k], g_recv_sem.at[k], {"ctx": there}
            ).start()

    for which in range(2):
        move(own(which), (0, 3, 0, which), right)
        move(own(which), (0, 1, 0, which), left)
    grecv_ref[me] = gsend[0]
    kv[0, 0, 0, 0] = k_ref[...]
    kv[0, 0, 0, 1] = v_ref[...]
    pos_col = me * 256 + lax.broadcasted_iota(jnp.int32, (256, 128), 0)
    pos_row = me * 256 + lax.broadcasted_iota(jnp.int32, (8, 256), 1)
    ends_col, ends_row = jnp.full_like(pos_col, 4096), jnp.full_like(pos_row, 4096)
    end = jnp.int32(0)
    for f in range(16):
        end = end + lengths_ref[f]
        ends_col = jnp.minimum(ends_col, jnp.where(end > pos_col, end, 4096))
        ends_row = jnp.minimum(ends_row, jnp.where(end > pos_row, end, 4096))
    qend_s[...] = ends_col
    qend_row_ref[...] = ends_row
    summing = GrpSum(48, part, sums, p_send_sem, p_recv_sem)
    m_s[...] = jnp.full_like(m_s, LOW)
    l_s[...] = jnp.zeros_like(l_s)
    acc_s[...] = jnp.zeros_like(acc_s)
    outs = []

    def wait_slot(dy, dx, dc, which):
        copies[(dy, dx, dc, which)].wait_recv()

    def forward(dy, dx, which):
        wait_slot(dy, dx, 0, which)
        move(kv.at[dy, dx, 0, which], (dy, dx, 1, which), sibling)

    def relay(dy):
        forward(dy, 3, 0)
        move(kv.at[dy, 3, 0, 0], (dy, 2, 0, 0), right)
        forward(dy, 1, 1)
        move(kv.at[dy, 1, 0, 1], (dy, 2, 0, 1), left)
        forward(dy, 3, 1)
        forward(dy, 1, 0)

    def attend(dy, dx):
        for which in range(2):
            wait_slot(dy, dx, 1, which)
        copy = pltpu.make_async_copy(kv.at[dy, dx], kv_out_ref.at[dy, dx], out_sem.at[dy, dx])
        copy.start()
        outs.append(copy)
        there = lax.rem(yh + dy, 2) * 4 + lax.rem(x + dx, 4)
        lane = lax.broadcasted_iota(jnp.int32, (256, 256), 1)
        qend = qend_s[:, 0:1]
        limits = [qend - (there * 512 + lax.rem(core + dc, 2) * 256) for dc in range(2)]

        @pl.loop(0, 4)
        def _(h):
            cols = pl.ds(pl.multiple_of(h * 128, 128), 128)
            qh = q_ref[:, cols]
            scores = []
            for dc in range(2):
                s = dot_nt(qh, kv[dy, dx, dc, 0, :, cols]) * (LOG2E * HEAD_DIM**-0.5)
                scores.append(jnp.where(lane < limits[dc], s, LOW))
            top = jnp.max(jnp.maximum(scores[0], scores[1]), axis=1, keepdims=True)
            m_old = m_s[h]
            m_new = jnp.maximum(m_old, top)
            alpha = jnp.exp2(m_old - m_new)
            probs = [jnp.exp2(s - m_new[:, 0:1]) for s in scores]
            total = jnp.sum(probs[0] + probs[1], axis=1, keepdims=True)
            m_s[h] = m_new
            l_s[h] = l_s[h] * alpha + total
            acc = acc_s[h] * alpha
            for dc in range(2):
                acc += dot_nn(probs[dc].astype(jnp.bfloat16), kv[dy, dx, dc, 1, :, cols])
            acc_s[h] = acc

    attend(0, 0)
    for which in range(2):
        wait_slot(1, 0, 0, which)
        move(kv.at[1, 0, 0, which], (1, 3, 0, which), right)
        move(kv.at[1, 0, 0, which], (1, 1, 0, which), left)
        move(kv.at[1, 0, 0, which], (1, 0, 1, which), sibling)

    relay(0)

    @pl.loop(1, 16)
    def _(k):
        source = lax.rem(me + 16 - k, 16)
        remote(
            gsend.at[k], grecv_ref.at[source], g_send_sem.at[k], g_recv_sem.at[k], {"ctx": source}
        ).wait_recv()

    w_copy.wait()
    for dy, dz in CHUNK_ORDER:
        expert, _ = chunk_of(dy, dz)
        rows = chunk_rows(grecv_ref, dy, dz)

        @pl.loop(0, 3)
        def _(piece):
            cols = pl.ds(pl.multiple_of(piece * 512, 512), 512)
            part[dy, dz, :, cols] = dot_nt(rows, w_out_ref[expert, cols, :]).astype(jnp.bfloat16)

        summing.send_first(dy, dz)

    attend(0, 3)
    attend(0, 1)
    relay(1)
    attend(1, 0)
    for which in range(2):
        forward(0, 2, which)
    attend(0, 2)
    attend(1, 3)
    attend(1, 1)
    for which in range(2):
        forward(1, 2, which)
    attend(1, 2)

    squares = jnp.zeros((256, 1), jnp.float32)
    for h in range(4):
        cols = slice(h * 128, h * 128 + 128)
        out = (acc_s[h] / l_s[h]).astype(jnp.bfloat16)
        lse_ref[h] = jnp.transpose(m_s[h] + jnp.log2(l_s[h]))[0:8]
        attn_ref[:, cols] = out
        mixed = (res_ref[:, cols].astype(jnp.float32) + out.astype(jnp.float32)).astype(
            jnp.bfloat16
        )
        mixed_ref[:, cols] = mixed
        mixed_f = mixed.astype(jnp.float32)
        squares += jnp.sum(mixed_f * mixed_f, axis=1, keepdims=True)
    turned = jnp.transpose(jnp.broadcast_to(squares, (256, 128)))
    sq_send[...] = turned[0:8]
    sq_recv[grp] = turned[0:8]

    @pl.loop(1, 8)
    def _(k):
        there = lax.rem(grp + k, 8)
        remote(
            sq_send, sq_recv.at[grp], sq_send_sem.at[k], sq_recv_sem.at[k], {"grp": there}
        ).start()

    @pl.loop(1, 8)
    def _(k):
        source = lax.rem(grp + 8 - k, 8)
        copy = remote(
            sq_send, sq_recv.at[source], sq_send_sem.at[k], sq_recv_sem.at[k], {"grp": source}
        )
        copy.wait_recv()
        copy.wait_send()

    total = sq_recv[0]
    for k in range(1, 8):
        total = total + sq_recv[k]
    inv = lax.rsqrt(total / 4096 + 1e-06)
    inv = jnp.transpose(jnp.concatenate([inv] * 16, axis=0))
    inv_ref[...] = inv
    normed = jnp.concatenate(
        [
            (mixed_ref[:, h * 128 : h * 128 + 128].astype(jnp.float32) * inv).astype(jnp.bfloat16)
            for h in range(4)
        ],
        axis=1,
    )

    @pl.loop(0, 16)
    def _(k):
        there = lax.rem(me + k, 16)
        xsend[k] = dot_nn(pick_both(rows_ref, there), normed).astype(jnp.bfloat16)

        @pl.when(k > 0)
        def _():
            remote(
                xsend.at[k], xrecv_ref.at[me], x_send_sem.at[k], x_recv_sem.at[k], {"ctx": there}
            ).start()

    xrecv_ref[me] = xsend[0]

    for dz in (1, 3, 2):
        summing.second(dz)
    summing.second_rest()

    def keep(rows, total):
        act_grad_ref[rows, :] = total

    summing.finish(keep)
    summing.drain()

    @pl.loop(1, 16)
    def _(k):
        source = lax.rem(me + 16 - k, 16)
        copy = remote(
            gsend.at[k], grecv_ref.at[source], g_send_sem.at[k], g_recv_sem.at[k], {"ctx": source}
        )
        copy.wait_send()
        copy = remote(
            xsend.at[k], xrecv_ref.at[source], x_send_sem.at[k], x_recv_sem.at[k], {"ctx": source}
        )
        copy.wait_recv()
        copy.wait_send()

    for copy in sent:
        copy.wait_send()
    for copy in outs:
        copy.wait()


def forward_call(*operands):
    bf, f32 = jnp.bfloat16, jnp.float32
    vmem = pl.BlockSpec(memory_space=pltpu.VMEM)
    shape = jax.ShapeDtypeStruct
    return pl.pallas_call(
        forward_kernel,
        out_shape=(
            shape((8, 512), jnp.int32),
            shape((8, 256), jnp.int32),
            shape((256, 512), bf),
            shape((4, 8, 256), f32),
            shape((256, 512), bf),
            shape((256, 128), f32),
            shape((16, 96, 512), bf),
            shape((16, 96, 512), bf),
            shape((192, 1536), f32),
            shape((2, 4, 2, 2, 256, 512), bf),
        ),
        in_specs=[vmem] * 4
        + [pl.BlockSpec(memory_space=pltpu.SMEM)]
        + [vmem] * 3
        + [pl.BlockSpec(memory_space=pl.ANY)],
        out_specs=[vmem] * 9 + [pl.BlockSpec(memory_space=pl.ANY)],
        scratch_shapes=[
            pltpu.VMEM((2, 4, 2, 2, 256, 512), bf),
            pltpu.VMEM((4, 256, 128), f32),
            pltpu.VMEM((4, 256, 128), f32),
            pltpu.VMEM((4, 256, 128), f32),
            pltpu.VMEM((16, 96, 512), bf),
            pltpu.VMEM((16, 96, 512), bf),
            pltpu.VMEM((2, 4, 192, 1536), bf),
            pltpu.VMEM((14, 192, 1536), bf),
            pltpu.VMEM((8, 256), f32),
            pltpu.VMEM((8, 8, 256), f32),
            pltpu.VMEM((512, 512), bf),
            pltpu.VMEM((256, 128), jnp.int32),
            pltpu.VMEM((2, 1536, 512), bf),
            pltpu.SemaphoreType.DMA,
            pltpu.SemaphoreType.DMA((30,)),
            pltpu.SemaphoreType.DMA((2, 4, 2, 2)),
            pltpu.SemaphoreType.DMA((2, 4)),
            pltpu.SemaphoreType.DMA((16,)),
            pltpu.SemaphoreType.DMA((16,)),
            pltpu.SemaphoreType.DMA((16,)),
            pltpu.SemaphoreType.DMA((16,)),
            pltpu.SemaphoreType.DMA((14,)),
            pltpu.SemaphoreType.DMA((14,)),
            pltpu.SemaphoreType.DMA((8,)),
            pltpu.SemaphoreType.DMA((8,)),
        ],
        compiler_params=pltpu.CompilerParams(
            collective_id=0, has_side_effects=True, vmem_limit_bytes=56 * 2**20
        ),
        name="forward",
    )(*operands)


TERM_ORDER = [(1, 3), (1, 1), (1, 2), (1, 0), (0, 3), (0, 1), (0, 2), (0, 0)]


def backward_kernel(
    q_ref, kv_hbm, lse_ref, attn_ref, qend_ref, og_ref, inv_ref, rows_ref, rg_ref, act_ref,
    w_out_hbm, g_hbm, mixed_ref, gates_ref,
    layer_ref, ig_ref, dq_ref, dk_ref, dv_ref, w_out_grad_ref,
    full, eo_send, eo_recv, kv_ref, w_out_ref, g_ref, load_sem, normed_grad, returned, row_dot, dqt, own_terms, sib_send, sib_recv, ring_send,
    ring_recv, part_send, part_recv,
    f_send_sem, f_recv_sem, r_send_sem, r_recv_sem, sib_send_sem, sib_recv_sem, ring_send_sem, ring_recv_sem,
    part_send_sem, part_recv_sem,
):
    me = lax.axis_index("ctx")
    core = lax.rem(me, 2)
    chip = me // 2
    x = lax.rem(chip, 4)
    yh = chip // 4
    bf, f32 = jnp.bfloat16, jnp.float32

    def device(dy, dx, dc):
        there = lax.rem(yh + dy, 2) * 4 + lax.rem(x + dx, 4)
        return {"ctx": there * 2 + lax.rem(core + dc, 2)}

    right, left = device(0, 1, 0), device(0, 3, 0)
    sibling, partner = device(0, 0, 1), device(1, 0, 0)
    loads = {}
    for dy, dx in TERM_ORDER:
        loads[(dy, dx)] = pltpu.make_async_copy(
            kv_hbm.at[dy, dx], kv_ref.at[dy, dx], load_sem.at[dy * 4 + dx]
        )
    w_load = pltpu.make_async_copy(w_out_hbm, w_out_ref, load_sem.at[8])
    g_load = pltpu.make_async_copy(g_hbm, g_ref, load_sem.at[9])
    loads[(1, 3)].start()
    loads[(1, 1)].start()
    greet()
    gathering = GrpGather(48, full, f_send_sem, f_recv_sem)
    full[0, 0] = act_ref[...]
    gathering.send_own()
    for dy, dx in TERM_ORDER[2:]:
        loads[(dy, dx)].start()
    w_load.start()
    g_load.start()
    dqt[...] = jnp.zeros_like(dqt)
    normed_grad[...] = jnp.zeros_like(normed_grad)

    @pl.loop(0, 16)
    def _(k):
        normed_grad[...] += dot_tn(pick_both(rows_ref, k), rg_ref[k])

    for h in range(4):
        cols = slice(h * 128, h * 128 + 128)
        grad = og_ref[:, cols].astype(f32) + inv_ref[...] * normed_grad[:, cols]
        grad = grad.astype(bf)
        ig_ref[:, cols] = grad
        dots = jnp.sum(grad.astype(f32) * attn_ref[:, cols].astype(f32), axis=1, keepdims=True)
        row_dot[h] = jnp.transpose(jnp.broadcast_to(dots, (256, 128)))[0:8]

    scale = HEAD_DIM**-0.5

    def terms(dy, dx):
        loads[(dy, dx)].wait()
        there = lax.rem(yh + dy, 2) * 4 + lax.rem(x + dx, 4)
        sub = lax.broadcasted_iota(jnp.int32, (256, 256), 0)
        qend = qend_ref[0:1, :]
        limits = [qend - (there * 512 + lax.rem(core + dc, 2) * 256) for dc in range(2)]

        @pl.loop(0, 4)
        def _(h):
            cols = pl.ds(pl.multiple_of(h * 128, 128), 128)
            qh = q_ref[:, cols]
            gh = ig_ref[:, cols]
            lse = lse_ref[h][0:1, :]
            dots = row_dot[h][0:1, :]
            for dc in range(2):
                kh = kv_ref[dy, dx, dc, 0, :, cols]
                vh = kv_ref[dy, dx, dc, 1, :, cols]
                s = dot_nt(kh, qh) * (LOG2E * scale)
                p = jnp.exp2(jnp.where(sub < limits[dc], s, LOW) - lse)
                dp = dot_nt(vh, gh)
                ds = (p * (dp - dots) * scale).astype(bf)
                dk = dot_nn(ds, qh).astype(bf)
                dv = dot_nn(p.astype(bf), gh).astype(bf)
                dqt[h] += dot_tn(kh, ds)
                to = own_terms if dc == 0 else sib_send
                to[dy, dx, 0, :, cols] = dk
                to[dy, dx, 1, :, cols] = dv

        for which in range(2):
            sib_copy(dy, dx, which).start()

    def sib_copy(dy, dx, which):
        return remote(
            sib_send.at[dy, dx, which],
            sib_recv.at[dy, dx, which],
            sib_send_sem.at[dy, dx, which],
            sib_recv_sem.at[dy, dx, which],
            sibling,
        )

    def ring_copy(dy, dx, which):
        to = (dx + 3) % 4 if which == 0 else (dx + 1) % 4
        return remote(
            ring_send.at[dy, dx, which],
            ring_recv.at[dy, to, which],
            ring_send_sem.at[dy, dx, which],
            ring_recv_sem.at[dy, to, which],
            right if which == 0 else left,
        )

    def arrival(dy, dx, which):
        return ring_copy(dy, (dx + 1) % 4 if which == 0 else (dx + 3) % 4, which)

    def total_of(dy, dx, which, ring):
        sib_copy(dy, dx, which).wait_recv()
        if ring:
            arrival(dy, dx, which).wait_recv()
        sums = own_terms[dy, dx, which].astype(f32) + sib_recv[dy, dx, which].astype(f32)
        if ring:
            sums = sums + ring_recv[dy, dx, which].astype(f32)
        return sums

    def send_ring(dy, dx, which, ring):
        ring_send[dy, dx, which] = total_of(dy, dx, which, ring).astype(bf)
        ring_copy(dy, dx, which).start()

    def part_copy(which):
        return remote(
            part_send.at[which],
            part_recv.at[which],
            part_send_sem.at[which],
            part_recv_sem.at[which],
            partner,
        )

    def expert_rows(dy, dz):
        expert, _ = chunk_of(dy, dz)
        rows = dot_nn(full[dy, dz], w_out_ref[expert]).astype(bf)
        return_rows(rows, dy, dz, eo_send, eo_recv, r_send_sem, r_recv_sem)

    terms(1, 3)
    terms(1, 1)
    send_ring(1, 3, 0, False)
    send_ring(1, 1, 1, False)
    terms(1, 2)
    terms(1, 0)
    w_load.wait()
    gathering.pass_rest()
    for dz in (1, 3, 2):
        gathering.pass_head(dz)
    send_ring(1, 2, 0, True)
    send_ring(1, 2, 1, True)
    expert_rows(0, 0)
    terms(0, 3)
    terms(0, 1)
    send_ring(1, 1, 0, True)
    send_ring(1, 3, 1, True)
    send_ring(0, 3, 0, False)
    send_ring(0, 1, 1, False)
    terms(0, 2)
    for which in range(2):
        part_send[which] = total_of(1, 0, which, True).astype(bf)
        part_copy(which).start()
    send_ring(0, 2, 0, True)
    send_ring(0, 2, 1, True)
    terms(0, 0)
    gathering.wait_chunk(1, 0)
    expert_rows(1, 0)
    for h in range(4):
        dq_ref[:, h * 128 : h * 128 + 128] = jnp.transpose(dqt[h]).astype(bf)
    send_ring(0, 1, 0, True)
    send_ring(0, 3, 1, True)
    for dz in (1, 3, 2):
        for dy in range(2):
            gathering.wait_chunk(dy, dz)
            expert_rows(dy, dz)
    for which in range(2):
        sums = total_of(0, 0, which, True)
        part_copy(which).wait_recv()
        sums = sums + part_recv[which].astype(f32)
        if which == 0:
            dk_ref[...] = sums.astype(bf)
        else:
            dv_ref[...] = sums.astype(bf)

    for dy in range(2):
        for dx in range(4):
            for which in range(2):
                sib_copy(dy, dx, which).wait_send()
                if dx > 0:
                    ring_copy(dy, dx, which).wait_send()
    for which in range(2):
        part_copy(which).wait_send()

    g_load.wait()
    for dy in range(2):
        expert, _ = chunk_of(dy, 0)

        @pl.loop(0, 3)
        def _(piece):
            cols = pl.ds(pl.multiple_of(piece * 512, 512), 512)
            total = dot_tn(full[dy, 0, :, cols], chunk_rows(g_ref, dy, 0))
            for dz in range(1, 4):
                total += dot_tn(full[dy, dz, :, cols], chunk_rows(g_ref, dy, dz))
            w_out_grad_ref[expert, cols, :] = total.astype(bf)

    wait_returns(eo_send, eo_recv, r_send_sem, r_recv_sem)
    returned[...] = jnp.zeros_like(returned)

    @pl.loop(0, 16)
    def _(k):
        returned[...] += dot_tn(pick_two(rows_ref, k), eo_recv[k].reshape(96, 512))

    for h in range(4):
        cols = slice(h * 128, h * 128 + 128)
        sums = (
            gates_ref[:, 0:1] * returned[0:256, cols] + gates_ref[:, 1:2] * returned[256:512, cols]
        )
        layer_ref[:, cols] = (mixed_ref[:, cols].astype(f32) + sums).astype(bf)

    gathering.drain()


def backward_call(*operands):
    bf, f32 = jnp.bfloat16, jnp.float32
    vmem = pl.BlockSpec(memory_space=pltpu.VMEM)
    anywhere = pl.BlockSpec(memory_space=pl.ANY)
    shape = jax.ShapeDtypeStruct
    return pl.pallas_call(
        backward_kernel,
        out_shape=(shape((256, 512), bf),) * 5 + (shape((2, 1536, 512), bf),),
        in_specs=[vmem, anywhere] + [vmem] * 8 + [anywhere] * 2 + [vmem] * 2,
        out_specs=(vmem,) * 6,
        scratch_shapes=[
            pltpu.VMEM((2, 4, 192, 1536), bf),
            pltpu.VMEM((2, 16, 48, 512), bf),
            pltpu.VMEM((16, 2, 48, 512), bf),
            pltpu.VMEM((2, 4, 2, 2, 256, 512), bf),
            pltpu.VMEM((2, 1536, 512), bf),
            pltpu.VMEM((16, 96, 512), bf),
            pltpu.SemaphoreType.DMA((10,)),
            pltpu.VMEM((256, 512), f32),
            pltpu.VMEM((512, 512), f32),
            pltpu.VMEM((4, 8, 256), f32),
            pltpu.VMEM((4, 128, 256), f32),
            pltpu.VMEM((2, 4, 2, 256, 512), bf),
            pltpu.VMEM((2, 4, 2, 256, 512), bf),
            pltpu.VMEM((2, 4, 2, 256, 512), bf),
            pltpu.VMEM((2, 4, 2, 256, 512), bf),
            pltpu.VMEM((2, 4, 2, 256, 512), bf),
            pltpu.VMEM((2, 256, 512), bf),
            pltpu.VMEM((2, 256, 512), bf),
            pltpu.SemaphoreType.DMA((14,)),
            pltpu.SemaphoreType.DMA((14,)),
            pltpu.SemaphoreType.DMA((2, 16)),
            pltpu.SemaphoreType.DMA((2, 16)),
            pltpu.SemaphoreType.DMA((2, 4, 2)),
            pltpu.SemaphoreType.DMA((2, 4, 2)),
            pltpu.SemaphoreType.DMA((2, 4, 2)),
            pltpu.SemaphoreType.DMA((2, 4, 2)),
            pltpu.SemaphoreType.DMA((2,)),
            pltpu.SemaphoreType.DMA((2,)),
        ],
        compiler_params=pltpu.CompilerParams(
            collective_id=1, has_side_effects=True, vmem_limit_bytes=56 * 2**20
        ),
        name="backward",
    )(*operands)


def publish_kernel(*refs):
    count = len(refs) // 2
    sems = refs[-1]
    copies = [
        pltpu.make_async_copy(refs[n], refs[count + n], sems.at[n]) for n in range(count)
    ]
    for copy in copies:
        copy.start()
    for copy in copies:
        copy.wait()


def publish(*arrays):
    anywhere = pl.BlockSpec(memory_space=pl.ANY)
    return pl.pallas_call(
        publish_kernel,
        out_shape=tuple(jax.ShapeDtypeStruct(a.shape, a.dtype) for a in arrays),
        in_specs=[anywhere] * len(arrays),
        out_specs=(anywhere,) * len(arrays),
        scratch_shapes=[pltpu.SemaphoreType.DMA((len(arrays),))],
        compiler_params=pltpu.CompilerParams(vmem_limit_bytes=56 * 2**20),
        name="publish",
    )(*arrays)


def shards(
    residual, queries, keys, values, frame_lengths, routes, route_gates, w_in, w_out, out_grad
):
    n_ctx = lax.axis_size("ctx")
    tok_rows, feat_dev = residual.shape
    exp_dev = w_in.shape[0]
    rows_wide, qend_row, attn, lse, mixed, inv_wide, rows_recv, grads_recv, act_grad, kv_all = (
        forward_call(
            queries,
            keys,
            values,
            residual,
            frame_lengths,
            routes,
            route_gates,
            out_grad,
            w_out,
        )
    )
    activated, row_grad, w_in_grad = experts_call(rows_recv, act_grad, w_in)
    layer_out, input_grad, query_grad, key_grad, value_grad, w_out_grad = backward_call(
        queries,
        kv_all,
        lse,
        attn,
        qend_row,
        out_grad,
        inv_wide,
        rows_wide,
        row_grad.reshape(n_ctx, exp_dev * row_grad.shape[2], feat_dev),
        activated,
        w_out,
        grads_recv,
        mixed,
        route_gates,
    )
    return publish(
        layer_out,
        input_grad,
        query_grad,
        key_grad,
        value_grad,
        w_in_grad,
        w_out_grad,
    )


def solution(mesh):
    in_specs = (
        P("ctx", "grp"),
        P("ctx", "grp"),
        P("ctx", "grp"),
        P("ctx", "grp"),
        P(),
        P("ctx", None),
        P("ctx", None),
        P("ctx", "grp", None),
        P("ctx", None, "grp"),
        P("ctx", "grp"),
    )
    out_specs = (
        P("ctx", "grp"),
        P("ctx", "grp"),
        P("ctx", "grp"),
        P("ctx", "grp"),
        P("ctx", "grp"),
        P("ctx", "grp", None),
        P("ctx", None, "grp"),
    )
    return jax.shard_map(shards, mesh=mesh, in_specs=in_specs, out_specs=out_specs, check_vma=False)
```

```python
import functools

import jax
import jax.numpy as jnp
from jax import lax
from jax.experimental import pallas as pl
from jax.experimental.pallas import tpu as pltpu
from jax.sharding import PartitionSpec as P

HEAD_DIM = 128


gelu_coef = 0.7978845608028654


def gelu_tanh(field):
    return 0.5 * field * (1.0 + jnp.tanh(gelu_coef * (field + 0.044715 * field * field * field)))


def gelu_slope(field):
    tanh_val = jnp.tanh(gelu_coef * (field + 0.044715 * field * field * field))
    return 0.5 * (1.0 + tanh_val) + 0.5 * field * (1.0 - tanh_val * tanh_val) * gelu_coef * (
        1.0 + 3.0 * 0.044715 * field * field
    )


MESH_ID = pl.DeviceIdType.MESH
LOG2E = 1.4426950408889634
LOW = -1e30


def dot_nt(a, b):
    return lax.dot_general(a, b, (((1,), (1,)), ((), ())), preferred_element_type=jnp.float32)


def dot_tn(a, b):
    return lax.dot_general(a, b, (((0,), (0,)), ((), ())), preferred_element_type=jnp.float32)


def dot_nn(a, b):
    return jnp.dot(a, b, preferred_element_type=jnp.float32)


def greet():
    me = lax.axis_index("ctx")
    grp = lax.axis_index("grp")
    barrier = pltpu.get_barrier_semaphore()

    @pl.loop(1, 16)
    def _(k):
        pl.semaphore_signal(
            barrier, inc=1, device_id={"ctx": lax.rem(me + k, 16)}, device_id_type=MESH_ID
        )

    @pl.loop(1, 8)
    def _(k):
        pl.semaphore_signal(
            barrier, inc=1, device_id={"grp": lax.rem(grp + k, 8)}, device_id_type=MESH_ID
        )

    pl.semaphore_wait(barrier, 22)


def remote(src, dst, send_sem, recv_sem, where):
    return pltpu.make_async_remote_copy(
        src_ref=src,
        dst_ref=dst,
        send_sem=send_sem,
        recv_sem=recv_sem,
        device_id=where,
        device_id_type=MESH_ID,
    )


def pick_two(rows_ref, there):
    rows = lax.broadcasted_iota(jnp.int32, (96, 512), 0) + there * 96
    return jnp.where(rows == rows_ref[0:1, :], 1.0, 0.0).astype(jnp.bfloat16)


def pick_both(rows_ref, there):
    rows = lax.broadcasted_iota(jnp.int32, (96, 256), 0) + there * 96
    hit = (rows == rows_ref[0:1, 0:256]) | (rows == rows_ref[0:1, 256:512])
    return jnp.where(hit, 1.0, 0.0).astype(jnp.bfloat16)


def grp_device(dy, dz):
    grp = lax.axis_index("grp")
    there = lax.rem(grp // 4 + dy, 2) * 4 + lax.rem(lax.rem(grp, 4) + dz, 4)
    return {"grp": there}


class GrpSum:
    def __init__(self, cut, part, recv, send_sem, recv_sem):
        self.cut, self.part, self.recv = cut, part, recv
        self.send_sem, self.recv_sem = send_sem, recv_sem
        self.head, self.rest = pl.ds(0, cut), pl.ds(cut, 192 - cut)

    def halves(self, group):
        start, size = (0, self.cut) if group == 2 else (self.cut, 192 - self.cut)
        low = size // 32 * 16
        return (start, low), (start + low, size - low)

    def make(self, number, src, slot, rows, where):
        return remote(
            src,
            self.recv.at[slot, rows],
            self.send_sem.at[number],
            self.recv_sem.at[number],
            where,
        )

    def partner_head(self, dz):
        return self.make(dz, self.part.at[1, dz, self.head], dz, self.head, grp_device(1, 0))

    def partner_rest(self):
        return self.make(22, self.part.at[1, 0, self.rest], 13, self.rest, grp_device(1, 0))

    def along(self, group, kind):
        dy, base = (0 if group == 2 else group), 4 + 3 * group
        low, high = [pl.ds(*half) for half in self.halves(group)]
        dz, rows, slot, to = [
            (2, low, base, 1),
            (2, high, base, 3),
            (1, high, base + 1, 1),
            (3, low, base + 2, 3),
            (1, low, base + 1, 1),
            (3, high, base + 2, 3),
        ][kind]
        number = 4 + 6 * group + kind
        return self.make(number, self.part.at[dy, dz, rows], slot, rows, grp_device(0, to))

    def start_along(self, group, dz):
        for kind in {0: [], 1: [2], 2: [0, 1], 3: [3]}[dz]:
            self.along(group, kind).start()

    def send_first(self, dy, dz):
        if dy == 1:
            self.partner_head(dz).start()
        self.start_along(dy, dz)

    def add(self, target, start, size, slots, out=None):
        def keep(rows, total):
            self.part[target[0], target[1], rows, :] = total.astype(jnp.bfloat16)

        @pl.loop(0, size // 16)
        def _(step):
            rows = pl.ds(pl.multiple_of(start + step * 16, 16), 16)
            total = self.part[target[0], target[1], rows, :].astype(jnp.float32)
            for slot in slots:
                total += self.recv[slot, rows, :].astype(jnp.float32)
            (out or keep)(rows, total)

    def relay(self, group):
        dy, base = (0 if group == 2 else group), 4 + 3 * group
        low, high = self.halves(group)
        self.along(group, 0).wait_recv()
        self.add((dy, 1), *low, [base])
        self.along(group, 4).start()
        self.along(group, 1).wait_recv()
        self.add((dy, 3), *high, [base])
        self.along(group, 5).start()

    def second(self, dz):
        self.partner_head(dz).wait_recv()
        self.add((0, dz), 0, self.cut, [dz])
        self.start_along(2, dz)

    def wait_along(self, group):
        for kind in range(2, 6):
            self.along(group, kind).wait_recv()

    def second_rest(self):
        self.wait_along(1)
        self.add((1, 0), self.cut, 192 - self.cut, [8, 9])
        self.partner_rest().start()

    def finish(self, out):
        self.partner_head(0).wait_recv()
        self.wait_along(2)
        self.add((0, 0), 0, self.cut, [0, 11, 12], out)
        self.wait_along(0)
        self.partner_rest().wait_recv()
        self.add((0, 0), self.cut, 192 - self.cut, [5, 6, 13], out)

    def drain(self):
        for dz in range(4):
            self.partner_head(dz).wait_send()
        for group in range(3):
            for kind in range(6):
                self.along(group, kind).wait_send()
        self.partner_rest().wait_send()


class GrpGather:
    def __init__(self, cut, full, send_sem, recv_sem):
        self.cut, self.full, self.send_sem, self.recv_sem = cut, full, send_sem, recv_sem
        self.head, self.rest = pl.ds(0, cut), pl.ds(cut, 192 - cut)
        self.waited = set()

    def make(self, number, src, dst, rows, where):
        return remote(
            self.full.at[src[0], src[1], rows],
            self.full.at[dst[0], dst[1], rows],
            self.send_sem.at[number],
            self.recv_sem.at[number],
            where,
        )

    def copy(self, number):
        if number < 12:
            group, kind = number // 4, number % 4
            dy = 1 if group == 2 else 0
            start, size = (0, self.cut) if group == 0 else (self.cut, 192 - self.cut)
            low = size // 32 * 16
            src, dst, rows, to = [
                (0, 3, (start, size), 1),
                (0, 1, (start, size), 3),
                (3, 2, (start, low), 1),
                (1, 2, (start + low, size - low), 3),
            ][kind]
            return self.make(number, (dy, src), (dy, dst), pl.ds(*rows), grp_device(0, to))
        if number < 16:
            dz = number - 12
            return self.make(number, (0, dz), (1, dz), self.head, grp_device(1, 0))
        return self.make(number, (0, 0), (1, 0), self.rest, grp_device(1, 0))

    def start(self, *numbers):
        for number in numbers:
            self.copy(number).start()

    def wait(self, *numbers):
        for number in numbers:
            if number not in self.waited:
                self.waited.add(number)
                self.copy(number).wait_recv()

    def send_own(self):
        self.start(16, 0, 1, 12, 4, 5)

    def relay(self, group):
        for kind in range(2):
            self.wait(4 * group + kind)
            self.start(4 * group + 2 + kind)

    def pass_head(self, dz):
        self.wait(*{1: [1], 2: [2, 3], 3: [0]}[dz])
        self.start(12 + dz)

    def pass_rest(self):
        self.wait(16)
        self.start(8, 9)

    def wait_chunk(self, dy, dz):
        self.wait(*[4 + 4 * dy + kind for kind in {0: [], 1: [1], 2: [2, 3], 3: [0]}[dz]])
        if dy == 1:
            self.wait(12 + dz, 16)

    def drain(self):
        for number in range(17):
            self.copy(number).wait_send()


def chunk_of(dy, dz):
    grp = lax.axis_index("grp")
    return lax.rem(grp // 4 + dy, 2), lax.rem(lax.rem(grp, 4) + dz, 4) * 4


def chunk_rows(ref, dy, dz):
    expert, first = chunk_of(dy, dz)
    rows = ref[pl.ds(first, 4), pl.ds(pl.multiple_of(expert * 48, 16), 48), :]
    return rows.reshape(192, 512)


CHUNK_ORDER = [(1, 2), (1, 1), (1, 3), (0, 2), (1, 0), (0, 1), (0, 3), (0, 0)]


def return_rows(rows, dy, dz, send, recv, send_sem, recv_sem):
    me = lax.axis_index("ctx")
    expert, first = chunk_of(dy, dz)
    send[expert, pl.ds(first, 4)] = rows.reshape(4, 48, 512)

    @pl.loop(0, 4)
    def _(i):
        there = first + i

        @pl.when(there != me)
        def _():
            return_copy(expert, there, me, there, send, recv, send_sem, recv_sem).start()


def return_copy(expert, there, mine, partner, send, recv, send_sem, recv_sem):
    return remote(
        send.at[expert, there],
        recv.at[mine, expert],
        send_sem.at[expert, there],
        recv_sem.at[expert, mine],
        {"ctx": partner},
    )


def wait_returns(send, recv, send_sem, recv_sem):
    me = lax.axis_index("ctx")
    for expert in range(2):
        recv[me, expert] = send[expert, me]

        @pl.loop(1, 16)
        def _(k):
            source = lax.rem(me + k, 16)
            copy = return_copy(
                expert, source, source, source, send, recv, send_sem, recv_sem
            )
            copy.wait_recv()
            copy.wait_send()


def experts_kernel(
    x_ref, act_grad_ref, w_in_hbm,
    act_ref, rg_ref, w_in_grad_ref,
    part, sums, full, rg_send, w_in_ref, w_sem,
    s_send_sem, s_recv_sem, f_send_sem, f_recv_sem, r_send_sem, r_recv_sem,
):
    bf = jnp.bfloat16
    w_copy = pltpu.make_async_copy(w_in_hbm, w_in_ref, w_sem)
    w_copy.start()
    greet()
    w_copy.wait()
    summing = GrpSum(96, part, sums, s_send_sem, s_recv_sem)
    gathering = GrpGather(96, full, f_send_sem, f_recv_sem)
    for dy, dz in CHUNK_ORDER:
        expert, _ = chunk_of(dy, dz)
        rows = chunk_rows(x_ref, dy, dz)

        @pl.loop(0, 3)
        def _(piece):
            cols = pl.ds(pl.multiple_of(piece * 512, 512), 512)
            part[dy, dz, :, cols] = dot_nn(rows, w_in_ref[expert, :, cols]).astype(bf)

        summing.send_first(dy, dz)
    summing.relay(1)
    summing.relay(0)
    for dz in (2, 1, 3):
        summing.second(dz)
    summing.relay(2)
    summing.second_rest()

    def activate(rows, pre):
        act_ref[rows, :] = gelu_tanh(pre).astype(bf)
        full[0, 0, rows, :] = (act_grad_ref[rows, :] * gelu_slope(pre)).astype(bf)

    summing.finish(activate)
    gathering.send_own()

    def row_grads(dy, dz):
        expert, _ = chunk_of(dy, dz)
        rows = dot_nt(full[dy, dz], w_in_ref[expert]).astype(bf)
        return_rows(rows, dy, dz, rg_send, rg_ref, r_send_sem, r_recv_sem)

    row_grads(0, 0)
    gathering.relay(0)
    for dz in (3, 1):
        gathering.pass_head(dz)
    gathering.pass_rest()
    gathering.relay(1)
    gathering.pass_head(2)
    for dy, dz in [(0, 1), (0, 3)]:
        gathering.wait_chunk(dy, dz)
        row_grads(dy, dz)
    gathering.relay(2)
    for dy, dz in [(1, 0), (1, 1), (1, 3), (0, 2), (1, 2)]:
        gathering.wait_chunk(dy, dz)
        row_grads(dy, dz)
    for dy in range(2):
        expert, _ = chunk_of(dy, 0)

        @pl.loop(0, 3)
        def _(piece):
            cols = pl.ds(pl.multiple_of(piece * 512, 512), 512)
            total = dot_tn(chunk_rows(x_ref, dy, 0), full[dy, 0, :, cols])
            for dz in range(1, 4):
                total += dot_tn(chunk_rows(x_ref, dy, dz), full[dy, dz, :, cols])
            w_in_grad_ref[expert, :, cols] = total.astype(bf)

    wait_returns(rg_send, rg_ref, r_send_sem, r_recv_sem)
    summing.drain()
    gathering.drain()


def experts_call(x_rows, act_grad, w_in):
    bf = jnp.bfloat16
    vmem = pl.BlockSpec(memory_space=pltpu.VMEM)
    shape = jax.ShapeDtypeStruct
    return pl.pallas_call(
        experts_kernel,
        out_shape=(
            shape((192, 1536), bf),
            shape((16, 2, 48, 512), bf),
            shape((2, 512, 1536), bf),
        ),
        in_specs=[vmem] * 2 + [pl.BlockSpec(memory_space=pl.ANY)],
        out_specs=(vmem,) * 3,
        scratch_shapes=[
            pltpu.VMEM((2, 4, 192, 1536), bf),
            pltpu.VMEM((14, 192, 1536), bf),
            pltpu.VMEM((2, 4, 192, 1536), bf),
            pltpu.VMEM((2, 16, 48, 512), bf),
            pltpu.VMEM((2, 512, 1536), bf),
            pltpu.SemaphoreType.DMA,
            pltpu.SemaphoreType.DMA((23,)),
            pltpu.SemaphoreType.DMA((23,)),
            pltpu.SemaphoreType.DMA((17,)),
            pltpu.SemaphoreType.DMA((17,)),
            pltpu.SemaphoreType.DMA((2, 16)),
            pltpu.SemaphoreType.DMA((2, 16)),
        ],
        compiler_params=pltpu.CompilerParams(
            collective_id=2, has_side_effects=True, vmem_limit_bytes=56 * 2**20
        ),
        name="experts",
    )(x_rows, act_grad, w_in)


def forward_kernel(
    q_ref, k_ref, v_ref, res_ref, lengths_ref, routes_ref, gates_ref, og_ref, w_out_hbm,
    rows_ref, qend_row_ref, attn_ref, lse_ref, mixed_ref, inv_ref, xrecv_ref, grecv_ref, act_grad_ref, kv_out_ref,
    kv, m_s, l_s, acc_s, gsend, xsend, part, sums, sq_send, sq_recv, gated, qend_s, w_out_ref,
    w_sem,
    kv_send_sem, kv_recv_sem, out_sem, g_send_sem, g_recv_sem, x_send_sem, x_recv_sem,
    p_send_sem, p_recv_sem, sq_send_sem, sq_recv_sem,
):
    me = lax.axis_index("ctx")
    grp = lax.axis_index("grp")
    core = lax.rem(me, 2)
    chip = me // 2
    x = lax.rem(chip, 4)
    yh = chip // 4

    def device(dy, dx, dc):
        there = lax.rem(yh + dy, 2) * 4 + lax.rem(x + dx, 4)
        return {"ctx": there * 2 + lax.rem(core + dc, 2)}

    w_copy = pltpu.make_async_copy(w_out_hbm, w_out_ref, w_sem)
    w_copy.start()
    greet()

    copies = {}
    sent = []

    def move(src, slot, where):
        copy = remote(src, kv.at[slot], kv_send_sem.at[len(sent)], kv_recv_sem.at[slot], where)
        copy.start()
        copies[slot] = copy
        sent.append(copy)

    def own(which):
        return k_ref if which == 0 else v_ref

    right, left = device(0, 1, 0), device(0, 3, 0)
    sibling, partner = device(0, 0, 1), device(1, 0, 0)
    for which in range(2):
        move(own(which), (1, 0, 0, which), partner)
    for which in range(2):
        move(own(which), (0, 0, 1, which), sibling)
    early = lax.broadcasted_iota(jnp.int32, (256, 256), 0) < lax.broadcasted_iota(
        jnp.int32, (256, 256), 1
    )
    experts = [routes_ref[:, a : a + 1].astype(jnp.float32) for a in range(2)]
    for a in range(2):
        expert_row = jnp.transpose(jnp.broadcast_to(experts[a], (256, 128)))[0:8]
        rank = jnp.zeros((1, 256), jnp.float32)
        for b in range(2):
            same = early & (experts[b] == expert_row[0:1])
            rank += jnp.sum(jnp.where(same, 1.0, 0.0), axis=0, keepdims=True)
        cols = slice(a * 256, a * 256 + 256)
        rows_ref[:, cols] = (expert_row * 48 + rank).astype(jnp.int32)
        gate = gates_ref[:, a : a + 1]
        gated[cols, :] = (gate * og_ref[...].astype(jnp.float32)).astype(jnp.bfloat16)

    @pl.loop(0, 16)
    def _(k):
        there = lax.rem(me + k, 16)
        gsend[k] = dot_nn(pick_two(rows_ref, there), gated[...]).astype(jnp.bfloat16)

        @pl.when(k > 0)
        def _():
            remote(
                gsend.at[k], grecv_ref.at[me], g_send_sem.at[k], g_recv_sem.at[k], {"ctx": there}
            ).start()

    for which in range(2):
        move(own(which), (0, 3, 0, which), right)
        move(own(which), (0, 1, 0, which), left)
    grecv_ref[me] = gsend[0]
    kv[0, 0, 0, 0] = k_ref[...]
    kv[0, 0, 0, 1] = v_ref[...]
    pos_col = me * 256 + lax.broadcasted_iota(jnp.int32, (256, 128), 0)
    pos_row = me * 256 + lax.broadcasted_iota(jnp.int32, (8, 256), 1)
    ends_col, ends_row = jnp.full_like(pos_col, 4096), jnp.full_like(pos_row, 4096)
    end = jnp.int32(0)
    for f in range(16):
        end = end + lengths_ref[f]
        ends_col = jnp.minimum(ends_col, jnp.where(end > pos_col, end, 4096))
        ends_row = jnp.minimum(ends_row, jnp.where(end > pos_row, end, 4096))
    qend_s[...] = ends_col
    qend_row_ref[...] = ends_row
    summing = GrpSum(96, part, sums, p_send_sem, p_recv_sem)
    m_s[...] = jnp.full_like(m_s, LOW)
    l_s[...] = jnp.zeros_like(l_s)
    acc_s[...] = jnp.zeros_like(acc_s)
    outs = []

    def wait_slot(dy, dx, dc, which):
        copies[(dy, dx, dc, which)].wait_recv()

    def forward(dy, dx, which):
        wait_slot(dy, dx, 0, which)
        move(kv.at[dy, dx, 0, which], (dy, dx, 1, which), sibling)

    def relay(dy):
        forward(dy, 3, 0)
        move(kv.at[dy, 3, 0, 0], (dy, 2, 0, 0), right)
        forward(dy, 1, 1)
        move(kv.at[dy, 1, 0, 1], (dy, 2, 0, 1), left)
        forward(dy, 3, 1)
        forward(dy, 1, 0)

    def attend(dy, dx):
        for which in range(2):
            wait_slot(dy, dx, 1, which)
        copy = pltpu.make_async_copy(kv.at[dy, dx], kv_out_ref.at[dy, dx], out_sem.at[dy, dx])
        copy.start()
        outs.append(copy)
        there = lax.rem(yh + dy, 2) * 4 + lax.rem(x + dx, 4)
        lane = lax.broadcasted_iota(jnp.int32, (256, 256), 1)
        qend = qend_s[:, 0:1]
        limits = [qend - (there * 512 + lax.rem(core + dc, 2) * 256) for dc in range(2)]

        @pl.loop(0, 4)
        def _(h):
            cols = pl.ds(pl.multiple_of(h * 128, 128), 128)
            qh = q_ref[:, cols]
            scores = []
            for dc in range(2):
                s = dot_nt(qh, kv[dy, dx, dc, 0, :, cols]) * (LOG2E * HEAD_DIM**-0.5)
                scores.append(jnp.where(lane < limits[dc], s, LOW))
            top = jnp.max(jnp.maximum(scores[0], scores[1]), axis=1, keepdims=True)
            m_old = m_s[h]
            m_new = jnp.maximum(m_old, top)
            alpha = jnp.exp2(m_old - m_new)
            probs = [jnp.exp2(s - m_new[:, 0:1]) for s in scores]
            total = jnp.sum(probs[0] + probs[1], axis=1, keepdims=True)
            m_s[h] = m_new
            l_s[h] = l_s[h] * alpha + total
            acc = acc_s[h] * alpha
            for dc in range(2):
                acc += dot_nn(probs[dc].astype(jnp.bfloat16), kv[dy, dx, dc, 1, :, cols])
            acc_s[h] = acc

    attend(0, 0)
    for which in range(2):
        wait_slot(1, 0, 0, which)
        move(kv.at[1, 0, 0, which], (1, 3, 0, which), right)
        move(kv.at[1, 0, 0, which], (1, 1, 0, which), left)
        move(kv.at[1, 0, 0, which], (1, 0, 1, which), sibling)

    relay(0)

    @pl.loop(1, 16)
    def _(k):
        source = lax.rem(me + 16 - k, 16)
        remote(
            gsend.at[k], grecv_ref.at[source], g_send_sem.at[k], g_recv_sem.at[k], {"ctx": source}
        ).wait_recv()

    w_copy.wait()
    for dy, dz in CHUNK_ORDER:
        expert, _ = chunk_of(dy, dz)
        rows = chunk_rows(grecv_ref, dy, dz)

        @pl.loop(0, 3)
        def _(piece):
            cols = pl.ds(pl.multiple_of(piece * 512, 512), 512)
            part[dy, dz, :, cols] = dot_nt(rows, w_out_ref[expert, cols, :]).astype(jnp.bfloat16)

        summing.send_first(dy, dz)

    attend(0, 3)
    attend(0, 1)
    relay(1)
    summing.relay(1)
    summing.relay(0)
    attend(1, 0)
    for which in range(2):
        forward(0, 2, which)
    attend(0, 2)
    for dz in (2, 1, 3):
        summing.second(dz)
    attend(1, 3)
    attend(1, 1)
    summing.relay(2)
    for which in range(2):
        forward(1, 2, which)
    attend(1, 2)

    squares = jnp.zeros((256, 1), jnp.float32)
    for h in range(4):
        cols = slice(h * 128, h * 128 + 128)
        out = (acc_s[h] / l_s[h]).astype(jnp.bfloat16)
        lse_ref[h] = jnp.transpose(m_s[h] + jnp.log2(l_s[h]))[0:8]
        attn_ref[:, cols] = out
        mixed = (res_ref[:, cols].astype(jnp.float32) + out.astype(jnp.float32)).astype(
            jnp.bfloat16
        )
        mixed_ref[:, cols] = mixed
        mixed_f = mixed.astype(jnp.float32)
        squares += jnp.sum(mixed_f * mixed_f, axis=1, keepdims=True)
    turned = jnp.transpose(jnp.broadcast_to(squares, (256, 128)))
    sq_send[...] = turned[0:8]
    sq_recv[grp] = turned[0:8]

    @pl.loop(1, 8)
    def _(k):
        there = lax.rem(grp + k, 8)
        remote(
            sq_send, sq_recv.at[grp], sq_send_sem.at[k], sq_recv_sem.at[k], {"grp": there}
        ).start()

    @pl.loop(1, 8)
    def _(k):
        source = lax.rem(grp + 8 - k, 8)
        copy = remote(
            sq_send, sq_recv.at[source], sq_send_sem.at[k], sq_recv_sem.at[k], {"grp": source}
        )
        copy.wait_recv()
        copy.wait_send()

    total = sq_recv[0]
    for k in range(1, 8):
        total = total + sq_recv[k]
    inv = lax.rsqrt(total / 4096 + 1e-06)
    inv = jnp.transpose(jnp.concatenate([inv] * 16, axis=0))
    inv_ref[...] = inv
    normed = jnp.concatenate(
        [
            (mixed_ref[:, h * 128 : h * 128 + 128].astype(jnp.float32) * inv).astype(jnp.bfloat16)
            for h in range(4)
        ],
        axis=1,
    )

    @pl.loop(0, 16)
    def _(k):
        there = lax.rem(me + k, 16)
        xsend[k] = dot_nn(pick_both(rows_ref, there), normed).astype(jnp.bfloat16)

        @pl.when(k > 0)
        def _():
            remote(
                xsend.at[k], xrecv_ref.at[me], x_send_sem.at[k], x_recv_sem.at[k], {"ctx": there}
            ).start()

    xrecv_ref[me] = xsend[0]

    summing.second_rest()

    def keep(rows, total):
        act_grad_ref[rows, :] = total

    summing.finish(keep)
    summing.drain()

    @pl.loop(1, 16)
    def _(k):
        source = lax.rem(me + 16 - k, 16)
        copy = remote(
            gsend.at[k], grecv_ref.at[source], g_send_sem.at[k], g_recv_sem.at[k], {"ctx": source}
        )
        copy.wait_send()
        copy = remote(
            xsend.at[k], xrecv_ref.at[source], x_send_sem.at[k], x_recv_sem.at[k], {"ctx": source}
        )
        copy.wait_recv()
        copy.wait_send()

    for copy in sent:
        copy.wait_send()
    for copy in outs:
        copy.wait()


def forward_call(*operands):
    bf, f32 = jnp.bfloat16, jnp.float32
    vmem = pl.BlockSpec(memory_space=pltpu.VMEM)
    shape = jax.ShapeDtypeStruct
    return pl.pallas_call(
        forward_kernel,
        out_shape=(
            shape((8, 512), jnp.int32),
            shape((8, 256), jnp.int32),
            shape((256, 512), bf),
            shape((4, 8, 256), f32),
            shape((256, 512), bf),
            shape((256, 128), f32),
            shape((16, 96, 512), bf),
            shape((16, 96, 512), bf),
            shape((192, 1536), f32),
            shape((2, 4, 2, 2, 256, 512), bf),
        ),
        in_specs=[vmem] * 4
        + [pl.BlockSpec(memory_space=pltpu.SMEM)]
        + [vmem] * 3
        + [pl.BlockSpec(memory_space=pl.ANY)],
        out_specs=[vmem] * 9 + [pl.BlockSpec(memory_space=pl.ANY)],
        scratch_shapes=[
            pltpu.VMEM((2, 4, 2, 2, 256, 512), bf),
            pltpu.VMEM((4, 256, 128), f32),
            pltpu.VMEM((4, 256, 128), f32),
            pltpu.VMEM((4, 256, 128), f32),
            pltpu.VMEM((16, 96, 512), bf),
            pltpu.VMEM((16, 96, 512), bf),
            pltpu.VMEM((2, 4, 192, 1536), bf),
            pltpu.VMEM((14, 192, 1536), bf),
            pltpu.VMEM((8, 256), f32),
            pltpu.VMEM((8, 8, 256), f32),
            pltpu.VMEM((512, 512), bf),
            pltpu.VMEM((256, 128), jnp.int32),
            pltpu.VMEM((2, 1536, 512), bf),
            pltpu.SemaphoreType.DMA,
            pltpu.SemaphoreType.DMA((30,)),
            pltpu.SemaphoreType.DMA((2, 4, 2, 2)),
            pltpu.SemaphoreType.DMA((2, 4)),
            pltpu.SemaphoreType.DMA((16,)),
            pltpu.SemaphoreType.DMA((16,)),
            pltpu.SemaphoreType.DMA((16,)),
            pltpu.SemaphoreType.DMA((16,)),
            pltpu.SemaphoreType.DMA((23,)),
            pltpu.SemaphoreType.DMA((23,)),
            pltpu.SemaphoreType.DMA((8,)),
            pltpu.SemaphoreType.DMA((8,)),
        ],
        compiler_params=pltpu.CompilerParams(
            collective_id=0, has_side_effects=True, vmem_limit_bytes=56 * 2**20
        ),
        name="forward",
    )(*operands)


TERM_ORDER = [(1, 3), (1, 1), (1, 2), (1, 0), (0, 3), (0, 1), (0, 2), (0, 0)]


def backward_kernel(
    q_ref, kv_hbm, lse_ref, attn_ref, qend_ref, og_ref, inv_ref, rows_ref, rg_ref, act_ref,
    w_out_hbm, g_hbm, mixed_ref, gates_ref,
    layer_ref, ig_ref, dq_ref, dk_ref, dv_ref, w_out_grad_ref,
    full, eo_send, eo_recv, kv_ref, w_out_ref, g_ref, load_sem, normed_grad, returned, row_dot, dqt, own_terms, sib_send, sib_recv, ring_send,
    ring_recv, part_send, part_recv,
    f_send_sem, f_recv_sem, r_send_sem, r_recv_sem, sib_send_sem, sib_recv_sem, ring_send_sem, ring_recv_sem,
    part_send_sem, part_recv_sem,
):
    me = lax.axis_index("ctx")
    core = lax.rem(me, 2)
    chip = me // 2
    x = lax.rem(chip, 4)
    yh = chip // 4
    bf, f32 = jnp.bfloat16, jnp.float32

    def device(dy, dx, dc):
        there = lax.rem(yh + dy, 2) * 4 + lax.rem(x + dx, 4)
        return {"ctx": there * 2 + lax.rem(core + dc, 2)}

    right, left = device(0, 1, 0), device(0, 3, 0)
    sibling, partner = device(0, 0, 1), device(1, 0, 0)
    loads = {}
    for dy, dx in TERM_ORDER:
        loads[(dy, dx)] = pltpu.make_async_copy(
            kv_hbm.at[dy, dx], kv_ref.at[dy, dx], load_sem.at[dy * 4 + dx]
        )
    w_load = pltpu.make_async_copy(w_out_hbm, w_out_ref, load_sem.at[8])
    g_load = pltpu.make_async_copy(g_hbm, g_ref, load_sem.at[9])
    loads[(1, 3)].start()
    loads[(1, 1)].start()
    greet()
    gathering = GrpGather(64, full, f_send_sem, f_recv_sem)
    full[0, 0] = act_ref[...]
    gathering.send_own()
    for dy, dx in TERM_ORDER[2:]:
        loads[(dy, dx)].start()
    w_load.start()
    g_load.start()
    dqt[...] = jnp.zeros_like(dqt)
    normed_grad[...] = jnp.zeros_like(normed_grad)

    @pl.loop(0, 16)
    def _(k):
        normed_grad[...] += dot_tn(pick_both(rows_ref, k), rg_ref[k])

    for h in range(4):
        cols = slice(h * 128, h * 128 + 128)
        grad = og_ref[:, cols].astype(f32) + inv_ref[...] * normed_grad[:, cols]
        grad = grad.astype(bf)
        ig_ref[:, cols] = grad
        dots = jnp.sum(grad.astype(f32) * attn_ref[:, cols].astype(f32), axis=1, keepdims=True)
        row_dot[h] = jnp.transpose(jnp.broadcast_to(dots, (256, 128)))[0:8]

    scale = HEAD_DIM**-0.5

    def terms(dy, dx):
        loads[(dy, dx)].wait()
        there = lax.rem(yh + dy, 2) * 4 + lax.rem(x + dx, 4)
        sub = lax.broadcasted_iota(jnp.int32, (256, 256), 0)
        qend = qend_ref[0:1, :]
        limits = [qend - (there * 512 + lax.rem(core + dc, 2) * 256) for dc in range(2)]

        @pl.loop(0, 4)
        def _(h):
            cols = pl.ds(pl.multiple_of(h * 128, 128), 128)
            qh = q_ref[:, cols]
            gh = ig_ref[:, cols]
            lse = lse_ref[h][0:1, :]
            dots = row_dot[h][0:1, :]
            for dc in range(2):
                kh = kv_ref[dy, dx, dc, 0, :, cols]
                vh = kv_ref[dy, dx, dc, 1, :, cols]
                s = dot_nt(kh, qh) * (LOG2E * scale)
                p = jnp.exp2(jnp.where(sub < limits[dc], s, LOW) - lse)
                dp = dot_nt(vh, gh)
                ds = (p * (dp - dots) * scale).astype(bf)
                dk = dot_nn(ds, qh).astype(bf)
                dv = dot_nn(p.astype(bf), gh).astype(bf)
                dqt[h] += dot_tn(kh, ds)
                to = own_terms if dc == 0 else sib_send
                to[dy, dx, 0, :, cols] = dk
                to[dy, dx, 1, :, cols] = dv

        for which in range(2):
            sib_copy(dy, dx, which).start()

    def sib_copy(dy, dx, which):
        return remote(
            sib_send.at[dy, dx, which],
            sib_recv.at[dy, dx, which],
            sib_send_sem.at[dy, dx, which],
            sib_recv_sem.at[dy, dx, which],
            sibling,
        )

    def ring_copy(dy, dx, which):
        to = (dx + 3) % 4 if which == 0 else (dx + 1) % 4
        return remote(
            ring_send.at[dy, dx, which],
            ring_recv.at[dy, to, which],
            ring_send_sem.at[dy, dx, which],
            ring_recv_sem.at[dy, to, which],
            right if which == 0 else left,
        )

    def arrival(dy, dx, which):
        return ring_copy(dy, (dx + 1) % 4 if which == 0 else (dx + 3) % 4, which)

    def total_of(dy, dx, which, ring):
        sib_copy(dy, dx, which).wait_recv()
        if ring:
            arrival(dy, dx, which).wait_recv()
        sums = own_terms[dy, dx, which].astype(f32) + sib_recv[dy, dx, which].astype(f32)
        if ring:
            sums = sums + ring_recv[dy, dx, which].astype(f32)
        return sums

    def send_ring(dy, dx, which, ring):
        ring_send[dy, dx, which] = total_of(dy, dx, which, ring).astype(bf)
        ring_copy(dy, dx, which).start()

    def part_copy(which):
        return remote(
            part_send.at[which],
            part_recv.at[which],
            part_send_sem.at[which],
            part_recv_sem.at[which],
            partner,
        )

    def expert_rows(dy, dz):
        expert, _ = chunk_of(dy, dz)
        rows = dot_nn(full[dy, dz], w_out_ref[expert]).astype(bf)
        return_rows(rows, dy, dz, eo_send, eo_recv, r_send_sem, r_recv_sem)

    terms(1, 3)
    terms(1, 1)
    send_ring(1, 3, 0, False)
    send_ring(1, 1, 1, False)
    terms(1, 2)
    terms(1, 0)
    w_load.wait()
    gathering.relay(0)
    for dz in (3, 1):
        gathering.pass_head(dz)
    gathering.pass_rest()
    gathering.relay(1)
    send_ring(1, 2, 0, True)
    send_ring(1, 2, 1, True)
    expert_rows(0, 0)
    terms(0, 3)
    terms(0, 1)
    send_ring(1, 1, 0, True)
    send_ring(1, 3, 1, True)
    send_ring(0, 3, 0, False)
    send_ring(0, 1, 1, False)
    gathering.pass_head(2)
    gathering.relay(2)
    terms(0, 2)
    for which in range(2):
        part_send[which] = total_of(1, 0, which, True).astype(bf)
        part_copy(which).start()
    send_ring(0, 2, 0, True)
    send_ring(0, 2, 1, True)
    terms(0, 0)
    gathering.wait_chunk(1, 0)
    expert_rows(1, 0)
    for h in range(4):
        dq_ref[:, h * 128 : h * 128 + 128] = jnp.transpose(dqt[h]).astype(bf)
    send_ring(0, 1, 0, True)
    send_ring(0, 3, 1, True)
    for dz in (1, 3, 2):
        for dy in range(2):
            gathering.wait_chunk(dy, dz)
            expert_rows(dy, dz)
    for which in range(2):
        sums = total_of(0, 0, which, True)
        part_copy(which).wait_recv()
        sums = sums + part_recv[which].astype(f32)
        if which == 0:
            dk_ref[...] = sums.astype(bf)
        else:
            dv_ref[...] = sums.astype(bf)

    for dy in range(2):
        for dx in range(4):
            for which in range(2):
                sib_copy(dy, dx, which).wait_send()
                if dx > 0:
                    ring_copy(dy, dx, which).wait_send()
    for which in range(2):
        part_copy(which).wait_send()

    g_load.wait()
    for dy in range(2):
        expert, _ = chunk_of(dy, 0)

        @pl.loop(0, 3)
        def _(piece):
            cols = pl.ds(pl.multiple_of(piece * 512, 512), 512)
            total = dot_tn(full[dy, 0, :, cols], chunk_rows(g_ref, dy, 0))
            for dz in range(1, 4):
                total += dot_tn(full[dy, dz, :, cols], chunk_rows(g_ref, dy, dz))
            w_out_grad_ref[expert, cols, :] = total.astype(bf)

    wait_returns(eo_send, eo_recv, r_send_sem, r_recv_sem)
    returned[...] = jnp.zeros_like(returned)

    @pl.loop(0, 16)
    def _(k):
        returned[...] += dot_tn(pick_two(rows_ref, k), eo_recv[k].reshape(96, 512))

    for h in range(4):
        cols = slice(h * 128, h * 128 + 128)
        sums = (
            gates_ref[:, 0:1] * returned[0:256, cols] + gates_ref[:, 1:2] * returned[256:512, cols]
        )
        layer_ref[:, cols] = (mixed_ref[:, cols].astype(f32) + sums).astype(bf)

    gathering.drain()


def backward_call(*operands):
    bf, f32 = jnp.bfloat16, jnp.float32
    vmem = pl.BlockSpec(memory_space=pltpu.VMEM)
    anywhere = pl.BlockSpec(memory_space=pl.ANY)
    shape = jax.ShapeDtypeStruct
    return pl.pallas_call(
        backward_kernel,
        out_shape=(shape((256, 512), bf),) * 5 + (shape((2, 1536, 512), bf),),
        in_specs=[vmem, anywhere] + [vmem] * 8 + [anywhere] * 2 + [vmem] * 2,
        out_specs=(vmem,) * 6,
        scratch_shapes=[
            pltpu.VMEM((2, 4, 192, 1536), bf),
            pltpu.VMEM((2, 16, 48, 512), bf),
            pltpu.VMEM((16, 2, 48, 512), bf),
            pltpu.VMEM((2, 4, 2, 2, 256, 512), bf),
            pltpu.VMEM((2, 1536, 512), bf),
            pltpu.VMEM((16, 96, 512), bf),
            pltpu.SemaphoreType.DMA((10,)),
            pltpu.VMEM((256, 512), f32),
            pltpu.VMEM((512, 512), f32),
            pltpu.VMEM((4, 8, 256), f32),
            pltpu.VMEM((4, 128, 256), f32),
            pltpu.VMEM((2, 4, 2, 256, 512), bf),
            pltpu.VMEM((2, 4, 2, 256, 512), bf),
            pltpu.VMEM((2, 4, 2, 256, 512), bf),
            pltpu.VMEM((2, 4, 2, 256, 512), bf),
            pltpu.VMEM((2, 4, 2, 256, 512), bf),
            pltpu.VMEM((2, 256, 512), bf),
            pltpu.VMEM((2, 256, 512), bf),
            pltpu.SemaphoreType.DMA((17,)),
            pltpu.SemaphoreType.DMA((17,)),
            pltpu.SemaphoreType.DMA((2, 16)),
            pltpu.SemaphoreType.DMA((2, 16)),
            pltpu.SemaphoreType.DMA((2, 4, 2)),
            pltpu.SemaphoreType.DMA((2, 4, 2)),
            pltpu.SemaphoreType.DMA((2, 4, 2)),
            pltpu.SemaphoreType.DMA((2, 4, 2)),
            pltpu.SemaphoreType.DMA((2,)),
            pltpu.SemaphoreType.DMA((2,)),
        ],
        compiler_params=pltpu.CompilerParams(
            collective_id=1, has_side_effects=True, vmem_limit_bytes=56 * 2**20
        ),
        name="backward",
    )(*operands)


def publish_kernel(count, *refs):
    sources, targets, held = refs[:count], refs[count : 2 * count], refs[2 * count : 3 * count]
    in_sem, out_sem = refs[3 * count :]
    reads = [pltpu.make_async_copy(sources[n], held[n], in_sem.at[n]) for n in range(count)]
    writes = [pltpu.make_async_copy(held[n], targets[n], out_sem.at[n]) for n in range(count)]
    for read in reads:
        read.start()
    for read, write in zip(reads, writes):
        read.wait()
        write.start()
    for write in writes:
        write.wait()


def publish(*arrays):
    anywhere = pl.BlockSpec(memory_space=pl.ANY)
    count = len(arrays)
    return pl.pallas_call(
        functools.partial(publish_kernel, count),
        out_shape=tuple(jax.ShapeDtypeStruct(a.shape, a.dtype) for a in arrays),
        in_specs=[anywhere] * count,
        out_specs=(anywhere,) * count,
        scratch_shapes=[pltpu.VMEM(a.shape, a.dtype) for a in arrays]
        + [pltpu.SemaphoreType.DMA((count,))] * 2,
        compiler_params=pltpu.CompilerParams(vmem_limit_bytes=56 * 2**20),
        name="publish",
    )(*arrays)


def shards(
    residual, queries, keys, values, frame_lengths, routes, route_gates, w_in, w_out, out_grad
):
    n_ctx = lax.axis_size("ctx")
    tok_rows, feat_dev = residual.shape
    exp_dev = w_in.shape[0]
    rows_wide, qend_row, attn, lse, mixed, inv_wide, rows_recv, grads_recv, act_grad, kv_all = (
        forward_call(
            queries,
            keys,
            values,
            residual,
            frame_lengths,
            routes,
            route_gates,
            out_grad,
            w_out,
        )
    )
    activated, row_grad, w_in_grad = experts_call(rows_recv, act_grad, w_in)
    layer_out, input_grad, query_grad, key_grad, value_grad, w_out_grad = backward_call(
        queries,
        kv_all,
        lse,
        attn,
        qend_row,
        out_grad,
        inv_wide,
        rows_wide,
        row_grad.reshape(n_ctx, exp_dev * row_grad.shape[2], feat_dev),
        activated,
        w_out,
        grads_recv,
        mixed,
        route_gates,
    )
    return publish(
        layer_out,
        input_grad,
        query_grad,
        key_grad,
        value_grad,
        w_in_grad,
        w_out_grad,
    )


def solution(mesh):
    in_specs = (
        P("ctx", "grp"),
        P("ctx", "grp"),
        P("ctx", "grp"),
        P("ctx", "grp"),
        P(),
        P("ctx", None),
        P("ctx", None),
        P("ctx", "grp", None),
        P("ctx", None, "grp"),
        P("ctx", "grp"),
    )
    out_specs = (
        P("ctx", "grp"),
        P("ctx", "grp"),
        P("ctx", "grp"),
        P("ctx", "grp"),
        P("ctx", "grp"),
        P("ctx", "grp", None),
        P("ctx", None, "grp"),
    )
    return jax.shard_map(shards, mesh=mesh, in_specs=in_specs, out_specs=out_specs, check_vma=False)
```

```python
import functools

import jax
import jax.numpy as jnp
from jax import lax
from jax.experimental import pallas as pl
from jax.experimental.pallas import tpu as pltpu
from jax.sharding import PartitionSpec as P

HEAD_DIM = 128


gelu_coef = 0.7978845608028654


def gelu_tanh(field):
    return 0.5 * field * (1.0 + jnp.tanh(gelu_coef * (field + 0.044715 * field * field * field)))


def gelu_slope(field):
    tanh_val = jnp.tanh(gelu_coef * (field + 0.044715 * field * field * field))
    return 0.5 * (1.0 + tanh_val) + 0.5 * field * (1.0 - tanh_val * tanh_val) * gelu_coef * (
        1.0 + 3.0 * 0.044715 * field * field
    )


MESH_ID = pl.DeviceIdType.MESH
LOG2E = 1.4426950408889634
LOW = -1e30


def dot_nt(a, b):
    return lax.dot_general(a, b, (((1,), (1,)), ((), ())), preferred_element_type=jnp.float32)


def dot_tn(a, b):
    return lax.dot_general(a, b, (((0,), (0,)), ((), ())), preferred_element_type=jnp.float32)


def dot_nn(a, b):
    return jnp.dot(a, b, preferred_element_type=jnp.float32)


def greet():
    me = lax.axis_index("ctx")
    grp = lax.axis_index("grp")
    barrier = pltpu.get_barrier_semaphore()

    @pl.loop(1, 16)
    def _(k):
        pl.semaphore_signal(
            barrier, inc=1, device_id={"ctx": lax.rem(me + k, 16)}, device_id_type=MESH_ID
        )

    @pl.loop(1, 8)
    def _(k):
        pl.semaphore_signal(
            barrier, inc=1, device_id={"grp": lax.rem(grp + k, 8)}, device_id_type=MESH_ID
        )

    pl.semaphore_wait(barrier, 22)


def remote(src, dst, send_sem, recv_sem, where):
    return pltpu.make_async_remote_copy(
        src_ref=src,
        dst_ref=dst,
        send_sem=send_sem,
        recv_sem=recv_sem,
        device_id=where,
        device_id_type=MESH_ID,
    )


def pick_two(rows_ref, there):
    rows = lax.broadcasted_iota(jnp.int32, (96, 512), 0) + there * 96
    return jnp.where(rows == rows_ref[0:1, :], 1.0, 0.0).astype(jnp.bfloat16)


def pick_both(rows_ref, there):
    rows = lax.broadcasted_iota(jnp.int32, (96, 256), 0) + there * 96
    hit = (rows == rows_ref[0:1, 0:256]) | (rows == rows_ref[0:1, 256:512])
    return jnp.where(hit, 1.0, 0.0).astype(jnp.bfloat16)


def grp_device(dy, dz):
    grp = lax.axis_index("grp")
    there = lax.rem(grp // 4 + dy, 2) * 4 + lax.rem(lax.rem(grp, 4) + dz, 4)
    return {"grp": there}


class GrpSum:
    def __init__(self, cut, part, recv, send_sem, recv_sem):
        self.cut, self.part, self.recv = cut, part, recv
        self.send_sem, self.recv_sem = send_sem, recv_sem
        self.head, self.rest = pl.ds(0, cut), pl.ds(cut, 192 - cut)

    def halves(self, group):
        start, size = (0, self.cut) if group == 2 else (self.cut, 192 - self.cut)
        low = size // 32 * 16
        return (start, low), (start + low, size - low)

    def make(self, number, src, slot, rows, where):
        return remote(
            src,
            self.recv.at[slot, rows],
            self.send_sem.at[number],
            self.recv_sem.at[number],
            where,
        )

    def partner_head(self, dz):
        return self.make(dz, self.part.at[1, dz, self.head], dz, self.head, grp_device(1, 0))

    def partner_rest(self):
        return self.make(22, self.part.at[1, 0, self.rest], 13, self.rest, grp_device(1, 0))

    def along(self, group, kind):
        dy, base = (0 if group == 2 else group), 4 + 3 * group
        low, high = [pl.ds(*half) for half in self.halves(group)]
        dz, rows, slot, to = [
            (2, low, base, 1),
            (2, high, base, 3),
            (1, high, base + 1, 1),
            (3, low, base + 2, 3),
            (1, low, base + 1, 1),
            (3, high, base + 2, 3),
        ][kind]
        number = 4 + 6 * group + kind
        return self.make(number, self.part.at[dy, dz, rows], slot, rows, grp_device(0, to))

    def start_along(self, group, dz):
        for kind in {0: [], 1: [2], 2: [0, 1], 3: [3]}[dz]:
            self.along(group, kind).start()

    def send_first(self, dy, dz):
        if dy == 1:
            self.partner_head(dz).start()
        self.start_along(dy, dz)

    def add(self, target, start, size, slots, out=None):
        def keep(rows, total):
            self.part[target[0], target[1], rows, :] = total.astype(jnp.bfloat16)

        @pl.loop(0, size // 16)
        def _(step):
            rows = pl.ds(pl.multiple_of(start + step * 16, 16), 16)
            total = self.part[target[0], target[1], rows, :].astype(jnp.float32)
            for slot in slots:
                total += self.recv[slot, rows, :].astype(jnp.float32)
            (out or keep)(rows, total)

    def relay(self, group):
        dy, base = (0 if group == 2 else group), 4 + 3 * group
        low, high = self.halves(group)
        self.along(group, 0).wait_recv()
        self.add((dy, 1), *low, [base])
        self.along(group, 4).start()
        self.along(group, 1).wait_recv()
        self.add((dy, 3), *high, [base])
        self.along(group, 5).start()

    def second(self, dz):
        self.partner_head(dz).wait_recv()
        self.add((0, dz), 0, self.cut, [dz])
        self.start_along(2, dz)

    def wait_along(self, group):
        for kind in range(2, 6):
            self.along(group, kind).wait_recv()

    def second_rest(self):
        self.wait_along(1)
        self.add((1, 0), self.cut, 192 - self.cut, [8, 9])
        self.partner_rest().start()

    def finish_head(self, out):
        self.partner_head(0).wait_recv()
        self.wait_along(2)
        self.add((0, 0), 0, self.cut, [0, 11, 12], out)

    def finish_rest(self, out):
        self.wait_along(0)
        self.partner_rest().wait_recv()
        self.add((0, 0), self.cut, 192 - self.cut, [5, 6, 13], out)

    def drain(self):
        for dz in range(4):
            self.partner_head(dz).wait_send()
        for group in range(3):
            for kind in range(6):
                self.along(group, kind).wait_send()
        self.partner_rest().wait_send()


class GrpGather:
    def __init__(self, cut, full, send_sem, recv_sem):
        self.cut, self.full, self.send_sem, self.recv_sem = cut, full, send_sem, recv_sem
        self.head, self.rest = pl.ds(0, cut), pl.ds(cut, 192 - cut)
        self.waited = set()

    def make(self, number, src, dst, rows, where):
        return remote(
            self.full.at[src[0], src[1], rows],
            self.full.at[dst[0], dst[1], rows],
            self.send_sem.at[number],
            self.recv_sem.at[number],
            where,
        )

    def copy(self, number):
        if number < 12:
            group, kind = number // 4, number % 4
            dy = 1 if group == 2 else 0
            start, size = (0, self.cut) if group == 0 else (self.cut, 192 - self.cut)
            low = size // 32 * 16
            src, dst, rows, to = [
                (0, 3, (start, size), 1),
                (0, 1, (start, size), 3),
                (3, 2, (start, low), 1),
                (1, 2, (start + low, size - low), 3),
            ][kind]
            return self.make(number, (dy, src), (dy, dst), pl.ds(*rows), grp_device(0, to))
        if number < 16:
            dz = number - 12
            return self.make(number, (0, dz), (1, dz), self.head, grp_device(1, 0))
        return self.make(number, (0, 0), (1, 0), self.rest, grp_device(1, 0))

    def start(self, *numbers):
        for number in numbers:
            self.copy(number).start()

    def wait(self, *numbers):
        for number in numbers:
            if number not in self.waited:
                self.waited.add(number)
                self.copy(number).wait_recv()

    def send_own(self):
        self.start(16, 0, 1, 12, 4, 5)

    def relay(self, group):
        for kind in range(2):
            self.wait(4 * group + kind)
            self.start(4 * group + 2 + kind)

    def pass_head(self, dz):
        self.wait(*{1: [1], 2: [2, 3], 3: [0]}[dz])
        self.start(12 + dz)

    def pass_rest(self):
        self.wait(16)
        self.start(8, 9)

    def wait_chunk(self, dy, dz):
        self.wait(*[4 + 4 * dy + kind for kind in {0: [], 1: [1], 2: [2, 3], 3: [0]}[dz]])
        if dy == 1:
            self.wait(12 + dz, 16)

    def drain(self):
        for number in range(17):
            self.copy(number).wait_send()


def chunk_of(dy, dz):
    grp = lax.axis_index("grp")
    return lax.rem(grp // 4 + dy, 2), lax.rem(lax.rem(grp, 4) + dz, 4) * 4


def chunk_rows(ref, dy, dz):
    expert, first = chunk_of(dy, dz)
    rows = ref[pl.ds(first, 4), pl.ds(pl.multiple_of(expert * 48, 16), 48), :]
    return rows.reshape(192, 512)


CHUNK_ORDER = [(1, 2), (1, 1), (1, 3), (0, 2), (1, 0), (0, 1), (0, 3), (0, 0)]


def return_rows(rows, dy, dz, send, recv, send_sem, recv_sem):
    me = lax.axis_index("ctx")
    expert, first = chunk_of(dy, dz)
    send[expert, pl.ds(first, 4)] = rows.reshape(4, 48, 512)

    @pl.loop(0, 4)
    def _(i):
        there = first + i

        @pl.when(there != me)
        def _():
            return_copy(expert, there, me, there, send, recv, send_sem, recv_sem).start()


def return_copy(expert, there, mine, partner, send, recv, send_sem, recv_sem):
    return remote(
        send.at[expert, there],
        recv.at[mine, expert],
        send_sem.at[expert, there],
        recv_sem.at[expert, mine],
        {"ctx": partner},
    )


def wait_returns(send, recv, send_sem, recv_sem):
    me = lax.axis_index("ctx")
    for expert in range(2):
        recv[me, expert] = send[expert, me]

        @pl.loop(1, 16)
        def _(k):
            source = lax.rem(me + k, 16)
            copy = return_copy(
                expert, source, source, source, send, recv, send_sem, recv_sem
            )
            copy.wait_recv()
            copy.wait_send()


def experts_kernel(
    x_ref, act_grad_ref, w_in_hbm,
    act_ref, rg_ref, w_in_grad_ref,
    part, sums, full, rg_send, w_in_ref, w_sem,
    s_send_sem, s_recv_sem, f_send_sem, f_recv_sem, r_send_sem, r_recv_sem,
):
    bf = jnp.bfloat16
    w_copy = pltpu.make_async_copy(w_in_hbm, w_in_ref, w_sem)
    w_copy.start()
    greet()
    w_copy.wait()
    summing = GrpSum(96, part, sums, s_send_sem, s_recv_sem)
    gathering = GrpGather(96, full, f_send_sem, f_recv_sem)
    for dy, dz in CHUNK_ORDER:
        expert, _ = chunk_of(dy, dz)
        rows = chunk_rows(x_ref, dy, dz)

        @pl.loop(0, 3)
        def _(piece):
            cols = pl.ds(pl.multiple_of(piece * 512, 512), 512)
            part[dy, dz, :, cols] = dot_nn(rows, w_in_ref[expert, :, cols]).astype(bf)

        summing.send_first(dy, dz)
    summing.relay(1)
    summing.relay(0)
    for dz in (2, 1, 3):
        summing.second(dz)
    summing.relay(2)
    summing.second_rest()

    def activate(rows, pre):
        act_ref[rows, :] = gelu_tanh(pre).astype(bf)
        full[0, 0, rows, :] = (act_grad_ref[rows, :] * gelu_slope(pre)).astype(bf)

    summing.finish_head(activate)
    gathering.start(0, 1, 12)
    summing.finish_rest(activate)
    gathering.start(16, 4, 5)

    def row_grads(dy, dz):
        expert, _ = chunk_of(dy, dz)
        rows = dot_nt(full[dy, dz], w_in_ref[expert]).astype(bf)
        return_rows(rows, dy, dz, rg_send, rg_ref, r_send_sem, r_recv_sem)

    row_grads(0, 0)
    gathering.relay(0)
    for dz in (3, 1):
        gathering.pass_head(dz)
    gathering.pass_rest()
    gathering.relay(1)
    gathering.pass_head(2)
    for dy, dz in [(0, 1), (0, 3)]:
        gathering.wait_chunk(dy, dz)
        row_grads(dy, dz)
    gathering.relay(2)
    for dy, dz in [(1, 0), (1, 1), (1, 3), (0, 2), (1, 2)]:
        gathering.wait_chunk(dy, dz)
        row_grads(dy, dz)
    for dy in range(2):
        expert, _ = chunk_of(dy, 0)

        @pl.loop(0, 3)
        def _(piece):
            cols = pl.ds(pl.multiple_of(piece * 512, 512), 512)
            total = dot_tn(chunk_rows(x_ref, dy, 0), full[dy, 0, :, cols])
            for dz in range(1, 4):
                total += dot_tn(chunk_rows(x_ref, dy, dz), full[dy, dz, :, cols])
            w_in_grad_ref[expert, :, cols] = total.astype(bf)

    wait_returns(rg_send, rg_ref, r_send_sem, r_recv_sem)
    summing.drain()
    gathering.drain()


def experts_call(x_rows, act_grad, w_in):
    bf = jnp.bfloat16
    vmem = pl.BlockSpec(memory_space=pltpu.VMEM)
    shape = jax.ShapeDtypeStruct
    return pl.pallas_call(
        experts_kernel,
        out_shape=(
            shape((192, 1536), bf),
            shape((16, 2, 48, 512), bf),
            shape((2, 512, 1536), bf),
        ),
        in_specs=[vmem] * 2 + [pl.BlockSpec(memory_space=pl.ANY)],
        out_specs=(vmem,) * 3,
        scratch_shapes=[
            pltpu.VMEM((2, 4, 192, 1536), bf),
            pltpu.VMEM((14, 192, 1536), bf),
            pltpu.VMEM((2, 4, 192, 1536), bf),
            pltpu.VMEM((2, 16, 48, 512), bf),
            pltpu.VMEM((2, 512, 1536), bf),
            pltpu.SemaphoreType.DMA,
            pltpu.SemaphoreType.DMA((23,)),
            pltpu.SemaphoreType.DMA((23,)),
            pltpu.SemaphoreType.DMA((17,)),
            pltpu.SemaphoreType.DMA((17,)),
            pltpu.SemaphoreType.DMA((2, 16)),
            pltpu.SemaphoreType.DMA((2, 16)),
        ],
        compiler_params=pltpu.CompilerParams(
            collective_id=2, has_side_effects=True, vmem_limit_bytes=56 * 2**20
        ),
        name="experts",
    )(x_rows, act_grad, w_in)


def turn(row):
    return jnp.transpose(jnp.broadcast_to(row, (128, 256)))


def forward_kernel(
    q_ref, k_ref, v_ref, res_ref, lengths_ref, routes_ref, gates_ref, og_ref, w_out_hbm,
    rows_ref, rows_col_ref, qend_row_ref, attn_ref, lse_ref, mixed_ref, inv_ref, xrecv_ref, grecv_ref, act_grad_ref, kv_out_ref,
    kv, m_s, l_s, acc_s, gsend, xsend, part, sums, sq_send, sq_recv, gated, qend_s, w_out_ref,
    w_sem,
    kv_send_sem, kv_recv_sem, out_sem, g_send_sem, g_recv_sem, x_send_sem, x_recv_sem,
    p_send_sem, p_recv_sem, sq_send_sem, sq_recv_sem,
):
    me = lax.axis_index("ctx")
    grp = lax.axis_index("grp")
    core = lax.rem(me, 2)
    chip = me // 2
    x = lax.rem(chip, 4)
    yh = chip // 4

    def device(dy, dx, dc):
        there = lax.rem(yh + dy, 2) * 4 + lax.rem(x + dx, 4)
        return {"ctx": there * 2 + lax.rem(core + dc, 2)}

    w_copy = pltpu.make_async_copy(w_out_hbm, w_out_ref, w_sem)
    w_copy.start()
    greet()

    copies = {}
    sent = []

    def move(src, slot, where):
        copy = remote(src, kv.at[slot], kv_send_sem.at[len(sent)], kv_recv_sem.at[slot], where)
        copy.start()
        copies[slot] = copy
        sent.append(copy)

    def own(which):
        return k_ref if which == 0 else v_ref

    right, left = device(0, 1, 0), device(0, 3, 0)
    sibling, partner = device(0, 0, 1), device(1, 0, 0)
    for which in range(2):
        move(own(which), (1, 0, 0, which), partner)
        move(own(which), (0, 3, 0, which), right)
        move(own(which), (0, 1, 0, which), left)
    for which in range(2):
        move(own(which), (0, 0, 1, which), sibling)
    early = lax.broadcasted_iota(jnp.int32, (256, 256), 0) < lax.broadcasted_iota(
        jnp.int32, (256, 256), 1
    )
    experts = [routes_ref[a : a + 1, :].astype(jnp.float32) for a in range(2)]
    for a in range(2):
        rank = jnp.zeros((1, 256), jnp.float32)
        for b in range(2):
            same = early & (turn(experts[b])[:, 0:1] == experts[a])
            rank += jnp.sum(jnp.where(same, 1.0, 0.0), axis=0, keepdims=True)
        cols = slice(a * 256, a * 256 + 256)
        rows = experts[a] * 48 + rank
        rows_ref[:, cols] = jnp.broadcast_to(rows, (8, 256)).astype(jnp.int32)
        rows_col_ref[:, a * 128 : a * 128 + 128] = turn(rows).astype(jnp.int32)
        gate = turn(gates_ref[a : a + 1, :])[:, 0:1]
        gated[cols, :] = (gate * og_ref[...].astype(jnp.float32)).astype(jnp.bfloat16)

    @pl.loop(0, 16)
    def _(k):
        there = lax.rem(me + k, 16)
        gsend[k] = dot_nn(pick_two(rows_ref, there), gated[...]).astype(jnp.bfloat16)

        @pl.when(k > 0)
        def _():
            remote(
                gsend.at[k], grecv_ref.at[me], g_send_sem.at[k], g_recv_sem.at[k], {"ctx": there}
            ).start()

    grecv_ref[me] = gsend[0]
    kv[0, 0, 0, 0] = k_ref[...]
    kv[0, 0, 0, 1] = v_ref[...]
    pos_col = me * 256 + lax.broadcasted_iota(jnp.int32, (256, 128), 0)
    pos_row = me * 256 + lax.broadcasted_iota(jnp.int32, (8, 256), 1)
    ends_col, ends_row = jnp.full_like(pos_col, 4096), jnp.full_like(pos_row, 4096)
    end = jnp.int32(0)
    for f in range(16):
        end = end + lengths_ref[f]
        ends_col = jnp.minimum(ends_col, jnp.where(end > pos_col, end, 4096))
        ends_row = jnp.minimum(ends_row, jnp.where(end > pos_row, end, 4096))
    qend_s[...] = ends_col
    qend_row_ref[...] = ends_row
    summing = GrpSum(96, part, sums, p_send_sem, p_recv_sem)
    m_s[...] = jnp.full_like(m_s, LOW)
    l_s[...] = jnp.zeros_like(l_s)
    acc_s[...] = jnp.zeros_like(acc_s)
    outs = []

    def wait_slot(dy, dx, dc, which):
        copies[(dy, dx, dc, which)].wait_recv()

    def forward(dy, dx, which):
        wait_slot(dy, dx, 0, which)
        move(kv.at[dy, dx, 0, which], (dy, dx, 1, which), sibling)

    def relay(dy):
        forward(dy, 3, 0)
        move(kv.at[dy, 3, 0, 0], (dy, 2, 0, 0), right)
        forward(dy, 1, 1)
        move(kv.at[dy, 1, 0, 1], (dy, 2, 0, 1), left)
        forward(dy, 3, 1)
        forward(dy, 1, 0)

    def attend(dy, dx):
        for which in range(2):
            wait_slot(dy, dx, 1, which)
        copy = pltpu.make_async_copy(kv.at[dy, dx], kv_out_ref.at[dy, dx], out_sem.at[dy, dx])
        copy.start()
        outs.append(copy)
        there = lax.rem(yh + dy, 2) * 4 + lax.rem(x + dx, 4)
        lane = lax.broadcasted_iota(jnp.int32, (256, 256), 1)
        qend = qend_s[:, 0:1]
        limits = [qend - (there * 512 + lax.rem(core + dc, 2) * 256) for dc in range(2)]

        @pl.loop(0, 4)
        def _(h):
            cols = pl.ds(pl.multiple_of(h * 128, 128), 128)
            qh = q_ref[:, cols]
            scores = []
            for dc in range(2):
                s = dot_nt(qh, kv[dy, dx, dc, 0, :, cols]) * (LOG2E * HEAD_DIM**-0.5)
                scores.append(jnp.where(lane < limits[dc], s, LOW))
            top = jnp.max(jnp.maximum(scores[0], scores[1]), axis=1, keepdims=True)
            m_old = m_s[h]
            m_new = jnp.maximum(m_old, top)
            alpha = jnp.exp2(m_old - m_new)
            probs = [jnp.exp2(s - m_new[:, 0:1]) for s in scores]
            total = jnp.sum(probs[0] + probs[1], axis=1, keepdims=True)
            m_s[h] = m_new
            l_s[h] = l_s[h] * alpha + total
            acc = acc_s[h] * alpha
            for dc in range(2):
                acc += dot_nn(probs[dc].astype(jnp.bfloat16), kv[dy, dx, dc, 1, :, cols])
            acc_s[h] = acc

    attend(0, 0)
    for which in range(2):
        wait_slot(1, 0, 0, which)
        move(kv.at[1, 0, 0, which], (1, 3, 0, which), right)
        move(kv.at[1, 0, 0, which], (1, 1, 0, which), left)
        move(kv.at[1, 0, 0, which], (1, 0, 1, which), sibling)

    relay(0)

    @pl.loop(1, 16)
    def _(k):
        source = lax.rem(me + 16 - k, 16)
        remote(
            gsend.at[k], grecv_ref.at[source], g_send_sem.at[k], g_recv_sem.at[k], {"ctx": source}
        ).wait_recv()

    w_copy.wait()
    for dy, dz in CHUNK_ORDER:
        expert, _ = chunk_of(dy, dz)
        rows = chunk_rows(grecv_ref, dy, dz)

        @pl.loop(0, 3)
        def _(piece):
            cols = pl.ds(pl.multiple_of(piece * 512, 512), 512)
            part[dy, dz, :, cols] = dot_nt(rows, w_out_ref[expert, cols, :]).astype(jnp.bfloat16)

        summing.send_first(dy, dz)

    attend(0, 3)
    attend(0, 1)
    relay(1)
    summing.relay(1)
    summing.relay(0)
    attend(1, 0)
    for which in range(2):
        forward(0, 2, which)
    attend(0, 2)
    for dz in (2, 1, 3):
        summing.second(dz)
    attend(1, 3)
    attend(1, 1)
    summing.relay(2)
    for which in range(2):
        forward(1, 2, which)
    attend(1, 2)

    squares = jnp.zeros((256, 1), jnp.float32)
    for h in range(4):
        cols = slice(h * 128, h * 128 + 128)
        out = (acc_s[h] / l_s[h]).astype(jnp.bfloat16)
        lse_ref[h] = jnp.transpose(m_s[h] + jnp.log2(l_s[h]))[0:8]
        attn_ref[:, cols] = out
        mixed = (res_ref[:, cols].astype(jnp.float32) + out.astype(jnp.float32)).astype(
            jnp.bfloat16
        )
        mixed_ref[:, cols] = mixed
        mixed_f = mixed.astype(jnp.float32)
        squares += jnp.sum(mixed_f * mixed_f, axis=1, keepdims=True)
    turned = jnp.transpose(jnp.broadcast_to(squares, (256, 128)))
    sq_send[...] = turned[0:8]
    sq_recv[grp] = turned[0:8]

    @pl.loop(1, 8)
    def _(k):
        there = lax.rem(grp + k, 8)
        remote(
            sq_send, sq_recv.at[grp], sq_send_sem.at[k], sq_recv_sem.at[k], {"grp": there}
        ).start()

    @pl.loop(1, 8)
    def _(k):
        source = lax.rem(grp + 8 - k, 8)
        copy = remote(
            sq_send, sq_recv.at[source], sq_send_sem.at[k], sq_recv_sem.at[k], {"grp": source}
        )
        copy.wait_recv()
        copy.wait_send()

    total = sq_recv[0]
    for k in range(1, 8):
        total = total + sq_recv[k]
    inv = lax.rsqrt(total / 4096 + 1e-06)
    inv = jnp.transpose(jnp.concatenate([inv] * 16, axis=0))
    inv_ref[...] = inv
    normed = jnp.concatenate(
        [
            (mixed_ref[:, h * 128 : h * 128 + 128].astype(jnp.float32) * inv).astype(jnp.bfloat16)
            for h in range(4)
        ],
        axis=1,
    )

    @pl.loop(0, 16)
    def _(k):
        there = lax.rem(me + k, 16)
        xsend[k] = dot_nn(pick_both(rows_ref, there), normed).astype(jnp.bfloat16)

        @pl.when(k > 0)
        def _():
            remote(
                xsend.at[k], xrecv_ref.at[me], x_send_sem.at[k], x_recv_sem.at[k], {"ctx": there}
            ).start()

    xrecv_ref[me] = xsend[0]

    summing.second_rest()

    def keep(rows, total):
        act_grad_ref[rows, :] = total

    summing.finish_head(keep)
    summing.finish_rest(keep)
    summing.drain()

    @pl.loop(1, 16)
    def _(k):
        source = lax.rem(me + 16 - k, 16)
        copy = remote(
            gsend.at[k], grecv_ref.at[source], g_send_sem.at[k], g_recv_sem.at[k], {"ctx": source}
        )
        copy.wait_send()
        copy = remote(
            xsend.at[k], xrecv_ref.at[source], x_send_sem.at[k], x_recv_sem.at[k], {"ctx": source}
        )
        copy.wait_recv()
        copy.wait_send()

    for copy in sent:
        copy.wait_send()
    for copy in outs:
        copy.wait()


def forward_call(*operands):
    bf, f32 = jnp.bfloat16, jnp.float32
    vmem = pl.BlockSpec(memory_space=pltpu.VMEM)
    shape = jax.ShapeDtypeStruct
    return pl.pallas_call(
        forward_kernel,
        out_shape=(
            shape((8, 512), jnp.int32),
            shape((256, 256), jnp.int32),
            shape((8, 256), jnp.int32),
            shape((256, 512), bf),
            shape((4, 8, 256), f32),
            shape((256, 512), bf),
            shape((256, 128), f32),
            shape((16, 96, 512), bf),
            shape((16, 96, 512), bf),
            shape((192, 1536), f32),
            shape((2, 4, 2, 2, 256, 512), bf),
        ),
        in_specs=[vmem] * 4
        + [pl.BlockSpec(memory_space=pltpu.SMEM)]
        + [vmem] * 3
        + [pl.BlockSpec(memory_space=pl.ANY)],
        out_specs=[vmem] * 10 + [pl.BlockSpec(memory_space=pl.ANY)],
        scratch_shapes=[
            pltpu.VMEM((2, 4, 2, 2, 256, 512), bf),
            pltpu.VMEM((4, 256, 128), f32),
            pltpu.VMEM((4, 256, 128), f32),
            pltpu.VMEM((4, 256, 128), f32),
            pltpu.VMEM((16, 96, 512), bf),
            pltpu.VMEM((16, 96, 512), bf),
            pltpu.VMEM((2, 4, 192, 1536), bf),
            pltpu.VMEM((14, 192, 1536), bf),
            pltpu.VMEM((8, 256), f32),
            pltpu.VMEM((8, 8, 256), f32),
            pltpu.VMEM((512, 512), bf),
            pltpu.VMEM((256, 128), jnp.int32),
            pltpu.VMEM((2, 1536, 512), bf),
            pltpu.SemaphoreType.DMA,
            pltpu.SemaphoreType.DMA((30,)),
            pltpu.SemaphoreType.DMA((2, 4, 2, 2)),
            pltpu.SemaphoreType.DMA((2, 4)),
            pltpu.SemaphoreType.DMA((16,)),
            pltpu.SemaphoreType.DMA((16,)),
            pltpu.SemaphoreType.DMA((16,)),
            pltpu.SemaphoreType.DMA((16,)),
            pltpu.SemaphoreType.DMA((23,)),
            pltpu.SemaphoreType.DMA((23,)),
            pltpu.SemaphoreType.DMA((8,)),
            pltpu.SemaphoreType.DMA((8,)),
        ],
        compiler_params=pltpu.CompilerParams(
            collective_id=0, has_side_effects=True, vmem_limit_bytes=56 * 2**20
        ),
        name="forward",
    )(*operands)


TERM_ORDER = [(1, 3), (1, 1), (1, 2), (1, 0), (0, 3), (0, 1), (0, 2), (0, 0)]


def backward_kernel(
    q_ref, kv_hbm, lse_ref, attn_ref, qend_ref, og_ref, inv_ref, rows_ref, rg_ref, act_ref,
    w_out_hbm, g_hbm, mixed_ref, gates_ref,
    layer_ref, ig_ref, dq_ref, dk_ref, dv_ref, w_out_grad_ref,
    full, eo_send, eo_recv, kv_ref, w_out_ref, g_ref, load_sem, normed_grad, row_dot, dqt, own_terms, sib_send, sib_recv, ring_send,
    ring_recv, part_send, part_recv,
    f_send_sem, f_recv_sem, r_send_sem, r_recv_sem, sib_send_sem, sib_recv_sem, ring_send_sem, ring_recv_sem,
    part_send_sem, part_recv_sem,
):
    me = lax.axis_index("ctx")
    core = lax.rem(me, 2)
    chip = me // 2
    x = lax.rem(chip, 4)
    yh = chip // 4
    bf, f32 = jnp.bfloat16, jnp.float32

    def device(dy, dx, dc):
        there = lax.rem(yh + dy, 2) * 4 + lax.rem(x + dx, 4)
        return {"ctx": there * 2 + lax.rem(core + dc, 2)}

    right, left = device(0, 1, 0), device(0, 3, 0)
    sibling, partner = device(0, 0, 1), device(1, 0, 0)
    loads = {}
    for dy, dx in TERM_ORDER:
        loads[(dy, dx)] = pltpu.make_async_copy(
            kv_hbm.at[dy, dx], kv_ref.at[dy, dx], load_sem.at[dy * 4 + dx]
        )
    w_load = pltpu.make_async_copy(w_out_hbm, w_out_ref, load_sem.at[8])
    g_load = pltpu.make_async_copy(g_hbm, g_ref, load_sem.at[9])
    loads[(1, 3)].start()
    loads[(1, 1)].start()
    greet()
    gathering = GrpGather(64, full, f_send_sem, f_recv_sem)
    full[0, 0] = act_ref[...]
    gathering.send_own()
    for dy, dx in TERM_ORDER[2:]:
        loads[(dy, dx)].start()
    w_load.start()
    g_load.start()
    dqt[...] = jnp.zeros_like(dqt)
    row_id = lax.broadcasted_iota(jnp.int32, (256, 1536), 1)
    hits = [row_id == rows_ref[:, a * 128 : a * 128 + 1] for a in range(2)]
    pick = jnp.where(hits[0] | hits[1], 1.0, 0.0).astype(bf)
    normed_grad[...] = dot_nn(pick, rg_ref[...].reshape(1536, 512))

    for h in range(4):
        cols = slice(h * 128, h * 128 + 128)
        grad = og_ref[:, cols].astype(f32) + inv_ref[...] * normed_grad[:, cols]
        grad = grad.astype(bf)
        ig_ref[:, cols] = grad
        dots = jnp.sum(grad.astype(f32) * attn_ref[:, cols].astype(f32), axis=1, keepdims=True)
        row_dot[h] = jnp.transpose(jnp.broadcast_to(dots, (256, 128)))[0:8]

    scale = HEAD_DIM**-0.5

    def terms(dy, dx):
        loads[(dy, dx)].wait()
        there = lax.rem(yh + dy, 2) * 4 + lax.rem(x + dx, 4)
        sub = lax.broadcasted_iota(jnp.int32, (256, 256), 0)
        qend = qend_ref[0:1, :]
        limits = [qend - (there * 512 + lax.rem(core + dc, 2) * 256) for dc in range(2)]

        @pl.loop(0, 4)
        def _(h):
            cols = pl.ds(pl.multiple_of(h * 128, 128), 128)
            qh = q_ref[:, cols]
            gh = ig_ref[:, cols]
            lse = lse_ref[h][0:1, :]
            dots = row_dot[h][0:1, :]
            for dc in range(2):
                kh = kv_ref[dy, dx, dc, 0, :, cols]
                vh = kv_ref[dy, dx, dc, 1, :, cols]
                s = dot_nt(kh, qh) * (LOG2E * scale)
                p = jnp.exp2(jnp.where(sub < limits[dc], s, LOW) - lse)
                dp = dot_nt(vh, gh)
                ds = (p * (dp - dots) * scale).astype(bf)
                dk = dot_nn(ds, qh).astype(bf)
                dv = dot_nn(p.astype(bf), gh).astype(bf)
                dqt[h] += dot_tn(kh, ds)
                to = own_terms if dc == 0 else sib_send
                to[dy, dx, 0, :, cols] = dk
                to[dy, dx, 1, :, cols] = dv

        for which in range(2):
            sib_copy(dy, dx, which).start()

    def sib_copy(dy, dx, which):
        return remote(
            sib_send.at[dy, dx, which],
            sib_recv.at[dy, dx, which],
            sib_send_sem.at[dy, dx, which],
            sib_recv_sem.at[dy, dx, which],
            sibling,
        )

    def ring_copy(dy, dx, which):
        to = (dx + 3) % 4 if which == 0 else (dx + 1) % 4
        return remote(
            ring_send.at[dy, dx, which],
            ring_recv.at[dy, to, which],
            ring_send_sem.at[dy, dx, which],
            ring_recv_sem.at[dy, to, which],
            right if which == 0 else left,
        )

    def arrival(dy, dx, which):
        return ring_copy(dy, (dx + 1) % 4 if which == 0 else (dx + 3) % 4, which)

    def total_of(dy, dx, which, ring):
        sib_copy(dy, dx, which).wait_recv()
        if ring:
            arrival(dy, dx, which).wait_recv()
        sums = own_terms[dy, dx, which].astype(f32) + sib_recv[dy, dx, which].astype(f32)
        if ring:
            sums = sums + ring_recv[dy, dx, which].astype(f32)
        return sums

    def send_ring(dy, dx, which, ring):
        ring_send[dy, dx, which] = total_of(dy, dx, which, ring).astype(bf)
        ring_copy(dy, dx, which).start()

    def part_copy(which):
        return remote(
            part_send.at[which],
            part_recv.at[which],
            part_send_sem.at[which],
            part_recv_sem.at[which],
            partner,
        )

    def expert_rows(dy, dz):
        expert, _ = chunk_of(dy, dz)
        rows = dot_nn(full[dy, dz], w_out_ref[expert]).astype(bf)
        return_rows(rows, dy, dz, eo_send, eo_recv, r_send_sem, r_recv_sem)

    terms(1, 3)
    terms(1, 1)
    send_ring(1, 3, 0, False)
    send_ring(1, 1, 1, False)
    terms(1, 2)
    terms(1, 0)
    w_load.wait()
    gathering.relay(0)
    for dz in (3, 1):
        gathering.pass_head(dz)
    gathering.pass_rest()
    gathering.relay(1)
    send_ring(1, 2, 0, True)
    send_ring(1, 2, 1, True)
    expert_rows(0, 0)
    terms(0, 3)
    terms(0, 1)
    send_ring(1, 1, 0, True)
    send_ring(1, 3, 1, True)
    send_ring(0, 3, 0, False)
    send_ring(0, 1, 1, False)
    gathering.pass_head(2)
    gathering.relay(2)
    terms(0, 2)
    for which in range(2):
        part_send[which] = total_of(1, 0, which, True).astype(bf)
        part_copy(which).start()
    send_ring(0, 2, 0, True)
    send_ring(0, 2, 1, True)
    terms(0, 0)
    for dy, dz in [(0, 1), (0, 3), (1, 0)]:
        gathering.wait_chunk(dy, dz)
        expert_rows(dy, dz)
    for h in range(4):
        dq_ref[:, h * 128 : h * 128 + 128] = jnp.transpose(dqt[h]).astype(bf)
    send_ring(0, 1, 0, True)
    send_ring(0, 3, 1, True)
    for dy, dz in [(0, 2), (1, 1), (1, 3), (1, 2)]:
        gathering.wait_chunk(dy, dz)
        expert_rows(dy, dz)
    for which in range(2):
        sums = total_of(0, 0, which, True)
        part_copy(which).wait_recv()
        sums = sums + part_recv[which].astype(f32)
        if which == 0:
            dk_ref[...] = sums.astype(bf)
        else:
            dv_ref[...] = sums.astype(bf)

    for dy in range(2):
        for dx in range(4):
            for which in range(2):
                sib_copy(dy, dx, which).wait_send()
                if dx > 0:
                    ring_copy(dy, dx, which).wait_send()
    for which in range(2):
        part_copy(which).wait_send()

    g_load.wait()
    for dy in range(2):
        expert, _ = chunk_of(dy, 0)

        @pl.loop(0, 3)
        def _(piece):
            cols = pl.ds(pl.multiple_of(piece * 512, 512), 512)
            total = dot_tn(full[dy, 0, :, cols], chunk_rows(g_ref, dy, 0))
            for dz in range(1, 4):
                total += dot_tn(full[dy, dz, :, cols], chunk_rows(g_ref, dy, dz))
            w_out_grad_ref[expert, cols, :] = total.astype(bf)

    wait_returns(eo_send, eo_recv, r_send_sem, r_recv_sem)
    total = mixed_ref[...].astype(f32)
    for a in range(2):
        hit = row_id == rows_ref[:, a * 128 : a * 128 + 1]
        picked = dot_nn(jnp.where(hit, 1.0, 0.0).astype(bf), eo_recv[...].reshape(1536, 512))
        total = total + turn(gates_ref[a : a + 1, :])[:, 0:1] * picked
    layer_ref[...] = total.astype(bf)

    gathering.drain()


def backward_call(*operands):
    bf, f32 = jnp.bfloat16, jnp.float32
    vmem = pl.BlockSpec(memory_space=pltpu.VMEM)
    anywhere = pl.BlockSpec(memory_space=pl.ANY)
    shape = jax.ShapeDtypeStruct
    return pl.pallas_call(
        backward_kernel,
        out_shape=(shape((256, 512), bf),) * 5 + (shape((2, 1536, 512), bf),),
        in_specs=[vmem, anywhere] + [vmem] * 8 + [anywhere] * 2 + [vmem] * 2,
        out_specs=(vmem,) * 6,
        scratch_shapes=[
            pltpu.VMEM((2, 4, 192, 1536), bf),
            pltpu.VMEM((2, 16, 48, 512), bf),
            pltpu.VMEM((16, 2, 48, 512), bf),
            pltpu.VMEM((2, 4, 2, 2, 256, 512), bf),
            pltpu.VMEM((2, 1536, 512), bf),
            pltpu.VMEM((16, 96, 512), bf),
            pltpu.SemaphoreType.DMA((10,)),
            pltpu.VMEM((256, 512), f32),
            pltpu.VMEM((4, 8, 256), f32),
            pltpu.VMEM((4, 128, 256), f32),
            pltpu.VMEM((2, 4, 2, 256, 512), bf),
            pltpu.VMEM((2, 4, 2, 256, 512), bf),
            pltpu.VMEM((2, 4, 2, 256, 512), bf),
            pltpu.VMEM((2, 4, 2, 256, 512), bf),
            pltpu.VMEM((2, 4, 2, 256, 512), bf),
            pltpu.VMEM((2, 256, 512), bf),
            pltpu.VMEM((2, 256, 512), bf),
            pltpu.SemaphoreType.DMA((17,)),
            pltpu.SemaphoreType.DMA((17,)),
            pltpu.SemaphoreType.DMA((2, 16)),
            pltpu.SemaphoreType.DMA((2, 16)),
            pltpu.SemaphoreType.DMA((2, 4, 2)),
            pltpu.SemaphoreType.DMA((2, 4, 2)),
            pltpu.SemaphoreType.DMA((2, 4, 2)),
            pltpu.SemaphoreType.DMA((2, 4, 2)),
            pltpu.SemaphoreType.DMA((2,)),
            pltpu.SemaphoreType.DMA((2,)),
        ],
        compiler_params=pltpu.CompilerParams(
            collective_id=1, has_side_effects=True, vmem_limit_bytes=56 * 2**20
        ),
        name="backward",
    )(*operands)


def publish_kernel(count, *refs):
    sources, targets, held = refs[:count], refs[count : 2 * count], refs[2 * count : 3 * count]
    in_sem, out_sem = refs[3 * count :]
    reads = [pltpu.make_async_copy(sources[n], held[n], in_sem.at[n]) for n in range(count)]
    writes = [pltpu.make_async_copy(held[n], targets[n], out_sem.at[n]) for n in range(count)]
    for read in reads:
        read.start()
    for read, write in zip(reads, writes):
        read.wait()
        write.start()
    for write in writes:
        write.wait()


def publish(*arrays):
    anywhere = pl.BlockSpec(memory_space=pl.ANY)
    count = len(arrays)
    return pl.pallas_call(
        functools.partial(publish_kernel, count),
        out_shape=tuple(jax.ShapeDtypeStruct(a.shape, a.dtype) for a in arrays),
        in_specs=[anywhere] * count,
        out_specs=(anywhere,) * count,
        scratch_shapes=[pltpu.VMEM(a.shape, a.dtype) for a in arrays]
        + [pltpu.SemaphoreType.DMA((count,))] * 2,
        compiler_params=pltpu.CompilerParams(vmem_limit_bytes=56 * 2**20),
        name="publish",
    )(*arrays)


def shards(
    residual, queries, keys, values, frame_lengths, routes, route_gates, w_in, w_out, out_grad
):
    n_ctx = lax.axis_size("ctx")
    tok_rows, feat_dev = residual.shape
    exp_dev = w_in.shape[0]
    rows_wide, rows_col, qend_row, attn, lse, mixed, inv_wide, rows_recv, grads_recv, act_grad, kv_all = (
        forward_call(
            queries,
            keys,
            values,
            residual,
            frame_lengths,
            routes.T,
            route_gates.T,
            out_grad,
            w_out,
        )
    )
    activated, row_grad, w_in_grad = experts_call(rows_recv, act_grad, w_in)
    layer_out, input_grad, query_grad, key_grad, value_grad, w_out_grad = backward_call(
        queries,
        kv_all,
        lse,
        attn,
        qend_row,
        out_grad,
        inv_wide,
        rows_col,
        row_grad.reshape(n_ctx, exp_dev * row_grad.shape[2], feat_dev),
        activated,
        w_out,
        grads_recv,
        mixed,
        route_gates.T,
    )
    return publish(
        layer_out,
        input_grad,
        query_grad,
        key_grad,
        value_grad,
        w_in_grad,
        w_out_grad,
    )


def solution(mesh):
    in_specs = (
        P("ctx", "grp"),
        P("ctx", "grp"),
        P("ctx", "grp"),
        P("ctx", "grp"),
        P(),
        P("ctx", None),
        P("ctx", None),
        P("ctx", "grp", None),
        P("ctx", None, "grp"),
        P("ctx", "grp"),
    )
    out_specs = (
        P("ctx", "grp"),
        P("ctx", "grp"),
        P("ctx", "grp"),
        P("ctx", "grp"),
        P("ctx", "grp"),
        P("ctx", "grp", None),
        P("ctx", None, "grp"),
    )
    return jax.shard_map(shards, mesh=mesh, in_specs=in_specs, out_specs=out_specs, check_vma=False)
```

```python
import functools

import jax
import jax.numpy as jnp
from jax import lax
from jax.experimental import pallas as pl
from jax.experimental.pallas import tpu as pltpu
from jax.sharding import PartitionSpec as P

HEAD_DIM = 128


gelu_coef = 0.7978845608028654


def gelu_tanh(field):
    return 0.5 * field * (1.0 + jnp.tanh(gelu_coef * (field + 0.044715 * field * field * field)))


def gelu_slope(field):
    tanh_val = jnp.tanh(gelu_coef * (field + 0.044715 * field * field * field))
    return 0.5 * (1.0 + tanh_val) + 0.5 * field * (1.0 - tanh_val * tanh_val) * gelu_coef * (
        1.0 + 3.0 * 0.044715 * field * field
    )


MESH_ID = pl.DeviceIdType.MESH
LOG2E = 1.4426950408889634
LOW = -1e30


def dot_nt(a, b):
    return lax.dot_general(a, b, (((1,), (1,)), ((), ())), preferred_element_type=jnp.float32)


def dot_tn(a, b):
    return lax.dot_general(a, b, (((0,), (0,)), ((), ())), preferred_element_type=jnp.float32)


def dot_nn(a, b):
    return jnp.dot(a, b, preferred_element_type=jnp.float32)


def greet():
    me = lax.axis_index("ctx")
    grp = lax.axis_index("grp")
    barrier = pltpu.get_barrier_semaphore()

    @pl.loop(1, 16)
    def _(k):
        pl.semaphore_signal(
            barrier, inc=1, device_id={"ctx": lax.rem(me + k, 16)}, device_id_type=MESH_ID
        )

    @pl.loop(1, 8)
    def _(k):
        pl.semaphore_signal(
            barrier, inc=1, device_id={"grp": lax.rem(grp + k, 8)}, device_id_type=MESH_ID
        )

    pl.semaphore_wait(barrier, 22)


def remote(src, dst, send_sem, recv_sem, where):
    return pltpu.make_async_remote_copy(
        src_ref=src,
        dst_ref=dst,
        send_sem=send_sem,
        recv_sem=recv_sem,
        device_id=where,
        device_id_type=MESH_ID,
    )


def pick_two(rows_ref, there):
    rows = lax.broadcasted_iota(jnp.int32, (96, 512), 0) + there * 96
    return jnp.where(rows == rows_ref[0:1, :], 1.0, 0.0).astype(jnp.bfloat16)


def pick_both(rows_ref, there):
    rows = lax.broadcasted_iota(jnp.int32, (96, 256), 0) + there * 96
    hit = (rows == rows_ref[0:1, 0:256]) | (rows == rows_ref[0:1, 256:512])
    return jnp.where(hit, 1.0, 0.0).astype(jnp.bfloat16)


def grp_device(dy, dz):
    grp = lax.axis_index("grp")
    there = lax.rem(grp // 4 + dy, 2) * 4 + lax.rem(lax.rem(grp, 4) + dz, 4)
    return {"grp": there}


class GrpSum:
    def __init__(self, cut, part, recv, send_sem, recv_sem):
        self.cut, self.part, self.recv = cut, part, recv
        self.send_sem, self.recv_sem = send_sem, recv_sem
        self.head, self.rest = pl.ds(0, cut), pl.ds(cut, 192 - cut)

    def halves(self, group):
        start, size = (0, self.cut) if group == 2 else (self.cut, 192 - self.cut)
        low = size // 32 * 16
        return (start, low), (start + low, size - low)

    def make(self, number, src, slot, rows, where):
        return remote(
            src,
            self.recv.at[slot, rows],
            self.send_sem.at[number],
            self.recv_sem.at[number],
            where,
        )

    def partner_head(self, dz):
        return self.make(dz, self.part.at[1, dz, self.head], dz, self.head, grp_device(1, 0))

    def partner_rest(self):
        return self.make(22, self.part.at[1, 0, self.rest], 13, self.rest, grp_device(1, 0))

    def along(self, group, kind):
        dy, base = (0 if group == 2 else group), 4 + 3 * group
        low, high = [pl.ds(*half) for half in self.halves(group)]
        dz, rows, slot, to = [
            (2, low, base, 1),
            (2, high, base, 3),
            (1, high, base + 1, 1),
            (3, low, base + 2, 3),
            (1, low, base + 1, 1),
            (3, high, base + 2, 3),
        ][kind]
        number = 4 + 6 * group + kind
        return self.make(number, self.part.at[dy, dz, rows], slot, rows, grp_device(0, to))

    def start_along(self, group, dz):
        for kind in {0: [], 1: [2], 2: [0, 1], 3: [3]}[dz]:
            self.along(group, kind).start()

    def send_first(self, dy, dz):
        if dy == 1:
            self.partner_head(dz).start()
        self.start_along(dy, dz)

    def add(self, target, start, size, slots, out=None):
        def keep(rows, total):
            self.part[target[0], target[1], rows, :] = total.astype(jnp.bfloat16)

        @pl.loop(0, size // 16)
        def _(step):
            rows = pl.ds(pl.multiple_of(start + step * 16, 16), 16)
            total = self.part[target[0], target[1], rows, :].astype(jnp.float32)
            for slot in slots:
                total += self.recv[slot, rows, :].astype(jnp.float32)
            (out or keep)(rows, total)

    def relay(self, group):
        dy, base = (0 if group == 2 else group), 4 + 3 * group
        low, high = self.halves(group)
        self.along(group, 0).wait_recv()
        self.add((dy, 1), *low, [base])
        self.along(group, 4).start()
        self.along(group, 1).wait_recv()
        self.add((dy, 3), *high, [base])
        self.along(group, 5).start()

    def second(self, dz):
        self.partner_head(dz).wait_recv()
        self.add((0, dz), 0, self.cut, [dz])
        self.start_along(2, dz)

    def wait_along(self, group):
        for kind in range(2, 6):
            self.along(group, kind).wait_recv()

    def second_rest(self):
        self.wait_along(1)
        self.add((1, 0), self.cut, 192 - self.cut, [8, 9])
        self.partner_rest().start()

    def finish_head(self, out):
        self.partner_head(0).wait_recv()
        self.wait_along(2)
        self.add((0, 0), 0, self.cut, [0, 11, 12], out)

    def finish_rest(self, out):
        self.wait_along(0)
        self.partner_rest().wait_recv()
        self.add((0, 0), self.cut, 192 - self.cut, [5, 6, 13], out)

    def drain(self):
        for dz in range(4):
            self.partner_head(dz).wait_send()
        for group in range(3):
            for kind in range(6):
                self.along(group, kind).wait_send()
        self.partner_rest().wait_send()


class GrpGather:
    def __init__(self, cut, full, send_sem, recv_sem):
        self.cut, self.full, self.send_sem, self.recv_sem = cut, full, send_sem, recv_sem
        self.head, self.rest = pl.ds(0, cut), pl.ds(cut, 192 - cut)
        self.waited = set()

    def make(self, number, src, dst, rows, where):
        return remote(
            self.full.at[src[0], src[1], rows],
            self.full.at[dst[0], dst[1], rows],
            self.send_sem.at[number],
            self.recv_sem.at[number],
            where,
        )

    def copy(self, number):
        if number < 12:
            group, kind = number // 4, number % 4
            dy = 1 if group == 2 else 0
            start, size = (0, self.cut) if group == 0 else (self.cut, 192 - self.cut)
            low = size // 32 * 16
            src, dst, rows, to = [
                (0, 3, (start, size), 1),
                (0, 1, (start, size), 3),
                (3, 2, (start, low), 1),
                (1, 2, (start + low, size - low), 3),
            ][kind]
            return self.make(number, (dy, src), (dy, dst), pl.ds(*rows), grp_device(0, to))
        if number < 16:
            dz = number - 12
            return self.make(number, (0, dz), (1, dz), self.head, grp_device(1, 0))
        return self.make(number, (0, 0), (1, 0), self.rest, grp_device(1, 0))

    def start(self, *numbers):
        for number in numbers:
            self.copy(number).start()

    def wait(self, *numbers):
        for number in numbers:
            if number not in self.waited:
                self.waited.add(number)
                self.copy(number).wait_recv()

    def send_own(self):
        self.start(16, 0, 1, 12, 4, 5)

    def relay(self, group):
        for kind in range(2):
            self.wait(4 * group + kind)
            self.start(4 * group + 2 + kind)

    def pass_head(self, dz):
        self.wait(*{1: [1], 2: [2, 3], 3: [0]}[dz])
        self.start(12 + dz)

    def pass_rest(self):
        self.wait(16)
        self.start(8, 9)

    def wait_chunk(self, dy, dz):
        self.wait(*[4 + 4 * dy + kind for kind in {0: [], 1: [1], 2: [2, 3], 3: [0]}[dz]])
        if dy == 1:
            self.wait(12 + dz, 16)

    def drain(self):
        for number in range(17):
            self.copy(number).wait_send()


def chunk_of(dy, dz):
    grp = lax.axis_index("grp")
    return lax.rem(grp // 4 + dy, 2), lax.rem(lax.rem(grp, 4) + dz, 4) * 4


def chunk_rows(ref, dy, dz):
    expert, first = chunk_of(dy, dz)
    rows = ref[pl.ds(first, 4), pl.ds(pl.multiple_of(expert * 48, 16), 48), :]
    return rows.reshape(192, 512)


CHUNK_ORDER = [(1, 2), (1, 1), (1, 3), (0, 2), (1, 0), (0, 1), (0, 3), (0, 0)]


def return_rows(rows, dy, dz, send, recv, send_sem, recv_sem):
    me = lax.axis_index("ctx")
    expert, first = chunk_of(dy, dz)
    send[expert, pl.ds(first, 4)] = rows.reshape(4, 48, 512)

    @pl.loop(0, 4)
    def _(i):
        there = first + i

        @pl.when(there != me)
        def _():
            return_copy(expert, there, me, there, send, recv, send_sem, recv_sem).start()


def return_copy(expert, there, mine, partner, send, recv, send_sem, recv_sem):
    return remote(
        send.at[expert, there],
        recv.at[mine, expert],
        send_sem.at[expert, there],
        recv_sem.at[expert, mine],
        {"ctx": partner},
    )


def wait_returns(send, recv, send_sem, recv_sem):
    me = lax.axis_index("ctx")
    for expert in range(2):
        recv[me, expert] = send[expert, me]

        @pl.loop(1, 16)
        def _(k):
            source = lax.rem(me + k, 16)
            copy = return_copy(
                expert, source, source, source, send, recv, send_sem, recv_sem
            )
            copy.wait_recv()
            copy.wait_send()


def experts_kernel(
    x_ref, act_grad_ref, w_in_hbm,
    act_ref, rg_ref, w_in_grad_ref,
    part, sums, full, rg_send, w_in_ref, w_sem,
    s_send_sem, s_recv_sem, f_send_sem, f_recv_sem, r_send_sem, r_recv_sem,
):
    bf = jnp.bfloat16
    w_copy = pltpu.make_async_copy(w_in_hbm, w_in_ref, w_sem)
    w_copy.start()
    greet()
    w_copy.wait()
    summing = GrpSum(96, part, sums, s_send_sem, s_recv_sem)
    gathering = GrpGather(64, full, f_send_sem, f_recv_sem)
    for dy, dz in CHUNK_ORDER:
        expert, _ = chunk_of(dy, dz)
        rows = chunk_rows(x_ref, dy, dz)

        @pl.loop(0, 3)
        def _(piece):
            cols = pl.ds(pl.multiple_of(piece * 512, 512), 512)
            part[dy, dz, :, cols] = dot_nn(rows, w_in_ref[expert, :, cols]).astype(bf)

        summing.send_first(dy, dz)
    summing.relay(1)
    summing.relay(0)
    for dz in (2, 1):
        summing.second(dz)
    summing.second_rest()
    summing.second(3)
    summing.relay(2)

    def activate(rows, pre):
        act_ref[rows, :] = gelu_tanh(pre).astype(bf)
        full[0, 0, rows, :] = (act_grad_ref[rows, :] * gelu_slope(pre)).astype(bf)

    summing.finish_head(activate)
    gathering.start(0, 1, 12)
    summing.finish_rest(activate)
    gathering.start(16, 4, 5)

    def row_grads(dy, dz):
        expert, _ = chunk_of(dy, dz)
        rows = dot_nt(full[dy, dz], w_in_ref[expert]).astype(bf)
        return_rows(rows, dy, dz, rg_send, rg_ref, r_send_sem, r_recv_sem)

    row_grads(0, 0)
    gathering.relay(0)
    for dz in (3, 1):
        gathering.pass_head(dz)
    gathering.pass_rest()
    gathering.relay(1)
    gathering.pass_head(2)
    for dy, dz in [(0, 1), (0, 3)]:
        gathering.wait_chunk(dy, dz)
        row_grads(dy, dz)
    gathering.relay(2)
    for dy, dz in [(1, 0), (1, 1), (1, 3), (0, 2), (1, 2)]:
        gathering.wait_chunk(dy, dz)
        row_grads(dy, dz)
    for dy in range(2):
        expert, _ = chunk_of(dy, 0)

        @pl.loop(0, 3)
        def _(piece):
            cols = pl.ds(pl.multiple_of(piece * 512, 512), 512)
            total = dot_tn(chunk_rows(x_ref, dy, 0), full[dy, 0, :, cols])
            for dz in range(1, 4):
                total += dot_tn(chunk_rows(x_ref, dy, dz), full[dy, dz, :, cols])
            w_in_grad_ref[expert, :, cols] = total.astype(bf)

    wait_returns(rg_send, rg_ref, r_send_sem, r_recv_sem)
    summing.drain()
    gathering.drain()


def experts_call(x_rows, act_grad, w_in):
    bf = jnp.bfloat16
    vmem = pl.BlockSpec(memory_space=pltpu.VMEM)
    shape = jax.ShapeDtypeStruct
    return pl.pallas_call(
        experts_kernel,
        out_shape=(
            shape((192, 1536), bf),
            shape((16, 2, 48, 512), bf),
            shape((2, 512, 1536), bf),
        ),
        in_specs=[vmem] * 2 + [pl.BlockSpec(memory_space=pl.ANY)],
        out_specs=(vmem,) * 3,
        scratch_shapes=[
            pltpu.VMEM((2, 4, 192, 1536), bf),
            pltpu.VMEM((14, 192, 1536), bf),
            pltpu.VMEM((2, 4, 192, 1536), bf),
            pltpu.VMEM((2, 16, 48, 512), bf),
            pltpu.VMEM((2, 512, 1536), bf),
            pltpu.SemaphoreType.DMA,
            pltpu.SemaphoreType.DMA((23,)),
            pltpu.SemaphoreType.DMA((23,)),
            pltpu.SemaphoreType.DMA((17,)),
            pltpu.SemaphoreType.DMA((17,)),
            pltpu.SemaphoreType.DMA((2, 16)),
            pltpu.SemaphoreType.DMA((2, 16)),
        ],
        compiler_params=pltpu.CompilerParams(
            collective_id=2, has_side_effects=True, vmem_limit_bytes=56 * 2**20
        ),
        name="experts",
    )(x_rows, act_grad, w_in)


def turn(row):
    return jnp.transpose(jnp.broadcast_to(row, (128, 256)))


def forward_kernel(
    q_ref, k_ref, v_ref, res_ref, lengths_ref, routes_ref, gates_ref, og_ref, w_out_hbm,
    rows_ref, rows_col_ref, qend_row_ref, attn_ref, lse_ref, mixed_ref, inv_ref, xrecv_ref, grecv_ref, act_grad_ref, kv_out_ref,
    kv, m_s, l_s, acc_s, gsend, xsend, part, sums, sq_send, sq_recv, gated, qend_s, w_out_ref,
    w_sem,
    kv_send_sem, kv_recv_sem, out_sem, g_send_sem, g_recv_sem, x_send_sem, x_recv_sem,
    p_send_sem, p_recv_sem, sq_send_sem, sq_recv_sem,
):
    me = lax.axis_index("ctx")
    grp = lax.axis_index("grp")
    core = lax.rem(me, 2)
    chip = me // 2
    x = lax.rem(chip, 4)
    yh = chip // 4

    def device(dy, dx, dc):
        there = lax.rem(yh + dy, 2) * 4 + lax.rem(x + dx, 4)
        return {"ctx": there * 2 + lax.rem(core + dc, 2)}

    w_copy = pltpu.make_async_copy(w_out_hbm, w_out_ref, w_sem)
    w_copy.start()
    greet()

    copies = {}
    sent = []

    def move(src, slot, where):
        copy = remote(src, kv.at[slot], kv_send_sem.at[len(sent)], kv_recv_sem.at[slot], where)
        copy.start()
        copies[slot] = copy
        sent.append(copy)

    def own(which):
        return k_ref if which == 0 else v_ref

    right, left = device(0, 1, 0), device(0, 3, 0)
    sibling, partner = device(0, 0, 1), device(1, 0, 0)
    early = lax.broadcasted_iota(jnp.int32, (256, 256), 0) < lax.broadcasted_iota(
        jnp.int32, (256, 256), 1
    )
    experts = [routes_ref[a : a + 1, :].astype(jnp.float32) for a in range(2)]
    for a in range(2):
        rank = jnp.zeros((1, 256), jnp.float32)
        for b in range(2):
            same = early & (turn(experts[b])[:, 0:1] == experts[a])
            rank += jnp.sum(jnp.where(same, 1.0, 0.0), axis=0, keepdims=True)
        cols = slice(a * 256, a * 256 + 256)
        rows = experts[a] * 48 + rank
        rows_ref[:, cols] = jnp.broadcast_to(rows, (8, 256)).astype(jnp.int32)
        rows_col_ref[:, a * 128 : a * 128 + 128] = turn(rows).astype(jnp.int32)
        gate = turn(gates_ref[a : a + 1, :])[:, 0:1]
        gated[cols, :] = (gate * og_ref[...].astype(jnp.float32)).astype(jnp.bfloat16)

    @pl.loop(0, 16)
    def _(k):
        there = lax.rem(me + k, 16)
        gsend[k] = dot_nn(pick_two(rows_ref, there), gated[...]).astype(jnp.bfloat16)

        @pl.when(k > 0)
        def _():
            remote(
                gsend.at[k], grecv_ref.at[me], g_send_sem.at[k], g_recv_sem.at[k], {"ctx": there}
            ).start()

    for which in range(2):
        move(own(which), (0, 0, 1, which), sibling)
    for which in range(2):
        move(own(which), (1, 0, 0, which), partner)
        move(own(which), (0, 3, 0, which), right)
        move(own(which), (0, 1, 0, which), left)
    grecv_ref[me] = gsend[0]
    kv[0, 0, 0, 0] = k_ref[...]
    kv[0, 0, 0, 1] = v_ref[...]
    pos_col = me * 256 + lax.broadcasted_iota(jnp.int32, (256, 128), 0)
    pos_row = me * 256 + lax.broadcasted_iota(jnp.int32, (8, 256), 1)
    ends_col, ends_row = jnp.full_like(pos_col, 4096), jnp.full_like(pos_row, 4096)
    end = jnp.int32(0)
    for f in range(16):
        end = end + lengths_ref[f]
        ends_col = jnp.minimum(ends_col, jnp.where(end > pos_col, end, 4096))
        ends_row = jnp.minimum(ends_row, jnp.where(end > pos_row, end, 4096))
    qend_s[...] = ends_col
    qend_row_ref[...] = ends_row
    summing = GrpSum(96, part, sums, p_send_sem, p_recv_sem)
    m_s[...] = jnp.full_like(m_s, LOW)
    l_s[...] = jnp.zeros_like(l_s)
    acc_s[...] = jnp.zeros_like(acc_s)
    outs = []

    def wait_slot(dy, dx, dc, which):
        copies[(dy, dx, dc, which)].wait_recv()

    def forward(dy, dx, which):
        wait_slot(dy, dx, 0, which)
        move(kv.at[dy, dx, 0, which], (dy, dx, 1, which), sibling)

    def relay(dy):
        forward(dy, 3, 0)
        move(kv.at[dy, 3, 0, 0], (dy, 2, 0, 0), right)
        forward(dy, 1, 1)
        move(kv.at[dy, 1, 0, 1], (dy, 2, 0, 1), left)
        forward(dy, 3, 1)
        forward(dy, 1, 0)

    def attend(dy, dx):
        for which in range(2):
            wait_slot(dy, dx, 1, which)
        copy = pltpu.make_async_copy(kv.at[dy, dx], kv_out_ref.at[dy, dx], out_sem.at[dy, dx])
        copy.start()
        outs.append(copy)
        there = lax.rem(yh + dy, 2) * 4 + lax.rem(x + dx, 4)
        lane = lax.broadcasted_iota(jnp.int32, (256, 256), 1)
        qend = qend_s[:, 0:1]
        limits = [qend - (there * 512 + lax.rem(core + dc, 2) * 256) for dc in range(2)]

        @pl.loop(0, 4)
        def _(h):
            cols = pl.ds(pl.multiple_of(h * 128, 128), 128)
            qh = q_ref[:, cols]
            scores = []
            for dc in range(2):
                s = dot_nt(qh, kv[dy, dx, dc, 0, :, cols]) * (LOG2E * HEAD_DIM**-0.5)
                scores.append(jnp.where(lane < limits[dc], s, LOW))
            top = jnp.max(jnp.maximum(scores[0], scores[1]), axis=1, keepdims=True)
            m_old = m_s[h]
            m_new = jnp.maximum(m_old, top)
            alpha = jnp.exp2(m_old - m_new)
            probs = [jnp.exp2(s - m_new[:, 0:1]) for s in scores]
            total = jnp.sum(probs[0] + probs[1], axis=1, keepdims=True)
            m_s[h] = m_new
            l_s[h] = l_s[h] * alpha + total
            acc = acc_s[h] * alpha
            for dc in range(2):
                acc += dot_nn(probs[dc].astype(jnp.bfloat16), kv[dy, dx, dc, 1, :, cols])
            acc_s[h] = acc

    attend(0, 0)

    @pl.loop(1, 16)
    def _(k):
        source = lax.rem(me + 16 - k, 16)
        remote(
            gsend.at[k], grecv_ref.at[source], g_send_sem.at[k], g_recv_sem.at[k], {"ctx": source}
        ).wait_recv()

    w_copy.wait()
    for dy, dz in CHUNK_ORDER:
        expert, _ = chunk_of(dy, dz)
        rows = chunk_rows(grecv_ref, dy, dz)

        @pl.loop(0, 3)
        def _(piece):
            cols = pl.ds(pl.multiple_of(piece * 512, 512), 512)
            part[dy, dz, :, cols] = dot_nt(rows, w_out_ref[expert, cols, :]).astype(jnp.bfloat16)

        summing.send_first(dy, dz)

    for which in range(2):
        wait_slot(1, 0, 0, which)
        move(kv.at[1, 0, 0, which], (1, 3, 0, which), right)
        move(kv.at[1, 0, 0, which], (1, 1, 0, which), left)
        move(kv.at[1, 0, 0, which], (1, 0, 1, which), sibling)
    relay(0)
    attend(0, 3)
    attend(0, 1)
    relay(1)
    summing.relay(1)
    summing.relay(0)
    attend(1, 0)
    for which in range(2):
        forward(0, 2, which)
    attend(0, 2)
    for dz in (2, 1, 3):
        summing.second(dz)
    attend(1, 3)
    attend(1, 1)
    summing.relay(2)
    for which in range(2):
        forward(1, 2, which)
    attend(1, 2)

    squares = jnp.zeros((256, 1), jnp.float32)
    for h in range(4):
        cols = slice(h * 128, h * 128 + 128)
        out = (acc_s[h] / l_s[h]).astype(jnp.bfloat16)
        lse_ref[h] = jnp.transpose(m_s[h] + jnp.log2(l_s[h]))[0:8]
        attn_ref[:, cols] = out
        mixed = (res_ref[:, cols].astype(jnp.float32) + out.astype(jnp.float32)).astype(
            jnp.bfloat16
        )
        mixed_ref[:, cols] = mixed
        mixed_f = mixed.astype(jnp.float32)
        squares += jnp.sum(mixed_f * mixed_f, axis=1, keepdims=True)
    turned = jnp.transpose(jnp.broadcast_to(squares, (256, 128)))
    sq_send[...] = turned[0:8]
    sq_recv[grp] = turned[0:8]

    @pl.loop(1, 8)
    def _(k):
        there = lax.rem(grp + k, 8)
        remote(
            sq_send, sq_recv.at[grp], sq_send_sem.at[k], sq_recv_sem.at[k], {"grp": there}
        ).start()

    @pl.loop(1, 8)
    def _(k):
        source = lax.rem(grp + 8 - k, 8)
        copy = remote(
            sq_send, sq_recv.at[source], sq_send_sem.at[k], sq_recv_sem.at[k], {"grp": source}
        )
        copy.wait_recv()
        copy.wait_send()

    total = sq_recv[0]
    for k in range(1, 8):
        total = total + sq_recv[k]
    inv = lax.rsqrt(total / 4096 + 1e-06)
    inv = jnp.transpose(jnp.concatenate([inv] * 16, axis=0))
    inv_ref[...] = inv
    normed = jnp.concatenate(
        [
            (mixed_ref[:, h * 128 : h * 128 + 128].astype(jnp.float32) * inv).astype(jnp.bfloat16)
            for h in range(4)
        ],
        axis=1,
    )

    @pl.loop(0, 16)
    def _(k):
        there = lax.rem(me + k, 16)
        xsend[k] = dot_nn(pick_both(rows_ref, there), normed).astype(jnp.bfloat16)

        @pl.when(k > 0)
        def _():
            remote(
                xsend.at[k], xrecv_ref.at[me], x_send_sem.at[k], x_recv_sem.at[k], {"ctx": there}
            ).start()

    xrecv_ref[me] = xsend[0]

    summing.second_rest()

    def keep(rows, total):
        act_grad_ref[rows, :] = total

    summing.finish_head(keep)
    summing.finish_rest(keep)
    summing.drain()

    @pl.loop(1, 16)
    def _(k):
        source = lax.rem(me + 16 - k, 16)
        copy = remote(
            gsend.at[k], grecv_ref.at[source], g_send_sem.at[k], g_recv_sem.at[k], {"ctx": source}
        )
        copy.wait_send()
        copy = remote(
            xsend.at[k], xrecv_ref.at[source], x_send_sem.at[k], x_recv_sem.at[k], {"ctx": source}
        )
        copy.wait_recv()
        copy.wait_send()

    for copy in sent:
        copy.wait_send()
    for copy in outs:
        copy.wait()


def forward_call(*operands):
    bf, f32 = jnp.bfloat16, jnp.float32
    vmem = pl.BlockSpec(memory_space=pltpu.VMEM)
    shape = jax.ShapeDtypeStruct
    return pl.pallas_call(
        forward_kernel,
        out_shape=(
            shape((8, 512), jnp.int32),
            shape((256, 256), jnp.int32),
            shape((8, 256), jnp.int32),
            shape((256, 512), bf),
            shape((4, 8, 256), f32),
            shape((256, 512), bf),
            shape((256, 128), f32),
            shape((16, 96, 512), bf),
            shape((16, 96, 512), bf),
            shape((192, 1536), f32),
            shape((2, 4, 2, 2, 256, 512), bf),
        ),
        in_specs=[vmem] * 4
        + [pl.BlockSpec(memory_space=pltpu.SMEM)]
        + [vmem] * 3
        + [pl.BlockSpec(memory_space=pl.ANY)],
        out_specs=[vmem] * 10 + [pl.BlockSpec(memory_space=pl.ANY)],
        scratch_shapes=[
            pltpu.VMEM((2, 4, 2, 2, 256, 512), bf),
            pltpu.VMEM((4, 256, 128), f32),
            pltpu.VMEM((4, 256, 128), f32),
            pltpu.VMEM((4, 256, 128), f32),
            pltpu.VMEM((16, 96, 512), bf),
            pltpu.VMEM((16, 96, 512), bf),
            pltpu.VMEM((2, 4, 192, 1536), bf),
            pltpu.VMEM((14, 192, 1536), bf),
            pltpu.VMEM((8, 256), f32),
            pltpu.VMEM((8, 8, 256), f32),
            pltpu.VMEM((512, 512), bf),
            pltpu.VMEM((256, 128), jnp.int32),
            pltpu.VMEM((2, 1536, 512), bf),
            pltpu.SemaphoreType.DMA,
            pltpu.SemaphoreType.DMA((30,)),
            pltpu.SemaphoreType.DMA((2, 4, 2, 2)),
            pltpu.SemaphoreType.DMA((2, 4)),
            pltpu.SemaphoreType.DMA((16,)),
            pltpu.SemaphoreType.DMA((16,)),
            pltpu.SemaphoreType.DMA((16,)),
            pltpu.SemaphoreType.DMA((16,)),
            pltpu.SemaphoreType.DMA((23,)),
            pltpu.SemaphoreType.DMA((23,)),
            pltpu.SemaphoreType.DMA((8,)),
            pltpu.SemaphoreType.DMA((8,)),
        ],
        compiler_params=pltpu.CompilerParams(
            collective_id=0, has_side_effects=True, vmem_limit_bytes=56 * 2**20
        ),
        name="forward",
    )(*operands)


TERM_ORDER = [(1, 3), (1, 1), (1, 2), (1, 0), (0, 3), (0, 1), (0, 2), (0, 0)]


def backward_kernel(
    q_ref, kv_hbm, lse_ref, attn_ref, qend_ref, og_ref, inv_ref, rows_ref, rg_ref, act_ref,
    w_out_hbm, g_hbm, mixed_ref, gates_ref,
    layer_ref, ig_ref, dq_ref, dk_ref, dv_ref, w_out_grad_ref,
    full, eo_send, eo_recv, kv_ref, w_out_ref, g_ref, load_sem, normed_grad, row_dot, dqt, own_terms, sib_send, sib_recv, ring_send,
    ring_recv, part_send, part_recv,
    f_send_sem, f_recv_sem, r_send_sem, r_recv_sem, sib_send_sem, sib_recv_sem, ring_send_sem, ring_recv_sem,
    part_send_sem, part_recv_sem,
):
    me = lax.axis_index("ctx")
    core = lax.rem(me, 2)
    chip = me // 2
    x = lax.rem(chip, 4)
    yh = chip // 4
    bf, f32 = jnp.bfloat16, jnp.float32

    def device(dy, dx, dc):
        there = lax.rem(yh + dy, 2) * 4 + lax.rem(x + dx, 4)
        return {"ctx": there * 2 + lax.rem(core + dc, 2)}

    right, left = device(0, 1, 0), device(0, 3, 0)
    sibling, partner = device(0, 0, 1), device(1, 0, 0)
    loads = {}
    for dy, dx in TERM_ORDER:
        loads[(dy, dx)] = pltpu.make_async_copy(
            kv_hbm.at[dy, dx], kv_ref.at[dy, dx], load_sem.at[dy * 4 + dx]
        )
    w_load = pltpu.make_async_copy(w_out_hbm, w_out_ref, load_sem.at[8])
    g_load = pltpu.make_async_copy(g_hbm, g_ref, load_sem.at[9])
    loads[(1, 3)].start()
    loads[(1, 1)].start()
    greet()
    gathering = GrpGather(64, full, f_send_sem, f_recv_sem)
    full[0, 0] = act_ref[...]
    gathering.send_own()
    for dy, dx in TERM_ORDER[2:]:
        loads[(dy, dx)].start()
    w_load.start()
    g_load.start()
    dqt[...] = jnp.zeros_like(dqt)
    row_id = lax.broadcasted_iota(jnp.int32, (256, 1536), 1)
    hits = [row_id == rows_ref[:, a * 128 : a * 128 + 1] for a in range(2)]
    pick = jnp.where(hits[0] | hits[1], 1.0, 0.0).astype(bf)
    normed_grad[...] = dot_nn(pick, rg_ref[...].reshape(1536, 512))

    for h in range(4):
        cols = slice(h * 128, h * 128 + 128)
        grad = og_ref[:, cols].astype(f32) + inv_ref[...] * normed_grad[:, cols]
        grad = grad.astype(bf)
        ig_ref[:, cols] = grad
        dots = jnp.sum(grad.astype(f32) * attn_ref[:, cols].astype(f32), axis=1, keepdims=True)
        row_dot[h] = jnp.transpose(jnp.broadcast_to(dots, (256, 128)))[0:8]

    scale = HEAD_DIM**-0.5

    def terms(dy, dx):
        loads[(dy, dx)].wait()
        there = lax.rem(yh + dy, 2) * 4 + lax.rem(x + dx, 4)
        sub = lax.broadcasted_iota(jnp.int32, (256, 256), 0)
        qend = qend_ref[0:1, :]
        limits = [qend - (there * 512 + lax.rem(core + dc, 2) * 256) for dc in range(2)]

        @pl.loop(0, 4)
        def _(h):
            cols = pl.ds(pl.multiple_of(h * 128, 128), 128)
            qh = q_ref[:, cols]
            gh = ig_ref[:, cols]
            lse = lse_ref[h][0:1, :]
            dots = row_dot[h][0:1, :]
            for dc in range(2):
                kh = kv_ref[dy, dx, dc, 0, :, cols]
                vh = kv_ref[dy, dx, dc, 1, :, cols]
                s = dot_nt(kh, qh) * (LOG2E * scale)
                p = jnp.exp2(jnp.where(sub < limits[dc], s, LOW) - lse)
                dp = dot_nt(vh, gh)
                ds = (p * (dp - dots) * scale).astype(bf)
                dk = dot_nn(ds, qh).astype(bf)
                dv = dot_nn(p.astype(bf), gh).astype(bf)
                dqt[h] += dot_tn(kh, ds)
                to = own_terms if dc == 0 else sib_send
                to[dy, dx, 0, :, cols] = dk
                to[dy, dx, 1, :, cols] = dv

        for which in range(2):
            sib_copy(dy, dx, which).start()

    def sib_copy(dy, dx, which):
        return remote(
            sib_send.at[dy, dx, which],
            sib_recv.at[dy, dx, which],
            sib_send_sem.at[dy, dx, which],
            sib_recv_sem.at[dy, dx, which],
            sibling,
        )

    def ring_copy(dy, dx, which):
        to = (dx + 3) % 4 if which == 0 else (dx + 1) % 4
        return remote(
            ring_send.at[dy, dx, which],
            ring_recv.at[dy, to, which],
            ring_send_sem.at[dy, dx, which],
            ring_recv_sem.at[dy, to, which],
            right if which == 0 else left,
        )

    def arrival(dy, dx, which):
        return ring_copy(dy, (dx + 1) % 4 if which == 0 else (dx + 3) % 4, which)

    def total_of(dy, dx, which, ring):
        sib_copy(dy, dx, which).wait_recv()
        if ring:
            arrival(dy, dx, which).wait_recv()
        sums = own_terms[dy, dx, which].astype(f32) + sib_recv[dy, dx, which].astype(f32)
        if ring:
            sums = sums + ring_recv[dy, dx, which].astype(f32)
        return sums

    def send_ring(dy, dx, which, ring):
        ring_send[dy, dx, which] = total_of(dy, dx, which, ring).astype(bf)
        ring_copy(dy, dx, which).start()

    def part_copy(which):
        return remote(
            part_send.at[which],
            part_recv.at[which],
            part_send_sem.at[which],
            part_recv_sem.at[which],
            partner,
        )

    def expert_rows(dy, dz):
        expert, _ = chunk_of(dy, dz)
        rows = dot_nn(full[dy, dz], w_out_ref[expert]).astype(bf)
        return_rows(rows, dy, dz, eo_send, eo_recv, r_send_sem, r_recv_sem)

    terms(1, 3)
    terms(1, 1)
    send_ring(1, 3, 0, False)
    send_ring(1, 1, 1, False)
    terms(1, 2)
    terms(1, 0)
    send_ring(1, 2, 0, True)
    send_ring(1, 2, 1, True)
    w_load.wait()
    gathering.relay(0)
    for dz in (3, 1):
        gathering.pass_head(dz)
    gathering.pass_rest()
    gathering.relay(1)
    expert_rows(0, 0)
    terms(0, 3)
    send_ring(1, 1, 0, True)
    send_ring(1, 3, 1, True)
    send_ring(0, 3, 0, False)
    terms(0, 1)
    send_ring(0, 1, 1, False)
    gathering.pass_head(2)
    gathering.relay(2)
    terms(0, 2)
    for which in range(2):
        part_send[which] = total_of(1, 0, which, True).astype(bf)
        part_copy(which).start()
    send_ring(0, 2, 0, True)
    send_ring(0, 2, 1, True)
    terms(0, 0)
    send_ring(0, 1, 0, True)
    send_ring(0, 3, 1, True)
    for dy, dz in [(0, 1), (0, 3), (1, 0)]:
        gathering.wait_chunk(dy, dz)
        expert_rows(dy, dz)
    for h in range(4):
        dq_ref[:, h * 128 : h * 128 + 128] = jnp.transpose(dqt[h]).astype(bf)
    for dy, dz in [(0, 2), (1, 1), (1, 3), (1, 2)]:
        gathering.wait_chunk(dy, dz)
        expert_rows(dy, dz)
    for which in range(2):
        sums = total_of(0, 0, which, True)
        part_copy(which).wait_recv()
        sums = sums + part_recv[which].astype(f32)
        if which == 0:
            dk_ref[...] = sums.astype(bf)
        else:
            dv_ref[...] = sums.astype(bf)

    for dy in range(2):
        for dx in range(4):
            for which in range(2):
                sib_copy(dy, dx, which).wait_send()
                if dx > 0:
                    ring_copy(dy, dx, which).wait_send()
    for which in range(2):
        part_copy(which).wait_send()

    g_load.wait()
    for dy in range(2):
        expert, _ = chunk_of(dy, 0)

        @pl.loop(0, 3)
        def _(piece):
            cols = pl.ds(pl.multiple_of(piece * 512, 512), 512)
            total = dot_tn(full[dy, 0, :, cols], chunk_rows(g_ref, dy, 0))
            for dz in range(1, 4):
                total += dot_tn(full[dy, dz, :, cols], chunk_rows(g_ref, dy, dz))
            w_out_grad_ref[expert, cols, :] = total.astype(bf)

    wait_returns(eo_send, eo_recv, r_send_sem, r_recv_sem)
    total = mixed_ref[...].astype(f32)
    for a in range(2):
        hit = row_id == rows_ref[:, a * 128 : a * 128 + 1]
        picked = dot_nn(jnp.where(hit, 1.0, 0.0).astype(bf), eo_recv[...].reshape(1536, 512))
        total = total + turn(gates_ref[a : a + 1, :])[:, 0:1] * picked
    layer_ref[...] = total.astype(bf)

    gathering.drain()


def backward_call(*operands):
    bf, f32 = jnp.bfloat16, jnp.float32
    vmem = pl.BlockSpec(memory_space=pltpu.VMEM)
    anywhere = pl.BlockSpec(memory_space=pl.ANY)
    shape = jax.ShapeDtypeStruct
    return pl.pallas_call(
        backward_kernel,
        out_shape=(shape((256, 512), bf),) * 5 + (shape((2, 1536, 512), bf),),
        in_specs=[vmem, anywhere] + [vmem] * 8 + [anywhere] * 2 + [vmem] * 2,
        out_specs=(vmem,) * 6,
        scratch_shapes=[
            pltpu.VMEM((2, 4, 192, 1536), bf),
            pltpu.VMEM((2, 16, 48, 512), bf),
            pltpu.VMEM((16, 2, 48, 512), bf),
            pltpu.VMEM((2, 4, 2, 2, 256, 512), bf),
            pltpu.VMEM((2, 1536, 512), bf),
            pltpu.VMEM((16, 96, 512), bf),
            pltpu.SemaphoreType.DMA((10,)),
            pltpu.VMEM((256, 512), f32),
            pltpu.VMEM((4, 8, 256), f32),
            pltpu.VMEM((4, 128, 256), f32),
            pltpu.VMEM((2, 4, 2, 256, 512), bf),
            pltpu.VMEM((2, 4, 2, 256, 512), bf),
            pltpu.VMEM((2, 4, 2, 256, 512), bf),
            pltpu.VMEM((2, 4, 2, 256, 512), bf),
            pltpu.VMEM((2, 4, 2, 256, 512), bf),
            pltpu.VMEM((2, 256, 512), bf),
            pltpu.VMEM((2, 256, 512), bf),
            pltpu.SemaphoreType.DMA((17,)),
            pltpu.SemaphoreType.DMA((17,)),
            pltpu.SemaphoreType.DMA((2, 16)),
            pltpu.SemaphoreType.DMA((2, 16)),
            pltpu.SemaphoreType.DMA((2, 4, 2)),
            pltpu.SemaphoreType.DMA((2, 4, 2)),
            pltpu.SemaphoreType.DMA((2, 4, 2)),
            pltpu.SemaphoreType.DMA((2, 4, 2)),
            pltpu.SemaphoreType.DMA((2,)),
            pltpu.SemaphoreType.DMA((2,)),
        ],
        compiler_params=pltpu.CompilerParams(
            collective_id=1, has_side_effects=True, vmem_limit_bytes=56 * 2**20
        ),
        name="backward",
    )(*operands)


def publish_kernel(count, *refs):
    sources, targets, held = refs[:count], refs[count : 2 * count], refs[2 * count : 3 * count]
    in_sem, out_sem = refs[3 * count :]
    reads = [pltpu.make_async_copy(sources[n], held[n], in_sem.at[n]) for n in range(count)]
    writes = [pltpu.make_async_copy(held[n], targets[n], out_sem.at[n]) for n in range(count)]
    for read in reads:
        read.start()
    for read, write in zip(reads, writes):
        read.wait()
        write.start()
    for write in writes:
        write.wait()


def publish(*arrays):
    anywhere = pl.BlockSpec(memory_space=pl.ANY)
    count = len(arrays)
    return pl.pallas_call(
        functools.partial(publish_kernel, count),
        out_shape=tuple(jax.ShapeDtypeStruct(a.shape, a.dtype) for a in arrays),
        in_specs=[anywhere] * count,
        out_specs=(anywhere,) * count,
        scratch_shapes=[pltpu.VMEM(a.shape, a.dtype) for a in arrays]
        + [pltpu.SemaphoreType.DMA((count,))] * 2,
        compiler_params=pltpu.CompilerParams(vmem_limit_bytes=56 * 2**20),
        name="publish",
    )(*arrays)


def shards(
    residual, queries, keys, values, frame_lengths, routes, route_gates, w_in, w_out, out_grad
):
    n_ctx = lax.axis_size("ctx")
    tok_rows, feat_dev = residual.shape
    exp_dev = w_in.shape[0]
    rows_wide, rows_col, qend_row, attn, lse, mixed, inv_wide, rows_recv, grads_recv, act_grad, kv_all = (
        forward_call(
            queries,
            keys,
            values,
            residual,
            frame_lengths,
            routes.T,
            route_gates.T,
            out_grad,
            w_out,
        )
    )
    activated, row_grad, w_in_grad = experts_call(rows_recv, act_grad, w_in)
    layer_out, input_grad, query_grad, key_grad, value_grad, w_out_grad = backward_call(
        queries,
        kv_all,
        lse,
        attn,
        qend_row,
        out_grad,
        inv_wide,
        rows_col,
        row_grad.reshape(n_ctx, exp_dev * row_grad.shape[2], feat_dev),
        activated,
        w_out,
        grads_recv,
        mixed,
        route_gates.T,
    )
    return publish(
        layer_out,
        input_grad,
        query_grad,
        key_grad,
        value_grad,
        w_in_grad,
        w_out_grad,
    )


def solution(mesh):
    in_specs = (
        P("ctx", "grp"),
        P("ctx", "grp"),
        P("ctx", "grp"),
        P("ctx", "grp"),
        P(),
        P("ctx", None),
        P("ctx", None),
        P("ctx", "grp", None),
        P("ctx", None, "grp"),
        P("ctx", "grp"),
    )
    out_specs = (
        P("ctx", "grp"),
        P("ctx", "grp"),
        P("ctx", "grp"),
        P("ctx", "grp"),
        P("ctx", "grp"),
        P("ctx", "grp", None),
        P("ctx", None, "grp"),
    )
    return jax.shard_map(shards, mesh=mesh, in_specs=in_specs, out_specs=out_specs, check_vma=False)
```

```python
import functools

import jax
import jax.numpy as jnp
from jax import lax
from jax.experimental import pallas as pl
from jax.experimental.pallas import tpu as pltpu
from jax.sharding import PartitionSpec as P

HEAD_DIM = 128


gelu_coef = 0.7978845608028654


def gelu_tanh(field):
    return 0.5 * field * (1.0 + jnp.tanh(gelu_coef * (field + 0.044715 * field * field * field)))


def gelu_slope(field):
    tanh_val = jnp.tanh(gelu_coef * (field + 0.044715 * field * field * field))
    return 0.5 * (1.0 + tanh_val) + 0.5 * field * (1.0 - tanh_val * tanh_val) * gelu_coef * (
        1.0 + 3.0 * 0.044715 * field * field
    )


MESH_ID = pl.DeviceIdType.MESH
LOG2E = 1.4426950408889634
LOW = -1e30


def dot_nt(a, b):
    return lax.dot_general(a, b, (((1,), (1,)), ((), ())), preferred_element_type=jnp.float32)


def dot_tn(a, b):
    return lax.dot_general(a, b, (((0,), (0,)), ((), ())), preferred_element_type=jnp.float32)


def dot_nn(a, b):
    return jnp.dot(a, b, preferred_element_type=jnp.float32)


def greet():
    me = lax.axis_index("ctx")
    grp = lax.axis_index("grp")
    barrier = pltpu.get_barrier_semaphore()

    @pl.loop(1, 16)
    def _(k):
        pl.semaphore_signal(
            barrier, inc=1, device_id={"ctx": lax.rem(me + k, 16)}, device_id_type=MESH_ID
        )

    @pl.loop(1, 8)
    def _(k):
        pl.semaphore_signal(
            barrier, inc=1, device_id={"grp": lax.rem(grp + k, 8)}, device_id_type=MESH_ID
        )

    pl.semaphore_wait(barrier, 22)


def remote(src, dst, send_sem, recv_sem, where):
    return pltpu.make_async_remote_copy(
        src_ref=src,
        dst_ref=dst,
        send_sem=send_sem,
        recv_sem=recv_sem,
        device_id=where,
        device_id_type=MESH_ID,
    )


def pick_two(rows_ref, there):
    rows = lax.broadcasted_iota(jnp.int32, (96, 512), 0) + there * 96
    return jnp.where(rows == rows_ref[0:1, :], 1.0, 0.0).astype(jnp.bfloat16)


def pick_both(rows_ref, there):
    rows = lax.broadcasted_iota(jnp.int32, (96, 256), 0) + there * 96
    hit = (rows == rows_ref[0:1, 0:256]) | (rows == rows_ref[0:1, 256:512])
    return jnp.where(hit, 1.0, 0.0).astype(jnp.bfloat16)


def grp_device(dy, dz):
    grp = lax.axis_index("grp")
    there = lax.rem(grp // 4 + dy, 2) * 4 + lax.rem(lax.rem(grp, 4) + dz, 4)
    return {"grp": there}


class GrpSum:
    def __init__(self, cut, part, recv, send_sem, recv_sem):
        self.cut, self.part, self.recv = cut, part, recv
        self.send_sem, self.recv_sem = send_sem, recv_sem
        self.head, self.rest = pl.ds(0, cut), pl.ds(cut, 192 - cut)

    def halves(self, group):
        start, size = (0, self.cut) if group == 2 else (self.cut, 192 - self.cut)
        low = size // 32 * 16
        return (start, low), (start + low, size - low)

    def make(self, number, src, slot, rows, where):
        return remote(
            src,
            self.recv.at[slot, rows],
            self.send_sem.at[number],
            self.recv_sem.at[number],
            where,
        )

    def partner_head(self, dz):
        return self.make(dz, self.part.at[1, dz, self.head], dz, self.head, grp_device(1, 0))

    def partner_rest(self):
        return self.make(22, self.part.at[1, 0, self.rest], 13, self.rest, grp_device(1, 0))

    def along(self, group, kind):
        dy, base = (0 if group == 2 else group), 4 + 3 * group
        low, high = [pl.ds(*half) for half in self.halves(group)]
        dz, rows, slot, to = [
            (2, low, base, 1),
            (2, high, base, 3),
            (1, high, base + 1, 1),
            (3, low, base + 2, 3),
            (1, low, base + 1, 1),
            (3, high, base + 2, 3),
        ][kind]
        number = 4 + 6 * group + kind
        return self.make(number, self.part.at[dy, dz, rows], slot, rows, grp_device(0, to))

    def start_along(self, group, dz):
        for kind in {0: [], 1: [2], 2: [0, 1], 3: [3]}[dz]:
            self.along(group, kind).start()

    def send_first(self, dy, dz):
        if dy == 1:
            self.partner_head(dz).start()
        self.start_along(dy, dz)

    def add(self, target, start, size, slots, out=None):
        def keep(rows, total):
            self.part[target[0], target[1], rows, :] = total.astype(jnp.bfloat16)

        @pl.loop(0, size // 16)
        def _(step):
            rows = pl.ds(pl.multiple_of(start + step * 16, 16), 16)
            total = self.part[target[0], target[1], rows, :].astype(jnp.float32)
            for slot in slots:
                total += self.recv[slot, rows, :].astype(jnp.float32)
            (out or keep)(rows, total)

    def relay(self, group):
        dy, base = (0 if group == 2 else group), 4 + 3 * group
        low, high = self.halves(group)
        self.along(group, 0).wait_recv()
        self.add((dy, 1), *low, [base])
        self.along(group, 4).start()
        self.along(group, 1).wait_recv()
        self.add((dy, 3), *high, [base])
        self.along(group, 5).start()

    def second(self, dz):
        self.partner_head(dz).wait_recv()
        self.add((0, dz), 0, self.cut, [dz])
        self.start_along(2, dz)

    def wait_along(self, group):
        for kind in range(2, 6):
            self.along(group, kind).wait_recv()

    def second_rest(self):
        self.wait_along(1)
        self.add((1, 0), self.cut, 192 - self.cut, [8, 9])
        self.partner_rest().start()

    def finish_head(self, out):
        self.partner_head(0).wait_recv()
        self.wait_along(2)
        self.add((0, 0), 0, self.cut, [0, 11, 12], out)

    def finish_rest(self, out):
        self.wait_along(0)
        self.partner_rest().wait_recv()
        self.add((0, 0), self.cut, 192 - self.cut, [5, 6, 13], out)

    def drain(self):
        for dz in range(4):
            self.partner_head(dz).wait_send()
        for group in range(3):
            for kind in range(6):
                self.along(group, kind).wait_send()
        self.partner_rest().wait_send()


class GrpGather:
    def __init__(self, cut, full, send_sem, recv_sem):
        self.cut, self.full, self.send_sem, self.recv_sem = cut, full, send_sem, recv_sem
        self.head, self.rest = pl.ds(0, cut), pl.ds(cut, 192 - cut)
        self.waited = set()

    def make(self, number, src, dst, rows, where):
        return remote(
            self.full.at[src[0], src[1], rows],
            self.full.at[dst[0], dst[1], rows],
            self.send_sem.at[number],
            self.recv_sem.at[number],
            where,
        )

    def copy(self, number):
        if number < 12:
            group, kind = number // 4, number % 4
            dy = 1 if group == 2 else 0
            start, size = (0, self.cut) if group == 0 else (self.cut, 192 - self.cut)
            low = size // 32 * 16
            src, dst, rows, to = [
                (0, 3, (start, size), 1),
                (0, 1, (start, size), 3),
                (3, 2, (start, low), 1),
                (1, 2, (start + low, size - low), 3),
            ][kind]
            return self.make(number, (dy, src), (dy, dst), pl.ds(*rows), grp_device(0, to))
        if number < 16:
            dz = number - 12
            return self.make(number, (0, dz), (1, dz), self.head, grp_device(1, 0))
        return self.make(number, (0, 0), (1, 0), self.rest, grp_device(1, 0))

    def start(self, *numbers):
        for number in numbers:
            self.copy(number).start()

    def wait(self, *numbers):
        for number in numbers:
            if number not in self.waited:
                self.waited.add(number)
                self.copy(number).wait_recv()

    def send_own(self):
        self.start(16, 0, 1, 12, 4, 5)

    def relay(self, group):
        for kind in range(2):
            self.wait(4 * group + kind)
            self.start(4 * group + 2 + kind)

    def pass_head(self, dz):
        self.wait(*{1: [1], 2: [2, 3], 3: [0]}[dz])
        self.start(12 + dz)

    def pass_rest(self):
        self.wait(16)
        self.start(8, 9)

    def wait_chunk(self, dy, dz):
        self.wait(*[4 + 4 * dy + kind for kind in {0: [], 1: [1], 2: [2, 3], 3: [0]}[dz]])
        if dy == 1:
            self.wait(12 + dz, 16)

    def drain(self):
        for number in range(17):
            self.copy(number).wait_send()


def chunk_of(dy, dz):
    grp = lax.axis_index("grp")
    return lax.rem(grp // 4 + dy, 2), lax.rem(lax.rem(grp, 4) + dz, 4) * 4


def chunk_rows(ref, dy, dz):
    expert, first = chunk_of(dy, dz)
    rows = ref[pl.ds(first, 4), pl.ds(pl.multiple_of(expert * 48, 16), 48), :]
    return rows.reshape(192, 512)


CHUNK_ORDER = [(1, 2), (1, 1), (1, 3), (0, 2), (1, 0), (0, 1), (0, 3), (0, 0)]


def return_rows(rows, dy, dz, send, recv, send_sem, recv_sem):
    me = lax.axis_index("ctx")
    expert, first = chunk_of(dy, dz)
    send[expert, pl.ds(first, 4)] = rows.reshape(4, 48, 512)

    @pl.loop(0, 4)
    def _(i):
        there = first + i

        @pl.when(there != me)
        def _():
            return_copy(expert, there, me, there, send, recv, send_sem, recv_sem).start()


def return_copy(expert, there, mine, partner, send, recv, send_sem, recv_sem):
    return remote(
        send.at[expert, there],
        recv.at[mine, expert],
        send_sem.at[expert, there],
        recv_sem.at[expert, mine],
        {"ctx": partner},
    )


def wait_returns(send, recv, send_sem, recv_sem):
    me = lax.axis_index("ctx")
    for expert in range(2):
        recv[me, expert] = send[expert, me]

        @pl.loop(1, 16)
        def _(k):
            source = lax.rem(me + k, 16)
            copy = return_copy(
                expert, source, source, source, send, recv, send_sem, recv_sem
            )
            copy.wait_recv()
            copy.wait_send()


def experts_kernel(
    x_ref, act_grad_ref, w_in_hbm,
    act_ref, rg_ref, w_in_grad_ref,
    part, sums, full, rg_send, w_in_ref, w_in_grad_s, w_sem, out_sem,
    s_send_sem, s_recv_sem, f_send_sem, f_recv_sem, r_send_sem, r_recv_sem,
):
    bf = jnp.bfloat16
    w_copy = pltpu.make_async_copy(w_in_hbm, w_in_ref, w_sem)
    w_copy.start()
    greet()
    w_copy.wait()
    summing = GrpSum(96, part, sums, s_send_sem, s_recv_sem)
    gathering = GrpGather(64, full, f_send_sem, f_recv_sem)
    for dy, dz in CHUNK_ORDER:
        expert, _ = chunk_of(dy, dz)
        rows = chunk_rows(x_ref, dy, dz)

        @pl.loop(0, 3)
        def _(piece):
            cols = pl.ds(pl.multiple_of(piece * 512, 512), 512)
            part[dy, dz, :, cols] = dot_nn(rows, w_in_ref[expert, :, cols]).astype(bf)

        summing.send_first(dy, dz)
    summing.relay(1)
    summing.relay(0)
    for dz in (2, 1):
        summing.second(dz)
    summing.second_rest()
    summing.second(3)
    summing.relay(2)

    def activate(rows, pre):
        act_ref[rows, :] = gelu_tanh(pre).astype(bf)
        full[0, 0, rows, :] = (act_grad_ref[rows, :] * gelu_slope(pre)).astype(bf)

    summing.finish_head(activate)
    gathering.start(0, 1, 12)
    summing.finish_rest(activate)
    gathering.start(16, 4, 5)

    def row_grads(dy, dz):
        expert, _ = chunk_of(dy, dz)
        rows = dot_nt(full[dy, dz], w_in_ref[expert]).astype(bf)
        return_rows(rows, dy, dz, rg_send, rg_ref, r_send_sem, r_recv_sem)

    row_grads(0, 0)
    gathering.relay(0)
    for dz in (3, 1):
        gathering.pass_head(dz)
    gathering.pass_rest()
    gathering.relay(1)
    gathering.pass_head(2)
    for dy, dz in [(0, 1), (0, 3)]:
        gathering.wait_chunk(dy, dz)
        row_grads(dy, dz)
    gathering.relay(2)
    def weight_grads(dy):
        expert, _ = chunk_of(dy, 0)

        @pl.loop(0, 3)
        def _(piece):
            cols = pl.ds(pl.multiple_of(piece * 512, 512), 512)
            total = dot_tn(chunk_rows(x_ref, dy, 0), full[dy, 0, :, cols])
            for dz in range(1, 4):
                total += dot_tn(chunk_rows(x_ref, dy, dz), full[dy, dz, :, cols])
            w_in_grad_s[expert, :, cols] = total.astype(bf)

        out = pltpu.make_async_copy(
            w_in_grad_s.at[expert], w_in_grad_ref.at[expert], out_sem.at[dy]
        )
        out.start()
        return out

    for dy, dz in [(1, 0), (0, 2), (1, 1), (1, 3)]:
        gathering.wait_chunk(dy, dz)
        row_grads(dy, dz)
    outs = [weight_grads(0)]
    gathering.wait_chunk(1, 2)
    row_grads(1, 2)
    outs.append(weight_grads(1))
    wait_returns(rg_send, rg_ref, r_send_sem, r_recv_sem)
    summing.drain()
    gathering.drain()
    for out in outs:
        out.wait()


def experts_call(x_rows, act_grad, w_in):
    bf = jnp.bfloat16
    vmem = pl.BlockSpec(memory_space=pltpu.VMEM)
    shape = jax.ShapeDtypeStruct
    return pl.pallas_call(
        experts_kernel,
        out_shape=(
            shape((192, 1536), bf),
            shape((16, 2, 48, 512), bf),
            shape((2, 512, 1536), bf),
        ),
        in_specs=[vmem] * 2 + [pl.BlockSpec(memory_space=pl.ANY)],
        out_specs=(vmem, vmem, pl.BlockSpec(memory_space=pl.ANY)),
        scratch_shapes=[
            pltpu.VMEM((2, 4, 192, 1536), bf),
            pltpu.VMEM((14, 192, 1536), bf),
            pltpu.VMEM((2, 4, 192, 1536), bf),
            pltpu.VMEM((2, 16, 48, 512), bf),
            pltpu.VMEM((2, 512, 1536), bf),
            pltpu.VMEM((2, 512, 1536), bf),
            pltpu.SemaphoreType.DMA,
            pltpu.SemaphoreType.DMA((2,)),
            pltpu.SemaphoreType.DMA((23,)),
            pltpu.SemaphoreType.DMA((23,)),
            pltpu.SemaphoreType.DMA((17,)),
            pltpu.SemaphoreType.DMA((17,)),
            pltpu.SemaphoreType.DMA((2, 16)),
            pltpu.SemaphoreType.DMA((2, 16)),
        ],
        compiler_params=pltpu.CompilerParams(
            collective_id=2, has_side_effects=True, vmem_limit_bytes=56 * 2**20
        ),
        name="experts",
    )(x_rows, act_grad, w_in)


def turn(row):
    return jnp.transpose(jnp.broadcast_to(row, (128, 256)))


def forward_kernel(
    q_ref, k_ref, v_ref, res_ref, lengths_ref, routes_ref, gates_ref, og_ref, w_out_hbm,
    rows_ref, rows_col_ref, qend_row_ref, attn_ref, lse_ref, mixed_ref, inv_ref, xrecv_ref, grecv_ref, act_grad_ref, kv_out_ref,
    kv, m_s, l_s, acc_s, gsend, xsend, part, sums, sq_send, sq_recv, gated, qend_s, w_out_ref,
    w_sem,
    kv_send_sem, kv_recv_sem, out_sem, g_send_sem, g_recv_sem, x_send_sem, x_recv_sem,
    p_send_sem, p_recv_sem, sq_send_sem, sq_recv_sem,
):
    me = lax.axis_index("ctx")
    grp = lax.axis_index("grp")
    core = lax.rem(me, 2)
    chip = me // 2
    x = lax.rem(chip, 4)
    yh = chip // 4

    def device(dy, dx, dc):
        there = lax.rem(yh + dy, 2) * 4 + lax.rem(x + dx, 4)
        return {"ctx": there * 2 + lax.rem(core + dc, 2)}

    w_copy = pltpu.make_async_copy(w_out_hbm, w_out_ref, w_sem)
    w_copy.start()
    greet()

    copies = {}
    sent = []

    def move(src, slot, where):
        copy = remote(src, kv.at[slot], kv_send_sem.at[len(sent)], kv_recv_sem.at[slot], where)
        copy.start()
        copies[slot] = copy
        sent.append(copy)

    def own(which):
        return k_ref if which == 0 else v_ref

    right, left = device(0, 1, 0), device(0, 3, 0)
    sibling, partner = device(0, 0, 1), device(1, 0, 0)
    early = lax.broadcasted_iota(jnp.int32, (256, 256), 0) < lax.broadcasted_iota(
        jnp.int32, (256, 256), 1
    )
    experts = [routes_ref[a : a + 1, :].astype(jnp.float32) for a in range(2)]
    for a in range(2):
        rank = jnp.zeros((1, 256), jnp.float32)
        for b in range(2):
            same = early & (turn(experts[b])[:, 0:1] == experts[a])
            rank += jnp.sum(jnp.where(same, 1.0, 0.0), axis=0, keepdims=True)
        cols = slice(a * 256, a * 256 + 256)
        rows = experts[a] * 48 + rank
        rows_ref[:, cols] = jnp.broadcast_to(rows, (8, 256)).astype(jnp.int32)
        rows_col_ref[:, a * 128 : a * 128 + 128] = turn(rows).astype(jnp.int32)
        gate = turn(gates_ref[a : a + 1, :])[:, 0:1]
        gated[cols, :] = (gate * og_ref[...].astype(jnp.float32)).astype(jnp.bfloat16)

    @pl.loop(0, 16)
    def _(k):
        there = lax.rem(me + k, 16)
        gsend[k] = dot_nn(pick_two(rows_ref, there), gated[...]).astype(jnp.bfloat16)

        @pl.when(k > 0)
        def _():
            remote(
                gsend.at[k], grecv_ref.at[me], g_send_sem.at[k], g_recv_sem.at[k], {"ctx": there}
            ).start()

    for which in range(2):
        move(own(which), (0, 0, 1, which), sibling)
    for which in range(2):
        move(own(which), (1, 0, 0, which), partner)
        move(own(which), (0, 3, 0, which), right)
        move(own(which), (0, 1, 0, which), left)
    grecv_ref[me] = gsend[0]
    kv[0, 0, 0, 0] = k_ref[...]
    kv[0, 0, 0, 1] = v_ref[...]
    pos_col = me * 256 + lax.broadcasted_iota(jnp.int32, (256, 128), 0)
    pos_row = me * 256 + lax.broadcasted_iota(jnp.int32, (8, 256), 1)
    ends_col, ends_row = jnp.full_like(pos_col, 4096), jnp.full_like(pos_row, 4096)
    end = jnp.int32(0)
    for f in range(16):
        end = end + lengths_ref[f]
        ends_col = jnp.minimum(ends_col, jnp.where(end > pos_col, end, 4096))
        ends_row = jnp.minimum(ends_row, jnp.where(end > pos_row, end, 4096))
    qend_s[...] = ends_col
    qend_row_ref[...] = ends_row
    summing = GrpSum(96, part, sums, p_send_sem, p_recv_sem)
    m_s[...] = jnp.full_like(m_s, LOW)
    l_s[...] = jnp.zeros_like(l_s)
    acc_s[...] = jnp.zeros_like(acc_s)
    outs = []

    def wait_slot(dy, dx, dc, which):
        copies[(dy, dx, dc, which)].wait_recv()

    def forward(dy, dx, which):
        wait_slot(dy, dx, 0, which)
        move(kv.at[dy, dx, 0, which], (dy, dx, 1, which), sibling)

    def relay(dy):
        forward(dy, 3, 0)
        move(kv.at[dy, 3, 0, 0], (dy, 2, 0, 0), right)
        forward(dy, 1, 1)
        move(kv.at[dy, 1, 0, 1], (dy, 2, 0, 1), left)
        forward(dy, 3, 1)
        forward(dy, 1, 0)

    def attend(dy, dx):
        for which in range(2):
            wait_slot(dy, dx, 1, which)
        copy = pltpu.make_async_copy(kv.at[dy, dx], kv_out_ref.at[dy, dx], out_sem.at[dy, dx])
        copy.start()
        outs.append(copy)
        there = lax.rem(yh + dy, 2) * 4 + lax.rem(x + dx, 4)
        lane = lax.broadcasted_iota(jnp.int32, (256, 256), 1)
        qend = qend_s[:, 0:1]
        limits = [qend - (there * 512 + lax.rem(core + dc, 2) * 256) for dc in range(2)]

        @pl.loop(0, 4)
        def _(h):
            cols = pl.ds(pl.multiple_of(h * 128, 128), 128)
            qh = q_ref[:, cols]
            scores = []
            for dc in range(2):
                s = dot_nt(qh, kv[dy, dx, dc, 0, :, cols]) * (LOG2E * HEAD_DIM**-0.5)
                scores.append(jnp.where(lane < limits[dc], s, LOW))
            top = jnp.max(jnp.maximum(scores[0], scores[1]), axis=1, keepdims=True)
            m_old = m_s[h]
            m_new = jnp.maximum(m_old, top)
            alpha = jnp.exp2(m_old - m_new)
            probs = [jnp.exp2(s - m_new[:, 0:1]) for s in scores]
            total = jnp.sum(probs[0] + probs[1], axis=1, keepdims=True)
            m_s[h] = m_new
            l_s[h] = l_s[h] * alpha + total
            acc = acc_s[h] * alpha
            for dc in range(2):
                acc += dot_nn(probs[dc].astype(jnp.bfloat16), kv[dy, dx, dc, 1, :, cols])
            acc_s[h] = acc

    attend(0, 0)

    @pl.loop(1, 16)
    def _(k):
        source = lax.rem(me + 16 - k, 16)
        remote(
            gsend.at[k], grecv_ref.at[source], g_send_sem.at[k], g_recv_sem.at[k], {"ctx": source}
        ).wait_recv()

    w_copy.wait()
    for dy, dz in CHUNK_ORDER:
        expert, _ = chunk_of(dy, dz)
        rows = chunk_rows(grecv_ref, dy, dz)

        @pl.loop(0, 3)
        def _(piece):
            cols = pl.ds(pl.multiple_of(piece * 512, 512), 512)
            part[dy, dz, :, cols] = dot_nt(rows, w_out_ref[expert, cols, :]).astype(jnp.bfloat16)

        summing.send_first(dy, dz)

    for which in range(2):
        wait_slot(1, 0, 0, which)
        move(kv.at[1, 0, 0, which], (1, 3, 0, which), right)
        move(kv.at[1, 0, 0, which], (1, 1, 0, which), left)
        move(kv.at[1, 0, 0, which], (1, 0, 1, which), sibling)
    relay(0)
    attend(0, 3)
    attend(0, 1)
    relay(1)
    summing.relay(1)
    summing.relay(0)
    attend(1, 0)
    for which in range(2):
        forward(0, 2, which)
    attend(0, 2)
    for dz in (2, 1, 3):
        summing.second(dz)
    attend(1, 3)
    attend(1, 1)
    summing.relay(2)
    for which in range(2):
        forward(1, 2, which)
    attend(1, 2)

    squares = jnp.zeros((256, 1), jnp.float32)
    for h in range(4):
        cols = slice(h * 128, h * 128 + 128)
        out = (acc_s[h] / l_s[h]).astype(jnp.bfloat16)
        lse_ref[h] = jnp.transpose(m_s[h] + jnp.log2(l_s[h]))[0:8]
        attn_ref[:, cols] = out
        mixed = (res_ref[:, cols].astype(jnp.float32) + out.astype(jnp.float32)).astype(
            jnp.bfloat16
        )
        mixed_ref[:, cols] = mixed
        mixed_f = mixed.astype(jnp.float32)
        squares += jnp.sum(mixed_f * mixed_f, axis=1, keepdims=True)
    turned = jnp.transpose(jnp.broadcast_to(squares, (256, 128)))
    sq_send[...] = turned[0:8]
    sq_recv[grp] = turned[0:8]

    @pl.loop(1, 8)
    def _(k):
        there = lax.rem(grp + k, 8)
        remote(
            sq_send, sq_recv.at[grp], sq_send_sem.at[k], sq_recv_sem.at[k], {"grp": there}
        ).start()

    @pl.loop(1, 8)
    def _(k):
        source = lax.rem(grp + 8 - k, 8)
        copy = remote(
            sq_send, sq_recv.at[source], sq_send_sem.at[k], sq_recv_sem.at[k], {"grp": source}
        )
        copy.wait_recv()
        copy.wait_send()

    total = sq_recv[0]
    for k in range(1, 8):
        total = total + sq_recv[k]
    inv = lax.rsqrt(total / 4096 + 1e-06)
    inv = jnp.transpose(jnp.concatenate([inv] * 16, axis=0))
    inv_ref[...] = inv
    normed = jnp.concatenate(
        [
            (mixed_ref[:, h * 128 : h * 128 + 128].astype(jnp.float32) * inv).astype(jnp.bfloat16)
            for h in range(4)
        ],
        axis=1,
    )

    @pl.loop(0, 16)
    def _(k):
        there = lax.rem(me + k, 16)
        xsend[k] = dot_nn(pick_both(rows_ref, there), normed).astype(jnp.bfloat16)

        @pl.when(k > 0)
        def _():
            remote(
                xsend.at[k], xrecv_ref.at[me], x_send_sem.at[k], x_recv_sem.at[k], {"ctx": there}
            ).start()

    xrecv_ref[me] = xsend[0]

    summing.second_rest()

    def keep(rows, total):
        act_grad_ref[rows, :] = total

    summing.finish_head(keep)
    summing.finish_rest(keep)
    summing.drain()

    @pl.loop(1, 16)
    def _(k):
        source = lax.rem(me + 16 - k, 16)
        copy = remote(
            gsend.at[k], grecv_ref.at[source], g_send_sem.at[k], g_recv_sem.at[k], {"ctx": source}
        )
        copy.wait_send()
        copy = remote(
            xsend.at[k], xrecv_ref.at[source], x_send_sem.at[k], x_recv_sem.at[k], {"ctx": source}
        )
        copy.wait_recv()
        copy.wait_send()

    for copy in sent:
        copy.wait_send()
    for copy in outs:
        copy.wait()


def forward_call(*operands):
    bf, f32 = jnp.bfloat16, jnp.float32
    vmem = pl.BlockSpec(memory_space=pltpu.VMEM)
    shape = jax.ShapeDtypeStruct
    return pl.pallas_call(
        forward_kernel,
        out_shape=(
            shape((8, 512), jnp.int32),
            shape((256, 256), jnp.int32),
            shape((8, 256), jnp.int32),
            shape((256, 512), bf),
            shape((4, 8, 256), f32),
            shape((256, 512), bf),
            shape((256, 128), f32),
            shape((16, 96, 512), bf),
            shape((16, 96, 512), bf),
            shape((192, 1536), f32),
            shape((2, 4, 2, 2, 256, 512), bf),
        ),
        in_specs=[vmem] * 4
        + [pl.BlockSpec(memory_space=pltpu.SMEM)]
        + [vmem] * 3
        + [pl.BlockSpec(memory_space=pl.ANY)],
        out_specs=[vmem] * 10 + [pl.BlockSpec(memory_space=pl.ANY)],
        scratch_shapes=[
            pltpu.VMEM((2, 4, 2, 2, 256, 512), bf),
            pltpu.VMEM((4, 256, 128), f32),
            pltpu.VMEM((4, 256, 128), f32),
            pltpu.VMEM((4, 256, 128), f32),
            pltpu.VMEM((16, 96, 512), bf),
            pltpu.VMEM((16, 96, 512), bf),
            pltpu.VMEM((2, 4, 192, 1536), bf),
            pltpu.VMEM((14, 192, 1536), bf),
            pltpu.VMEM((8, 256), f32),
            pltpu.VMEM((8, 8, 256), f32),
            pltpu.VMEM((512, 512), bf),
            pltpu.VMEM((256, 128), jnp.int32),
            pltpu.VMEM((2, 1536, 512), bf),
            pltpu.SemaphoreType.DMA,
            pltpu.SemaphoreType.DMA((30,)),
            pltpu.SemaphoreType.DMA((2, 4, 2, 2)),
            pltpu.SemaphoreType.DMA((2, 4)),
            pltpu.SemaphoreType.DMA((16,)),
            pltpu.SemaphoreType.DMA((16,)),
            pltpu.SemaphoreType.DMA((16,)),
            pltpu.SemaphoreType.DMA((16,)),
            pltpu.SemaphoreType.DMA((23,)),
            pltpu.SemaphoreType.DMA((23,)),
            pltpu.SemaphoreType.DMA((8,)),
            pltpu.SemaphoreType.DMA((8,)),
        ],
        compiler_params=pltpu.CompilerParams(
            collective_id=0, has_side_effects=True, vmem_limit_bytes=56 * 2**20
        ),
        name="forward",
    )(*operands)


TERM_ORDER = [(1, 3), (1, 1), (1, 2), (1, 0), (0, 3), (0, 1), (0, 2), (0, 0)]


def backward_kernel(
    q_ref, kv_hbm, lse_ref, attn_ref, qend_ref, og_ref, inv_ref, rows_ref, rg_ref, act_ref,
    w_out_hbm, g_hbm, mixed_ref, gates_ref,
    layer_ref, ig_ref, dq_ref, dk_ref, dv_ref, w_out_grad_ref,
    full, eo_send, eo_recv, kv_ref, w_out_ref, g_ref, w_out_grad_s, load_sem, normed_grad, row_dot, dqt, own_terms, sib_send, sib_recv, ring_send,
    ring_recv, part_send, part_recv,
    f_send_sem, f_recv_sem, r_send_sem, r_recv_sem, sib_send_sem, sib_recv_sem, ring_send_sem, ring_recv_sem,
    part_send_sem, part_recv_sem,
):
    me = lax.axis_index("ctx")
    core = lax.rem(me, 2)
    chip = me // 2
    x = lax.rem(chip, 4)
    yh = chip // 4
    bf, f32 = jnp.bfloat16, jnp.float32

    def device(dy, dx, dc):
        there = lax.rem(yh + dy, 2) * 4 + lax.rem(x + dx, 4)
        return {"ctx": there * 2 + lax.rem(core + dc, 2)}

    right, left = device(0, 1, 0), device(0, 3, 0)
    sibling, partner = device(0, 0, 1), device(1, 0, 0)
    loads = {}
    for dy, dx in TERM_ORDER:
        loads[(dy, dx)] = pltpu.make_async_copy(
            kv_hbm.at[dy, dx], kv_ref.at[dy, dx], load_sem.at[dy * 4 + dx]
        )
    w_load = pltpu.make_async_copy(w_out_hbm, w_out_ref, load_sem.at[8])
    g_load = pltpu.make_async_copy(g_hbm, g_ref, load_sem.at[9])
    loads[(1, 3)].start()
    loads[(1, 1)].start()
    greet()
    gathering = GrpGather(64, full, f_send_sem, f_recv_sem)
    full[0, 0] = act_ref[...]
    gathering.send_own()
    for dy, dx in TERM_ORDER[2:]:
        loads[(dy, dx)].start()
    w_load.start()
    g_load.start()
    dqt[...] = jnp.zeros_like(dqt)
    row_id = lax.broadcasted_iota(jnp.int32, (256, 1536), 1)
    hits = [row_id == rows_ref[:, a * 128 : a * 128 + 1] for a in range(2)]
    pick = jnp.where(hits[0] | hits[1], 1.0, 0.0).astype(bf)
    normed_grad[...] = dot_nn(pick, rg_ref[...].reshape(1536, 512))

    for h in range(4):
        cols = slice(h * 128, h * 128 + 128)
        grad = og_ref[:, cols].astype(f32) + inv_ref[...] * normed_grad[:, cols]
        grad = grad.astype(bf)
        ig_ref[:, cols] = grad
        dots = jnp.sum(grad.astype(f32) * attn_ref[:, cols].astype(f32), axis=1, keepdims=True)
        row_dot[h] = jnp.transpose(jnp.broadcast_to(dots, (256, 128)))[0:8]

    scale = HEAD_DIM**-0.5

    def terms(dy, dx):
        loads[(dy, dx)].wait()
        there = lax.rem(yh + dy, 2) * 4 + lax.rem(x + dx, 4)
        sub = lax.broadcasted_iota(jnp.int32, (256, 256), 0)
        qend = qend_ref[0:1, :]
        limits = [qend - (there * 512 + lax.rem(core + dc, 2) * 256) for dc in range(2)]

        @pl.loop(0, 4)
        def _(h):
            cols = pl.ds(pl.multiple_of(h * 128, 128), 128)
            qh = q_ref[:, cols]
            gh = ig_ref[:, cols]
            lse = lse_ref[h][0:1, :]
            dots = row_dot[h][0:1, :]
            for dc in range(2):
                kh = kv_ref[dy, dx, dc, 0, :, cols]
                vh = kv_ref[dy, dx, dc, 1, :, cols]
                s = dot_nt(kh, qh) * (LOG2E * scale)
                p = jnp.exp2(jnp.where(sub < limits[dc], s, LOW) - lse)
                dp = dot_nt(vh, gh)
                ds = (p * (dp - dots) * scale).astype(bf)
                dk = dot_nn(ds, qh).astype(bf)
                dv = dot_nn(p.astype(bf), gh).astype(bf)
                dqt[h] += dot_tn(kh, ds)
                to = own_terms if dc == 0 else sib_send
                to[dy, dx, 0, :, cols] = dk
                to[dy, dx, 1, :, cols] = dv

        for which in range(2):
            sib_copy(dy, dx, which).start()

    def sib_copy(dy, dx, which):
        return remote(
            sib_send.at[dy, dx, which],
            sib_recv.at[dy, dx, which],
            sib_send_sem.at[dy, dx, which],
            sib_recv_sem.at[dy, dx, which],
            sibling,
        )

    def ring_copy(dy, dx, which):
        to = (dx + 3) % 4 if which == 0 else (dx + 1) % 4
        return remote(
            ring_send.at[dy, dx, which],
            ring_recv.at[dy, to, which],
            ring_send_sem.at[dy, dx, which],
            ring_recv_sem.at[dy, to, which],
            right if which == 0 else left,
        )

    def arrival(dy, dx, which):
        return ring_copy(dy, (dx + 1) % 4 if which == 0 else (dx + 3) % 4, which)

    def total_of(dy, dx, which, ring):
        sib_copy(dy, dx, which).wait_recv()
        if ring:
            arrival(dy, dx, which).wait_recv()
        sums = own_terms[dy, dx, which].astype(f32) + sib_recv[dy, dx, which].astype(f32)
        if ring:
            sums = sums + ring_recv[dy, dx, which].astype(f32)
        return sums

    def send_ring(dy, dx, which, ring):
        ring_send[dy, dx, which] = total_of(dy, dx, which, ring).astype(bf)
        ring_copy(dy, dx, which).start()

    def part_copy(which):
        return remote(
            part_send.at[which],
            part_recv.at[which],
            part_send_sem.at[which],
            part_recv_sem.at[which],
            partner,
        )

    def expert_rows(dy, dz):
        expert, _ = chunk_of(dy, dz)
        rows = dot_nn(full[dy, dz], w_out_ref[expert]).astype(bf)
        return_rows(rows, dy, dz, eo_send, eo_recv, r_send_sem, r_recv_sem)

    terms(1, 3)
    terms(1, 1)
    send_ring(1, 3, 0, False)
    send_ring(1, 1, 1, False)
    terms(1, 2)
    terms(1, 0)
    send_ring(1, 2, 0, True)
    send_ring(1, 2, 1, True)
    w_load.wait()
    gathering.relay(0)
    for dz in (3, 1):
        gathering.pass_head(dz)
    gathering.pass_rest()
    gathering.relay(1)
    expert_rows(0, 0)
    terms(0, 3)
    send_ring(1, 1, 0, True)
    send_ring(1, 3, 1, True)
    send_ring(0, 3, 0, False)
    terms(0, 1)
    send_ring(0, 1, 1, False)
    gathering.pass_head(2)
    gathering.relay(2)
    terms(0, 2)
    for which in range(2):
        part_send[which] = total_of(1, 0, which, True).astype(bf)
        part_copy(which).start()
    send_ring(0, 2, 0, True)
    send_ring(0, 2, 1, True)
    terms(0, 0)
    send_ring(0, 1, 0, True)
    send_ring(0, 3, 1, True)
    for dy, dz in [(0, 1), (0, 3), (1, 0)]:
        gathering.wait_chunk(dy, dz)
        expert_rows(dy, dz)
    for h in range(4):
        dq_ref[:, h * 128 : h * 128 + 128] = jnp.transpose(dqt[h]).astype(bf)
    def weight_grads(dy):
        expert, _ = chunk_of(dy, 0)

        @pl.loop(0, 3)
        def _(piece):
            cols = pl.ds(pl.multiple_of(piece * 512, 512), 512)
            total = dot_tn(full[dy, 0, :, cols], chunk_rows(g_ref, dy, 0))
            for dz in range(1, 4):
                total += dot_tn(full[dy, dz, :, cols], chunk_rows(g_ref, dy, dz))
            w_out_grad_s[expert, cols, :] = total.astype(bf)

        out = pltpu.make_async_copy(
            w_out_grad_s.at[expert], w_out_grad_ref.at[expert], load_sem.at[10 + dy]
        )
        out.start()
        return out

    g_load.wait()
    for dy, dz in [(0, 2), (1, 1), (1, 3)]:
        gathering.wait_chunk(dy, dz)
        expert_rows(dy, dz)
    w_outs = [weight_grads(0)]
    gathering.wait_chunk(1, 2)
    expert_rows(1, 2)
    for which in range(2):
        sums = total_of(0, 0, which, True)
        part_copy(which).wait_recv()
        sums = sums + part_recv[which].astype(f32)
        if which == 0:
            dk_ref[...] = sums.astype(bf)
        else:
            dv_ref[...] = sums.astype(bf)

    for dy in range(2):
        for dx in range(4):
            for which in range(2):
                sib_copy(dy, dx, which).wait_send()
                if dx > 0:
                    ring_copy(dy, dx, which).wait_send()
    for which in range(2):
        part_copy(which).wait_send()

    w_outs.append(weight_grads(1))
    wait_returns(eo_send, eo_recv, r_send_sem, r_recv_sem)
    total = mixed_ref[...].astype(f32)
    for a in range(2):
        hit = row_id == rows_ref[:, a * 128 : a * 128 + 1]
        picked = dot_nn(jnp.where(hit, 1.0, 0.0).astype(bf), eo_recv[...].reshape(1536, 512))
        total = total + turn(gates_ref[a : a + 1, :])[:, 0:1] * picked
    layer_ref[...] = total.astype(bf)

    gathering.drain()
    for out in w_outs:
        out.wait()


def backward_call(*operands):
    bf, f32 = jnp.bfloat16, jnp.float32
    vmem = pl.BlockSpec(memory_space=pltpu.VMEM)
    anywhere = pl.BlockSpec(memory_space=pl.ANY)
    shape = jax.ShapeDtypeStruct
    return pl.pallas_call(
        backward_kernel,
        out_shape=(shape((256, 512), bf),) * 5 + (shape((2, 1536, 512), bf),),
        in_specs=[vmem, anywhere] + [vmem] * 8 + [anywhere] * 2 + [vmem] * 2,
        out_specs=(vmem,) * 5 + (anywhere,),
        scratch_shapes=[
            pltpu.VMEM((2, 4, 192, 1536), bf),
            pltpu.VMEM((2, 16, 48, 512), bf),
            pltpu.VMEM((16, 2, 48, 512), bf),
            pltpu.VMEM((2, 4, 2, 2, 256, 512), bf),
            pltpu.VMEM((2, 1536, 512), bf),
            pltpu.VMEM((16, 96, 512), bf),
            pltpu.VMEM((2, 1536, 512), bf),
            pltpu.SemaphoreType.DMA((12,)),
            pltpu.VMEM((256, 512), f32),
            pltpu.VMEM((4, 8, 256), f32),
            pltpu.VMEM((4, 128, 256), f32),
            pltpu.VMEM((2, 4, 2, 256, 512), bf),
            pltpu.VMEM((2, 4, 2, 256, 512), bf),
            pltpu.VMEM((2, 4, 2, 256, 512), bf),
            pltpu.VMEM((2, 4, 2, 256, 512), bf),
            pltpu.VMEM((2, 4, 2, 256, 512), bf),
            pltpu.VMEM((2, 256, 512), bf),
            pltpu.VMEM((2, 256, 512), bf),
            pltpu.SemaphoreType.DMA((17,)),
            pltpu.SemaphoreType.DMA((17,)),
            pltpu.SemaphoreType.DMA((2, 16)),
            pltpu.SemaphoreType.DMA((2, 16)),
            pltpu.SemaphoreType.DMA((2, 4, 2)),
            pltpu.SemaphoreType.DMA((2, 4, 2)),
            pltpu.SemaphoreType.DMA((2, 4, 2)),
            pltpu.SemaphoreType.DMA((2, 4, 2)),
            pltpu.SemaphoreType.DMA((2,)),
            pltpu.SemaphoreType.DMA((2,)),
        ],
        compiler_params=pltpu.CompilerParams(
            collective_id=1, has_side_effects=True, vmem_limit_bytes=56 * 2**20
        ),
        name="backward",
    )(*operands)


def publish_kernel(count, *refs):
    sources, targets, held = refs[:count], refs[count : 2 * count], refs[2 * count : 3 * count]
    in_sem, out_sem = refs[3 * count :]
    reads = [pltpu.make_async_copy(sources[n], held[n], in_sem.at[n]) for n in range(count)]
    writes = [pltpu.make_async_copy(held[n], targets[n], out_sem.at[n]) for n in range(count)]
    for read in reads:
        read.start()
    for read, write in zip(reads, writes):
        read.wait()
        write.start()
    for write in writes:
        write.wait()


def publish(*arrays):
    anywhere = pl.BlockSpec(memory_space=pl.ANY)
    count = len(arrays)
    return pl.pallas_call(
        functools.partial(publish_kernel, count),
        out_shape=tuple(jax.ShapeDtypeStruct(a.shape, a.dtype) for a in arrays),
        in_specs=[anywhere] * count,
        out_specs=(anywhere,) * count,
        scratch_shapes=[pltpu.VMEM(a.shape, a.dtype) for a in arrays]
        + [pltpu.SemaphoreType.DMA((count,))] * 2,
        compiler_params=pltpu.CompilerParams(vmem_limit_bytes=56 * 2**20),
        name="publish",
    )(*arrays)


def shards(
    residual, queries, keys, values, frame_lengths, routes, route_gates, w_in, w_out, out_grad
):
    n_ctx = lax.axis_size("ctx")
    tok_rows, feat_dev = residual.shape
    exp_dev = w_in.shape[0]
    rows_wide, rows_col, qend_row, attn, lse, mixed, inv_wide, rows_recv, grads_recv, act_grad, kv_all = (
        forward_call(
            queries,
            keys,
            values,
            residual,
            frame_lengths,
            routes.T,
            route_gates.T,
            out_grad,
            w_out,
        )
    )
    activated, row_grad, w_in_grad = experts_call(rows_recv, act_grad, w_in)
    layer_out, input_grad, query_grad, key_grad, value_grad, w_out_grad = backward_call(
        queries,
        kv_all,
        lse,
        attn,
        qend_row,
        out_grad,
        inv_wide,
        rows_col,
        row_grad.reshape(n_ctx, exp_dev * row_grad.shape[2], feat_dev),
        activated,
        w_out,
        grads_recv,
        mixed,
        route_gates.T,
    )
    return publish(
        layer_out,
        input_grad,
        query_grad,
        key_grad,
        value_grad,
        w_in_grad,
        w_out_grad,
    )


def solution(mesh):
    in_specs = (
        P("ctx", "grp"),
        P("ctx", "grp"),
        P("ctx", "grp"),
        P("ctx", "grp"),
        P(),
        P("ctx", None),
        P("ctx", None),
        P("ctx", "grp", None),
        P("ctx", None, "grp"),
        P("ctx", "grp"),
    )
    out_specs = (
        P("ctx", "grp"),
        P("ctx", "grp"),
        P("ctx", "grp"),
        P("ctx", "grp"),
        P("ctx", "grp"),
        P("ctx", "grp", None),
        P("ctx", None, "grp"),
    )
    return jax.shard_map(shards, mesh=mesh, in_specs=in_specs, out_specs=out_specs, check_vma=False)
```

```python
import functools

import jax
import jax.numpy as jnp
from jax import lax
from jax.experimental import pallas as pl
from jax.experimental.pallas import tpu as pltpu
from jax.sharding import PartitionSpec as P

HEAD_DIM = 128


gelu_coef = 0.7978845608028654


def gelu_tanh(field):
    return 0.5 * field * (1.0 + jnp.tanh(gelu_coef * (field + 0.044715 * field * field * field)))


def gelu_slope(field):
    tanh_val = jnp.tanh(gelu_coef * (field + 0.044715 * field * field * field))
    return 0.5 * (1.0 + tanh_val) + 0.5 * field * (1.0 - tanh_val * tanh_val) * gelu_coef * (
        1.0 + 3.0 * 0.044715 * field * field
    )


MESH_ID = pl.DeviceIdType.MESH
LOG2E = 1.4426950408889634
LOW = -1e30


def dot_nt(a, b):
    return lax.dot_general(a, b, (((1,), (1,)), ((), ())), preferred_element_type=jnp.float32)


def dot_tn(a, b):
    return lax.dot_general(a, b, (((0,), (0,)), ((), ())), preferred_element_type=jnp.float32)


def dot_nn(a, b):
    return jnp.dot(a, b, preferred_element_type=jnp.float32)


def greet():
    me = lax.axis_index("ctx")
    grp = lax.axis_index("grp")
    barrier = pltpu.get_barrier_semaphore()

    @pl.loop(1, 16)
    def _(k):
        pl.semaphore_signal(
            barrier, inc=1, device_id={"ctx": lax.rem(me + k, 16)}, device_id_type=MESH_ID
        )

    @pl.loop(1, 8)
    def _(k):
        pl.semaphore_signal(
            barrier, inc=1, device_id={"grp": lax.rem(grp + k, 8)}, device_id_type=MESH_ID
        )

    pl.semaphore_wait(barrier, 22)


def remote(src, dst, send_sem, recv_sem, where):
    return pltpu.make_async_remote_copy(
        src_ref=src,
        dst_ref=dst,
        send_sem=send_sem,
        recv_sem=recv_sem,
        device_id=where,
        device_id_type=MESH_ID,
    )


def pick_two(rows_ref, there):
    rows = lax.broadcasted_iota(jnp.int32, (96, 512), 0) + there * 96
    return jnp.where(rows == rows_ref[0:1, :], 1.0, 0.0).astype(jnp.bfloat16)


def pick_both(rows_ref, there):
    rows = lax.broadcasted_iota(jnp.int32, (96, 256), 0) + there * 96
    hit = (rows == rows_ref[0:1, 0:256]) | (rows == rows_ref[0:1, 256:512])
    return jnp.where(hit, 1.0, 0.0).astype(jnp.bfloat16)


def grp_device(dy, dz):
    grp = lax.axis_index("grp")
    there = lax.rem(grp // 4 + dy, 2) * 4 + lax.rem(lax.rem(grp, 4) + dz, 4)
    return {"grp": there}


class GrpSum:
    def __init__(self, cut, part, recv, send_sem, recv_sem):
        self.cut, self.part, self.recv = cut, part, recv
        self.send_sem, self.recv_sem = send_sem, recv_sem
        self.head, self.rest = pl.ds(0, cut), pl.ds(cut, 192 - cut)

    def halves(self, group):
        start, size = (0, self.cut) if group == 2 else (self.cut, 192 - self.cut)
        low = size // 32 * 16
        return (start, low), (start + low, size - low)

    def make(self, number, src, slot, rows, where):
        return remote(
            src,
            self.recv.at[slot, rows],
            self.send_sem.at[number],
            self.recv_sem.at[number],
            where,
        )

    def partner_head(self, dz):
        return self.make(dz, self.part.at[1, dz, self.head], dz, self.head, grp_device(1, 0))

    def partner_rest(self):
        return self.make(22, self.part.at[1, 0, self.rest], 13, self.rest, grp_device(1, 0))

    def along(self, group, kind):
        dy, base = (0 if group == 2 else group), 4 + 3 * group
        low, high = [pl.ds(*half) for half in self.halves(group)]
        dz, rows, slot, to = [
            (2, low, base, 1),
            (2, high, base, 3),
            (1, high, base + 1, 1),
            (3, low, base + 2, 3),
            (1, low, base + 1, 1),
            (3, high, base + 2, 3),
        ][kind]
        number = 4 + 6 * group + kind
        return self.make(number, self.part.at[dy, dz, rows], slot, rows, grp_device(0, to))

    def start_along(self, group, dz):
        for kind in {0: [], 1: [2], 2: [0, 1], 3: [3]}[dz]:
            self.along(group, kind).start()

    def send_first(self, dy, dz):
        if dy == 1:
            self.partner_head(dz).start()
        self.start_along(dy, dz)

    def add(self, target, start, size, slots, out=None):
        def keep(rows, total):
            self.part[target[0], target[1], rows, :] = total.astype(jnp.bfloat16)

        @pl.loop(0, size // 16)
        def _(step):
            rows = pl.ds(pl.multiple_of(start + step * 16, 16), 16)
            total = self.part[target[0], target[1], rows, :].astype(jnp.float32)
            for slot in slots:
                total += self.recv[slot, rows, :].astype(jnp.float32)
            (out or keep)(rows, total)

    def relay(self, group):
        dy, base = (0 if group == 2 else group), 4 + 3 * group
        low, high = self.halves(group)
        self.along(group, 0).wait_recv()
        self.add((dy, 1), *low, [base])
        self.along(group, 4).start()
        self.along(group, 1).wait_recv()
        self.add((dy, 3), *high, [base])
        self.along(group, 5).start()

    def second(self, dz):
        self.partner_head(dz).wait_recv()
        self.add((0, dz), 0, self.cut, [dz])
        self.start_along(2, dz)

    def wait_along(self, group):
        for kind in range(2, 6):
            self.along(group, kind).wait_recv()

    def second_rest(self):
        self.wait_along(1)
        self.add((1, 0), self.cut, 192 - self.cut, [8, 9])
        self.partner_rest().start()

    def finish_head(self, out):
        self.partner_head(0).wait_recv()
        self.wait_along(2)
        self.add((0, 0), 0, self.cut, [0, 11, 12], out)

    def finish_rest(self, out):
        self.wait_along(0)
        self.partner_rest().wait_recv()
        self.add((0, 0), self.cut, 192 - self.cut, [5, 6, 13], out)

    def drain(self):
        for dz in range(4):
            self.partner_head(dz).wait_send()
        for group in range(3):
            for kind in range(6):
                self.along(group, kind).wait_send()
        self.partner_rest().wait_send()


class GrpGather:
    def __init__(self, cut, full, send_sem, recv_sem):
        self.cut, self.full, self.send_sem, self.recv_sem = cut, full, send_sem, recv_sem
        self.head, self.rest = pl.ds(0, cut), pl.ds(cut, 192 - cut)
        self.waited = set()

    def make(self, number, src, dst, rows, where):
        return remote(
            self.full.at[src[0], src[1], rows],
            self.full.at[dst[0], dst[1], rows],
            self.send_sem.at[number],
            self.recv_sem.at[number],
            where,
        )

    def copy(self, number):
        if number < 12:
            group, kind = number // 4, number % 4
            dy = 1 if group == 2 else 0
            start, size = (0, self.cut) if group == 0 else (self.cut, 192 - self.cut)
            low = size // 32 * 16
            src, dst, rows, to = [
                (0, 3, (start, size), 1),
                (0, 1, (start, size), 3),
                (3, 2, (start, low), 1),
                (1, 2, (start + low, size - low), 3),
            ][kind]
            return self.make(number, (dy, src), (dy, dst), pl.ds(*rows), grp_device(0, to))
        if number < 16:
            dz = number - 12
            return self.make(number, (0, dz), (1, dz), self.head, grp_device(1, 0))
        return self.make(number, (0, 0), (1, 0), self.rest, grp_device(1, 0))

    def start(self, *numbers):
        for number in numbers:
            self.copy(number).start()

    def wait(self, *numbers):
        for number in numbers:
            if number not in self.waited:
                self.waited.add(number)
                self.copy(number).wait_recv()

    def send_own(self):
        self.start(16, 0, 1, 12, 4, 5)

    def relay(self, group):
        for kind in range(2):
            self.wait(4 * group + kind)
            self.start(4 * group + 2 + kind)

    def pass_head(self, dz):
        self.wait(*{1: [1], 2: [2, 3], 3: [0]}[dz])
        self.start(12 + dz)

    def pass_rest(self):
        self.wait(16)
        self.start(8, 9)

    def wait_chunk(self, dy, dz):
        self.wait(*[4 + 4 * dy + kind for kind in {0: [], 1: [1], 2: [2, 3], 3: [0]}[dz]])
        if dy == 1:
            self.wait(12 + dz, 16)

    def drain(self):
        for number in range(17):
            self.copy(number).wait_send()


def chunk_of(dy, dz):
    grp = lax.axis_index("grp")
    return lax.rem(grp // 4 + dy, 2), lax.rem(lax.rem(grp, 4) + dz, 4) * 4


def chunk_rows(ref, dy, dz):
    expert, first = chunk_of(dy, dz)
    rows = ref[pl.ds(first, 4), pl.ds(pl.multiple_of(expert * 48, 16), 48), :]
    return rows.reshape(192, 512)


CHUNK_ORDER = [(1, 2), (1, 1), (1, 3), (0, 2), (1, 0), (0, 1), (0, 3), (0, 0)]


def return_rows(rows, dy, dz, send, recv, send_sem, recv_sem):
    me = lax.axis_index("ctx")
    expert, first = chunk_of(dy, dz)
    send[expert, pl.ds(first, 4)] = rows.reshape(4, 48, 512)

    @pl.loop(0, 4)
    def _(i):
        there = first + i

        @pl.when(there != me)
        def _():
            return_copy(expert, there, me, there, send, recv, send_sem, recv_sem).start()


def return_copy(expert, there, mine, partner, send, recv, send_sem, recv_sem):
    return remote(
        send.at[expert, there],
        recv.at[mine, expert],
        send_sem.at[expert, there],
        recv_sem.at[expert, mine],
        {"ctx": partner},
    )


def wait_returns(send, recv, send_sem, recv_sem):
    me = lax.axis_index("ctx")
    for expert in range(2):
        recv[me, expert] = send[expert, me]

        @pl.loop(1, 16)
        def _(k):
            source = lax.rem(me + k, 16)
            copy = return_copy(
                expert, source, source, source, send, recv, send_sem, recv_sem
            )
            copy.wait_recv()
            copy.wait_send()


def experts_kernel(
    x_ref, act_grad_ref, w_in_hbm,
    act_ref, rg_ref, w_in_grad_ref,
    part, sums, full, rg_send, w_in_ref, w_in_grad_s, w_sem, out_sem,
    s_send_sem, s_recv_sem, f_send_sem, f_recv_sem, r_send_sem, r_recv_sem,
):
    bf = jnp.bfloat16
    w_copy = pltpu.make_async_copy(w_in_hbm, w_in_ref, w_sem)
    w_copy.start()
    greet()
    w_copy.wait()
    summing = GrpSum(96, part, sums, s_send_sem, s_recv_sem)
    gathering = GrpGather(64, full, f_send_sem, f_recv_sem)
    for dy, dz in CHUNK_ORDER:
        expert, _ = chunk_of(dy, dz)
        rows = chunk_rows(x_ref, dy, dz)

        @pl.loop(0, 3)
        def _(piece):
            cols = pl.ds(pl.multiple_of(piece * 512, 512), 512)
            part[dy, dz, :, cols] = dot_nn(rows, w_in_ref[expert, :, cols]).astype(bf)

        summing.send_first(dy, dz)
    summing.relay(1)
    summing.relay(0)
    for dz in (2, 1):
        summing.second(dz)
    summing.second_rest()
    summing.second(3)
    summing.relay(2)

    def activate(rows, pre):
        act_ref[rows, :] = gelu_tanh(pre).astype(bf)
        full[0, 0, rows, :] = (act_grad_ref[rows, :] * gelu_slope(pre)).astype(bf)

    summing.finish_head(activate)
    gathering.start(0, 1, 12)
    summing.finish_rest(activate)
    gathering.start(16, 4, 5)

    def row_grads(dy, dz):
        expert, _ = chunk_of(dy, dz)
        rows = dot_nt(full[dy, dz], w_in_ref[expert]).astype(bf)
        return_rows(rows, dy, dz, rg_send, rg_ref, r_send_sem, r_recv_sem)

    row_grads(0, 0)
    gathering.relay(0)
    for dz in (3, 1):
        gathering.pass_head(dz)
    gathering.pass_rest()
    gathering.relay(1)
    gathering.pass_head(2)
    for dy, dz in [(0, 1), (0, 3)]:
        gathering.wait_chunk(dy, dz)
        row_grads(dy, dz)
    gathering.relay(2)
    def weight_grads(dy):
        expert, _ = chunk_of(dy, 0)

        @pl.loop(0, 3)
        def _(piece):
            cols = pl.ds(pl.multiple_of(piece * 512, 512), 512)
            total = dot_tn(chunk_rows(x_ref, dy, 0), full[dy, 0, :, cols])
            for dz in range(1, 4):
                total += dot_tn(chunk_rows(x_ref, dy, dz), full[dy, dz, :, cols])
            w_in_grad_s[expert, :, cols] = total.astype(bf)

        out = pltpu.make_async_copy(
            w_in_grad_s.at[expert], w_in_grad_ref.at[expert], out_sem.at[dy]
        )
        out.start()
        return out

    for dy, dz in [(1, 0), (0, 2), (1, 1), (1, 3)]:
        gathering.wait_chunk(dy, dz)
        row_grads(dy, dz)
    outs = [weight_grads(0)]
    gathering.wait_chunk(1, 2)
    row_grads(1, 2)
    outs.append(weight_grads(1))
    wait_returns(rg_send, rg_ref, r_send_sem, r_recv_sem)
    summing.drain()
    gathering.drain()
    for out in outs:
        out.wait()


def experts_call(x_rows, act_grad, w_in):
    bf = jnp.bfloat16
    vmem = pl.BlockSpec(memory_space=pltpu.VMEM)
    shape = jax.ShapeDtypeStruct
    return pl.pallas_call(
        experts_kernel,
        out_shape=(
            shape((192, 1536), bf),
            shape((16, 2, 48, 512), bf),
            shape((2, 512, 1536), bf),
        ),
        in_specs=[vmem] * 2 + [pl.BlockSpec(memory_space=pl.ANY)],
        out_specs=(vmem, vmem, pl.BlockSpec(memory_space=pl.ANY)),
        scratch_shapes=[
            pltpu.VMEM((2, 4, 192, 1536), bf),
            pltpu.VMEM((14, 192, 1536), bf),
            pltpu.VMEM((2, 4, 192, 1536), bf),
            pltpu.VMEM((2, 16, 48, 512), bf),
            pltpu.VMEM((2, 512, 1536), bf),
            pltpu.VMEM((2, 512, 1536), bf),
            pltpu.SemaphoreType.DMA,
            pltpu.SemaphoreType.DMA((2,)),
            pltpu.SemaphoreType.DMA((23,)),
            pltpu.SemaphoreType.DMA((23,)),
            pltpu.SemaphoreType.DMA((17,)),
            pltpu.SemaphoreType.DMA((17,)),
            pltpu.SemaphoreType.DMA((2, 16)),
            pltpu.SemaphoreType.DMA((2, 16)),
        ],
        compiler_params=pltpu.CompilerParams(
            collective_id=2, has_side_effects=True, vmem_limit_bytes=56 * 2**20
        ),
        name="experts",
    )(x_rows, act_grad, w_in)


def turn(row):
    return jnp.transpose(jnp.broadcast_to(row, (128, 256)))


def forward_kernel(
    q_ref, k_ref, v_ref, res_ref, lengths_ref, routes_ref, gates_ref, og_ref, w_out_hbm,
    rows_ref, rows_col_ref, qend_row_ref, attn_ref, lse_ref, mixed_ref, inv_ref, xrecv_ref, grecv_ref, act_grad_ref, kv_out_ref,
    kv, m_s, l_s, acc_s, gsend, xsend, part, sums, sq_send, sq_recv, gated, qend_s, w_out_ref,
    w_sem,
    kv_send_sem, kv_recv_sem, out_sem, g_send_sem, g_recv_sem, x_send_sem, x_recv_sem,
    p_send_sem, p_recv_sem, sq_send_sem, sq_recv_sem,
):
    me = lax.axis_index("ctx")
    grp = lax.axis_index("grp")
    core = lax.rem(me, 2)
    chip = me // 2
    x = lax.rem(chip, 4)
    yh = chip // 4

    def device(dy, dx, dc):
        there = lax.rem(yh + dy, 2) * 4 + lax.rem(x + dx, 4)
        return {"ctx": there * 2 + lax.rem(core + dc, 2)}

    w_copy = pltpu.make_async_copy(w_out_hbm, w_out_ref, w_sem)
    w_copy.start()
    greet()

    copies = {}
    sent = []

    def move(src, slot, where):
        copy = remote(src, kv.at[slot], kv_send_sem.at[len(sent)], kv_recv_sem.at[slot], where)
        copy.start()
        copies[slot] = copy
        sent.append(copy)

    def own(which):
        return k_ref if which == 0 else v_ref

    right, left = device(0, 1, 0), device(0, 3, 0)
    sibling, partner = device(0, 0, 1), device(1, 0, 0)
    early = lax.broadcasted_iota(jnp.int32, (256, 256), 0) < lax.broadcasted_iota(
        jnp.int32, (256, 256), 1
    )
    experts = [routes_ref[a : a + 1, :].astype(jnp.float32) for a in range(2)]
    for a in range(2):
        rank = jnp.zeros((1, 256), jnp.float32)
        for b in range(2):
            same = early & (turn(experts[b])[:, 0:1] == experts[a])
            rank += jnp.sum(jnp.where(same, 1.0, 0.0), axis=0, keepdims=True)
        cols = slice(a * 256, a * 256 + 256)
        rows = experts[a] * 48 + rank
        rows_ref[:, cols] = jnp.broadcast_to(rows, (8, 256)).astype(jnp.int32)
        rows_col_ref[:, a * 128 : a * 128 + 128] = turn(rows).astype(jnp.int32)
        gate = turn(gates_ref[a : a + 1, :])[:, 0:1]
        gated[cols, :] = (gate * og_ref[...].astype(jnp.float32)).astype(jnp.bfloat16)

    @pl.loop(0, 16)
    def _(step):
        k = lax.rem(step + 4, 16)
        there = lax.rem(me + k, 16)
        gsend[k] = dot_nn(pick_two(rows_ref, there), gated[...]).astype(jnp.bfloat16)

        @pl.when(k > 0)
        def _():
            remote(
                gsend.at[k], grecv_ref.at[me], g_send_sem.at[k], g_recv_sem.at[k], {"ctx": there}
            ).start()

    for which in range(2):
        move(own(which), (0, 0, 1, which), sibling)
    for which in range(2):
        move(own(which), (1, 0, 0, which), partner)
        move(own(which), (0, 3, 0, which), right)
        move(own(which), (0, 1, 0, which), left)
    grecv_ref[me] = gsend[0]
    kv[0, 0, 0, 0] = k_ref[...]
    kv[0, 0, 0, 1] = v_ref[...]
    pos_col = me * 256 + lax.broadcasted_iota(jnp.int32, (256, 128), 0)
    pos_row = me * 256 + lax.broadcasted_iota(jnp.int32, (8, 256), 1)
    ends_col, ends_row = jnp.full_like(pos_col, 4096), jnp.full_like(pos_row, 4096)
    end = jnp.int32(0)
    for f in range(16):
        end = end + lengths_ref[f]
        ends_col = jnp.minimum(ends_col, jnp.where(end > pos_col, end, 4096))
        ends_row = jnp.minimum(ends_row, jnp.where(end > pos_row, end, 4096))
    qend_s[...] = ends_col
    qend_row_ref[...] = ends_row
    summing = GrpSum(96, part, sums, p_send_sem, p_recv_sem)
    m_s[...] = jnp.full_like(m_s, LOW)
    l_s[...] = jnp.zeros_like(l_s)
    acc_s[...] = jnp.zeros_like(acc_s)
    outs = []

    def wait_slot(dy, dx, dc, which):
        copies[(dy, dx, dc, which)].wait_recv()

    def forward(dy, dx, which):
        wait_slot(dy, dx, 0, which)
        move(kv.at[dy, dx, 0, which], (dy, dx, 1, which), sibling)

    def relay(dy):
        forward(dy, 3, 0)
        move(kv.at[dy, 3, 0, 0], (dy, 2, 0, 0), right)
        forward(dy, 1, 1)
        move(kv.at[dy, 1, 0, 1], (dy, 2, 0, 1), left)
        forward(dy, 3, 1)
        forward(dy, 1, 0)

    def attend(dy, dx):
        for which in range(2):
            wait_slot(dy, dx, 1, which)
        copy = pltpu.make_async_copy(kv.at[dy, dx], kv_out_ref.at[dy, dx], out_sem.at[dy, dx])
        copy.start()
        outs.append(copy)
        there = lax.rem(yh + dy, 2) * 4 + lax.rem(x + dx, 4)
        lane = lax.broadcasted_iota(jnp.int32, (256, 256), 1)
        qend = qend_s[:, 0:1]
        limits = [qend - (there * 512 + lax.rem(core + dc, 2) * 256) for dc in range(2)]

        @pl.loop(0, 4)
        def _(h):
            cols = pl.ds(pl.multiple_of(h * 128, 128), 128)
            qh = q_ref[:, cols]
            scores = []
            for dc in range(2):
                s = dot_nt(qh, kv[dy, dx, dc, 0, :, cols]) * (LOG2E * HEAD_DIM**-0.5)
                scores.append(jnp.where(lane < limits[dc], s, LOW))
            top = jnp.max(jnp.maximum(scores[0], scores[1]), axis=1, keepdims=True)
            m_old = m_s[h]
            m_new = jnp.maximum(m_old, top)
            alpha = jnp.exp2(m_old - m_new)
            probs = [jnp.exp2(s - m_new[:, 0:1]) for s in scores]
            total = jnp.sum(probs[0] + probs[1], axis=1, keepdims=True)
            m_s[h] = m_new
            l_s[h] = l_s[h] * alpha + total
            acc = acc_s[h] * alpha
            for dc in range(2):
                acc += dot_nn(probs[dc].astype(jnp.bfloat16), kv[dy, dx, dc, 1, :, cols])
            acc_s[h] = acc

    attend(0, 0)

    @pl.loop(1, 16)
    def _(k):
        source = lax.rem(me + 16 - k, 16)
        remote(
            gsend.at[k], grecv_ref.at[source], g_send_sem.at[k], g_recv_sem.at[k], {"ctx": source}
        ).wait_recv()

    w_copy.wait()
    for dy, dz in CHUNK_ORDER:
        expert, _ = chunk_of(dy, dz)
        rows = chunk_rows(grecv_ref, dy, dz)

        @pl.loop(0, 3)
        def _(piece):
            cols = pl.ds(pl.multiple_of(piece * 512, 512), 512)
            part[dy, dz, :, cols] = dot_nt(rows, w_out_ref[expert, cols, :]).astype(jnp.bfloat16)

        summing.send_first(dy, dz)

    for which in range(2):
        wait_slot(1, 0, 0, which)
        move(kv.at[1, 0, 0, which], (1, 3, 0, which), right)
        move(kv.at[1, 0, 0, which], (1, 1, 0, which), left)
        move(kv.at[1, 0, 0, which], (1, 0, 1, which), sibling)
    relay(0)
    attend(0, 3)
    attend(0, 1)
    relay(1)
    summing.relay(1)
    summing.relay(0)
    attend(1, 0)
    for which in range(2):
        forward(0, 2, which)
    attend(0, 2)
    for dz in (2, 1, 3):
        summing.second(dz)
    attend(1, 3)
    attend(1, 1)
    summing.relay(2)
    for which in range(2):
        forward(1, 2, which)
    attend(1, 2)

    squares = jnp.zeros((256, 1), jnp.float32)
    for h in range(4):
        cols = slice(h * 128, h * 128 + 128)
        out = (acc_s[h] / l_s[h]).astype(jnp.bfloat16)
        lse_ref[h] = jnp.transpose(m_s[h] + jnp.log2(l_s[h]))[0:8]
        attn_ref[:, cols] = out
        mixed = (res_ref[:, cols].astype(jnp.float32) + out.astype(jnp.float32)).astype(
            jnp.bfloat16
        )
        mixed_ref[:, cols] = mixed
        mixed_f = mixed.astype(jnp.float32)
        squares += jnp.sum(mixed_f * mixed_f, axis=1, keepdims=True)
    turned = jnp.transpose(jnp.broadcast_to(squares, (256, 128)))
    sq_send[...] = turned[0:8]
    sq_recv[grp] = turned[0:8]

    @pl.loop(1, 8)
    def _(k):
        there = lax.rem(grp + k, 8)
        remote(
            sq_send, sq_recv.at[grp], sq_send_sem.at[k], sq_recv_sem.at[k], {"grp": there}
        ).start()

    @pl.loop(1, 8)
    def _(k):
        source = lax.rem(grp + 8 - k, 8)
        copy = remote(
            sq_send, sq_recv.at[source], sq_send_sem.at[k], sq_recv_sem.at[k], {"grp": source}
        )
        copy.wait_recv()
        copy.wait_send()

    total = sq_recv[0]
    for k in range(1, 8):
        total = total + sq_recv[k]
    inv = lax.rsqrt(total / 4096 + 1e-06)
    inv = jnp.transpose(jnp.concatenate([inv] * 16, axis=0))
    inv_ref[...] = inv
    normed = jnp.concatenate(
        [
            (mixed_ref[:, h * 128 : h * 128 + 128].astype(jnp.float32) * inv).astype(jnp.bfloat16)
            for h in range(4)
        ],
        axis=1,
    )

    @pl.loop(0, 16)
    def _(step):
        k = lax.rem(step + 4, 16)
        there = lax.rem(me + k, 16)
        xsend[k] = dot_nn(pick_both(rows_ref, there), normed).astype(jnp.bfloat16)

        @pl.when(k > 0)
        def _():
            remote(
                xsend.at[k], xrecv_ref.at[me], x_send_sem.at[k], x_recv_sem.at[k], {"ctx": there}
            ).start()

    xrecv_ref[me] = xsend[0]

    summing.second_rest()

    def keep(rows, total):
        act_grad_ref[rows, :] = total

    summing.finish_head(keep)
    summing.finish_rest(keep)
    summing.drain()

    @pl.loop(1, 16)
    def _(k):
        source = lax.rem(me + 16 - k, 16)
        copy = remote(
            gsend.at[k], grecv_ref.at[source], g_send_sem.at[k], g_recv_sem.at[k], {"ctx": source}
        )
        copy.wait_send()
        copy = remote(
            xsend.at[k], xrecv_ref.at[source], x_send_sem.at[k], x_recv_sem.at[k], {"ctx": source}
        )
        copy.wait_recv()
        copy.wait_send()

    for copy in sent:
        copy.wait_send()
    for copy in outs:
        copy.wait()


def forward_call(*operands):
    bf, f32 = jnp.bfloat16, jnp.float32
    vmem = pl.BlockSpec(memory_space=pltpu.VMEM)
    shape = jax.ShapeDtypeStruct
    return pl.pallas_call(
        forward_kernel,
        out_shape=(
            shape((8, 512), jnp.int32),
            shape((256, 256), jnp.int32),
            shape((8, 256), jnp.int32),
            shape((256, 512), bf),
            shape((4, 8, 256), f32),
            shape((256, 512), bf),
            shape((256, 128), f32),
            shape((16, 96, 512), bf),
            shape((16, 96, 512), bf),
            shape((192, 1536), f32),
            shape((2, 4, 2, 2, 256, 512), bf),
        ),
        in_specs=[vmem] * 4
        + [pl.BlockSpec(memory_space=pltpu.SMEM)]
        + [vmem] * 3
        + [pl.BlockSpec(memory_space=pl.ANY)],
        out_specs=[vmem] * 10 + [pl.BlockSpec(memory_space=pl.ANY)],
        scratch_shapes=[
            pltpu.VMEM((2, 4, 2, 2, 256, 512), bf),
            pltpu.VMEM((4, 256, 128), f32),
            pltpu.VMEM((4, 256, 128), f32),
            pltpu.VMEM((4, 256, 128), f32),
            pltpu.VMEM((16, 96, 512), bf),
            pltpu.VMEM((16, 96, 512), bf),
            pltpu.VMEM((2, 4, 192, 1536), bf),
            pltpu.VMEM((14, 192, 1536), bf),
            pltpu.VMEM((8, 256), f32),
            pltpu.VMEM((8, 8, 256), f32),
            pltpu.VMEM((512, 512), bf),
            pltpu.VMEM((256, 128), jnp.int32),
            pltpu.VMEM((2, 1536, 512), bf),
            pltpu.SemaphoreType.DMA,
            pltpu.SemaphoreType.DMA((30,)),
            pltpu.SemaphoreType.DMA((2, 4, 2, 2)),
            pltpu.SemaphoreType.DMA((2, 4)),
            pltpu.SemaphoreType.DMA((16,)),
            pltpu.SemaphoreType.DMA((16,)),
            pltpu.SemaphoreType.DMA((16,)),
            pltpu.SemaphoreType.DMA((16,)),
            pltpu.SemaphoreType.DMA((23,)),
            pltpu.SemaphoreType.DMA((23,)),
            pltpu.SemaphoreType.DMA((8,)),
            pltpu.SemaphoreType.DMA((8,)),
        ],
        compiler_params=pltpu.CompilerParams(
            collective_id=0, has_side_effects=True, vmem_limit_bytes=56 * 2**20
        ),
        name="forward",
    )(*operands)


TERM_ORDER = [(1, 3), (1, 1), (1, 2), (1, 0), (0, 3), (0, 1), (0, 2), (0, 0)]


def backward_kernel(
    q_ref, kv_hbm, lse_ref, attn_ref, qend_ref, og_ref, inv_ref, rows_ref, rg_ref, act_ref,
    w_out_hbm, g_hbm, mixed_ref, gates_ref,
    layer_ref, ig_ref, dq_ref, dk_ref, dv_ref, w_out_grad_ref,
    full, eo_send, eo_recv, kv_ref, w_out_ref, g_ref, w_out_grad_s, load_sem, normed_grad, row_dot, dqt, own_terms, sib_send, sib_recv, ring_send,
    ring_recv, part_send, part_recv,
    f_send_sem, f_recv_sem, r_send_sem, r_recv_sem, sib_send_sem, sib_recv_sem, ring_send_sem, ring_recv_sem,
    part_send_sem, part_recv_sem,
):
    me = lax.axis_index("ctx")
    core = lax.rem(me, 2)
    chip = me // 2
    x = lax.rem(chip, 4)
    yh = chip // 4
    bf, f32 = jnp.bfloat16, jnp.float32

    def device(dy, dx, dc):
        there = lax.rem(yh + dy, 2) * 4 + lax.rem(x + dx, 4)
        return {"ctx": there * 2 + lax.rem(core + dc, 2)}

    right, left = device(0, 1, 0), device(0, 3, 0)
    sibling, partner = device(0, 0, 1), device(1, 0, 0)
    loads = {}
    for dy, dx in TERM_ORDER:
        loads[(dy, dx)] = pltpu.make_async_copy(
            kv_hbm.at[dy, dx], kv_ref.at[dy, dx], load_sem.at[dy * 4 + dx]
        )
    w_load = pltpu.make_async_copy(w_out_hbm, w_out_ref, load_sem.at[8])
    g_load = pltpu.make_async_copy(g_hbm, g_ref, load_sem.at[9])
    loads[(1, 3)].start()
    loads[(1, 1)].start()
    greet()
    gathering = GrpGather(64, full, f_send_sem, f_recv_sem)
    full[0, 0] = act_ref[...]
    gathering.send_own()
    for dy, dx in TERM_ORDER[2:]:
        loads[(dy, dx)].start()
    w_load.start()
    g_load.start()
    dqt[...] = jnp.zeros_like(dqt)
    row_id = lax.broadcasted_iota(jnp.int32, (256, 1536), 1)
    hits = [row_id == rows_ref[:, a * 128 : a * 128 + 1] for a in range(2)]
    pick = jnp.where(hits[0] | hits[1], 1.0, 0.0).astype(bf)
    normed_grad[...] = dot_nn(pick, rg_ref[...].reshape(1536, 512))

    for h in range(4):
        cols = slice(h * 128, h * 128 + 128)
        grad = og_ref[:, cols].astype(f32) + inv_ref[...] * normed_grad[:, cols]
        grad = grad.astype(bf)
        ig_ref[:, cols] = grad
        dots = jnp.sum(grad.astype(f32) * attn_ref[:, cols].astype(f32), axis=1, keepdims=True)
        row_dot[h] = jnp.transpose(jnp.broadcast_to(dots, (256, 128)))[0:8]

    scale = HEAD_DIM**-0.5

    def terms(dy, dx):
        loads[(dy, dx)].wait()
        there = lax.rem(yh + dy, 2) * 4 + lax.rem(x + dx, 4)
        sub = lax.broadcasted_iota(jnp.int32, (256, 256), 0)
        qend = qend_ref[0:1, :]
        limits = [qend - (there * 512 + lax.rem(core + dc, 2) * 256) for dc in range(2)]

        @pl.loop(0, 4)
        def _(h):
            cols = pl.ds(pl.multiple_of(h * 128, 128), 128)
            qh = q_ref[:, cols]
            gh = ig_ref[:, cols]
            lse = lse_ref[h][0:1, :]
            dots = row_dot[h][0:1, :]
            for dc in range(2):
                kh = kv_ref[dy, dx, dc, 0, :, cols]
                vh = kv_ref[dy, dx, dc, 1, :, cols]
                s = dot_nt(kh, qh) * (LOG2E * scale)
                p = jnp.exp2(jnp.where(sub < limits[dc], s, LOW) - lse)
                dp = dot_nt(vh, gh)
                ds = (p * (dp - dots) * scale).astype(bf)
                dk = dot_nn(ds, qh).astype(bf)
                dv = dot_nn(p.astype(bf), gh).astype(bf)
                dqt[h] += dot_tn(kh, ds)
                to = own_terms if dc == 0 else sib_send
                to[dy, dx, 0, :, cols] = dk
                to[dy, dx, 1, :, cols] = dv

        for which in range(2):
            sib_copy(dy, dx, which).start()

    def sib_copy(dy, dx, which):
        return remote(
            sib_send.at[dy, dx, which],
            sib_recv.at[dy, dx, which],
            sib_send_sem.at[dy, dx, which],
            sib_recv_sem.at[dy, dx, which],
            sibling,
        )

    def ring_copy(dy, dx, which):
        to = (dx + 3) % 4 if which == 0 else (dx + 1) % 4
        return remote(
            ring_send.at[dy, dx, which],
            ring_recv.at[dy, to, which],
            ring_send_sem.at[dy, dx, which],
            ring_recv_sem.at[dy, to, which],
            right if which == 0 else left,
        )

    def arrival(dy, dx, which):
        return ring_copy(dy, (dx + 1) % 4 if which == 0 else (dx + 3) % 4, which)

    def total_of(dy, dx, which, ring):
        sib_copy(dy, dx, which).wait_recv()
        if ring:
            arrival(dy, dx, which).wait_recv()
        sums = own_terms[dy, dx, which].astype(f32) + sib_recv[dy, dx, which].astype(f32)
        if ring:
            sums = sums + ring_recv[dy, dx, which].astype(f32)
        return sums

    def send_ring(dy, dx, which, ring):
        ring_send[dy, dx, which] = total_of(dy, dx, which, ring).astype(bf)
        ring_copy(dy, dx, which).start()

    def part_copy(which):
        return remote(
            part_send.at[which],
            part_recv.at[which],
            part_send_sem.at[which],
            part_recv_sem.at[which],
            partner,
        )

    def expert_rows(dy, dz):
        expert, _ = chunk_of(dy, dz)
        rows = dot_nn(full[dy, dz], w_out_ref[expert]).astype(bf)
        return_rows(rows, dy, dz, eo_send, eo_recv, r_send_sem, r_recv_sem)

    terms(1, 3)
    terms(1, 1)
    send_ring(1, 3, 0, False)
    send_ring(1, 1, 1, False)
    terms(1, 2)
    terms(1, 0)
    send_ring(1, 2, 0, True)
    send_ring(1, 2, 1, True)
    w_load.wait()
    gathering.relay(0)
    for dz in (3, 1):
        gathering.pass_head(dz)
    gathering.pass_rest()
    gathering.relay(1)
    expert_rows(0, 0)
    terms(0, 3)
    send_ring(1, 1, 0, True)
    send_ring(1, 3, 1, True)
    send_ring(0, 3, 0, False)
    terms(0, 1)
    send_ring(0, 1, 1, False)
    gathering.pass_head(2)
    gathering.relay(2)
    terms(0, 2)
    for which in range(2):
        part_send[which] = total_of(1, 0, which, True).astype(bf)
        part_copy(which).start()
    send_ring(0, 2, 0, True)
    send_ring(0, 2, 1, True)
    terms(0, 0)
    send_ring(0, 1, 0, True)
    send_ring(0, 3, 1, True)
    for dy, dz in [(0, 1), (0, 3), (1, 0)]:
        gathering.wait_chunk(dy, dz)
        expert_rows(dy, dz)
    for h in range(4):
        dq_ref[:, h * 128 : h * 128 + 128] = jnp.transpose(dqt[h]).astype(bf)
    def weight_grads(dy):
        expert, _ = chunk_of(dy, 0)

        @pl.loop(0, 3)
        def _(piece):
            cols = pl.ds(pl.multiple_of(piece * 512, 512), 512)
            total = dot_tn(full[dy, 0, :, cols], chunk_rows(g_ref, dy, 0))
            for dz in range(1, 4):
                total += dot_tn(full[dy, dz, :, cols], chunk_rows(g_ref, dy, dz))
            w_out_grad_s[expert, cols, :] = total.astype(bf)

        out = pltpu.make_async_copy(
            w_out_grad_s.at[expert], w_out_grad_ref.at[expert], load_sem.at[10 + dy]
        )
        out.start()
        return out

    g_load.wait()
    for dy, dz in [(0, 2), (1, 1), (1, 3)]:
        gathering.wait_chunk(dy, dz)
        expert_rows(dy, dz)
    w_outs = [weight_grads(0)]
    gathering.wait_chunk(1, 2)
    expert_rows(1, 2)
    for which in range(2):
        sums = total_of(0, 0, which, True)
        part_copy(which).wait_recv()
        sums = sums + part_recv[which].astype(f32)
        if which == 0:
            dk_ref[...] = sums.astype(bf)
        else:
            dv_ref[...] = sums.astype(bf)

    for dy in range(2):
        for dx in range(4):
            for which in range(2):
                sib_copy(dy, dx, which).wait_send()
                if dx > 0:
                    ring_copy(dy, dx, which).wait_send()
    for which in range(2):
        part_copy(which).wait_send()

    w_outs.append(weight_grads(1))
    wait_returns(eo_send, eo_recv, r_send_sem, r_recv_sem)
    total = mixed_ref[...].astype(f32)
    for a in range(2):
        hit = row_id == rows_ref[:, a * 128 : a * 128 + 1]
        picked = dot_nn(jnp.where(hit, 1.0, 0.0).astype(bf), eo_recv[...].reshape(1536, 512))
        total = total + turn(gates_ref[a : a + 1, :])[:, 0:1] * picked
    layer_ref[...] = total.astype(bf)

    gathering.drain()
    for out in w_outs:
        out.wait()


def backward_call(*operands):
    bf, f32 = jnp.bfloat16, jnp.float32
    vmem = pl.BlockSpec(memory_space=pltpu.VMEM)
    anywhere = pl.BlockSpec(memory_space=pl.ANY)
    shape = jax.ShapeDtypeStruct
    return pl.pallas_call(
        backward_kernel,
        out_shape=(shape((256, 512), bf),) * 5 + (shape((2, 1536, 512), bf),),
        in_specs=[vmem, anywhere] + [vmem] * 8 + [anywhere] * 2 + [vmem] * 2,
        out_specs=(vmem,) * 5 + (anywhere,),
        scratch_shapes=[
            pltpu.VMEM((2, 4, 192, 1536), bf),
            pltpu.VMEM((2, 16, 48, 512), bf),
            pltpu.VMEM((16, 2, 48, 512), bf),
            pltpu.VMEM((2, 4, 2, 2, 256, 512), bf),
            pltpu.VMEM((2, 1536, 512), bf),
            pltpu.VMEM((16, 96, 512), bf),
            pltpu.VMEM((2, 1536, 512), bf),
            pltpu.SemaphoreType.DMA((12,)),
            pltpu.VMEM((256, 512), f32),
            pltpu.VMEM((4, 8, 256), f32),
            pltpu.VMEM((4, 128, 256), f32),
            pltpu.VMEM((2, 4, 2, 256, 512), bf),
            pltpu.VMEM((2, 4, 2, 256, 512), bf),
            pltpu.VMEM((2, 4, 2, 256, 512), bf),
            pltpu.VMEM((2, 4, 2, 256, 512), bf),
            pltpu.VMEM((2, 4, 2, 256, 512), bf),
            pltpu.VMEM((2, 256, 512), bf),
            pltpu.VMEM((2, 256, 512), bf),
            pltpu.SemaphoreType.DMA((17,)),
            pltpu.SemaphoreType.DMA((17,)),
            pltpu.SemaphoreType.DMA((2, 16)),
            pltpu.SemaphoreType.DMA((2, 16)),
            pltpu.SemaphoreType.DMA((2, 4, 2)),
            pltpu.SemaphoreType.DMA((2, 4, 2)),
            pltpu.SemaphoreType.DMA((2, 4, 2)),
            pltpu.SemaphoreType.DMA((2, 4, 2)),
            pltpu.SemaphoreType.DMA((2,)),
            pltpu.SemaphoreType.DMA((2,)),
        ],
        compiler_params=pltpu.CompilerParams(
            collective_id=1, has_side_effects=True, vmem_limit_bytes=56 * 2**20
        ),
        name="backward",
    )(*operands)


def publish_kernel(count, *refs):
    sources, targets, held = refs[:count], refs[count : 2 * count], refs[2 * count : 3 * count]
    in_sem, out_sem = refs[3 * count :]
    reads = [pltpu.make_async_copy(sources[n], held[n], in_sem.at[n]) for n in range(count)]
    writes = [pltpu.make_async_copy(held[n], targets[n], out_sem.at[n]) for n in range(count)]
    for read in reads:
        read.start()
    for read, write in zip(reads, writes):
        read.wait()
        write.start()
    for write in writes:
        write.wait()


def publish(*arrays):
    anywhere = pl.BlockSpec(memory_space=pl.ANY)
    count = len(arrays)
    return pl.pallas_call(
        functools.partial(publish_kernel, count),
        out_shape=tuple(jax.ShapeDtypeStruct(a.shape, a.dtype) for a in arrays),
        in_specs=[anywhere] * count,
        out_specs=(anywhere,) * count,
        scratch_shapes=[pltpu.VMEM(a.shape, a.dtype) for a in arrays]
        + [pltpu.SemaphoreType.DMA((count,))] * 2,
        compiler_params=pltpu.CompilerParams(vmem_limit_bytes=56 * 2**20),
        name="publish",
    )(*arrays)


def shards(
    residual, queries, keys, values, frame_lengths, routes, route_gates, w_in, w_out, out_grad
):
    n_ctx = lax.axis_size("ctx")
    tok_rows, feat_dev = residual.shape
    exp_dev = w_in.shape[0]
    rows_wide, rows_col, qend_row, attn, lse, mixed, inv_wide, rows_recv, grads_recv, act_grad, kv_all = (
        forward_call(
            queries,
            keys,
            values,
            residual,
            frame_lengths,
            routes.T,
            route_gates.T,
            out_grad,
            w_out,
        )
    )
    activated, row_grad, w_in_grad = experts_call(rows_recv, act_grad, w_in)
    layer_out, input_grad, query_grad, key_grad, value_grad, w_out_grad = backward_call(
        queries,
        kv_all,
        lse,
        attn,
        qend_row,
        out_grad,
        inv_wide,
        rows_col,
        row_grad.reshape(n_ctx, exp_dev * row_grad.shape[2], feat_dev),
        activated,
        w_out,
        grads_recv,
        mixed,
        route_gates.T,
    )
    return publish(
        layer_out,
        input_grad,
        query_grad,
        key_grad,
        value_grad,
        w_in_grad,
        w_out_grad,
    )


def solution(mesh):
    in_specs = (
        P("ctx", "grp"),
        P("ctx", "grp"),
        P("ctx", "grp"),
        P("ctx", "grp"),
        P(),
        P("ctx", None),
        P("ctx", None),
        P("ctx", "grp", None),
        P("ctx", None, "grp"),
        P("ctx", "grp"),
    )
    out_specs = (
        P("ctx", "grp"),
        P("ctx", "grp"),
        P("ctx", "grp"),
        P("ctx", "grp"),
        P("ctx", "grp"),
        P("ctx", "grp", None),
        P("ctx", None, "grp"),
    )
    return jax.shard_map(shards, mesh=mesh, in_specs=in_specs, out_specs=out_specs, check_vma=False)
```
